32 devices in a mesh: ctx: 16 (over z, y, x), tp: 2 (over core).
Axes of the slice: x: 2, y: 2, z: 4, core: 2. Of those that a mesh axis runs over, the one named last changes fastest.
Arguments:
- queries: bfloat16 [2048, 4096], P('ctx', 'tp'), may hold values from -16 to 16
- keys: bfloat16 [2048, 1024], P('ctx', 'tp'), may hold values from -7.1 to 7.1
- values: bfloat16 [2048, 1024], P('ctx', 'tp'), may hold values from -6 to 6
- mixer_input: bfloat16 [2048, 8192], P('ctx', 'tp'), may hold values from -6 to 6
- gate: bfloat16 [2048, 8192], P('ctx', 'tp'), may hold values from -6 to 6
- step_weight: bfloat16 [8192, 128], P('tp'), may hold values from -0.0625 to 0.0625
- state_weight: bfloat16 [8192, 32], P('tp'), may hold values from -0.0625 to 0.0625
- step_bias: float32 [128], P('tp'), may hold values from -1 to 1
- decay_rate: float32 [128], P('tp'), may hold values from 4.8828124e-06 to 0.05
- skip_gain: float32 [128], P('tp'), may hold values from 0.5 to 2
- norm_gain: float32 [8192], P('tp'), may hold values from 0.1 to 1.9
Outputs:
- attention_out: bfloat16 [2048, 4096], P('ctx', 'tp')
- mamba_out: bfloat16 [2048, 8192], P('ctx', 'tp')
The draws below stay inside these ranges and needn't reach their ends.
All inputs are finite; a program needn't handle non-finite values.
Results may differ from the reference program's by a relative error of at most 0.0044.
Values may be sent and summed in bfloat16 or wider, within the bound.
No kernel may reach another device: no remote copies, remote signals or barrier semaphores. Data moves between devices by JAX's collectives and lax.ppermute only.
A program may use at most 64 MiB of HBM per device.

```python
import math
import jax
import jax.numpy as jnp
from jax import lax

QHEADS = 32
KVHEADS = 8
HD = 128
INNER_CHANNELS = 8192
STATE_WIDTH = 16
DECAY_CHANNELS = 64
SCAN_TOKENS = 128
TOK_DEV = 128
TOKENS = 2048
MHEADS = 128


def draw_keys(key, part):
    noise = jax.random.normal(jax.random.fold_in(key, 13), (TOKENS, KVHEADS, HD), jnp.float32)
    noise = jnp.clip(noise, -6.0, 6.0)
    return noise.reshape(TOKENS, KVHEADS * HD).astype(jnp.bfloat16)


def draw_queries(key, part):
    noise = jax.random.normal(jax.random.fold_in(key, 11), (TOKENS, QHEADS, HD), jnp.float32)
    noise = jnp.clip(noise, -6.0, 6.0)
    return noise.reshape(TOKENS, QHEADS * HD).astype(jnp.bfloat16)


def level_of(own_key, shape, shards, low, high):
    gain = 1.0
    for position, parts in shards:
        heights = jax.random.uniform(jax.random.fold_in(jax.random.fold_in(own_key, 6), position), (parts,), jnp.float32, low / len(shards), high / len(shards))
        gain = gain * jnp.repeat(jnp.exp(heights), shape[position] // parts).reshape((-1,) + (1,) * (len(shape) - 1 - position))
    return gain


def bell_draw(stream_key, shape, spread, most, pieces=(), held_as=jnp.bfloat16):
    values = spread * jax.random.normal(stream_key, shape, jnp.float32)
    if pieces:
        values = values * level_of(stream_key, shape, pieces, -0.22, 0.18)
    return jnp.clip(values, -most, most).astype(held_as)


def setup_inputs(seed: int = 0) -> dict:
    arg_keys = jax.random.split(jax.random.key(seed), 12)
    queries = draw_queries(jax.random.fold_in(arg_keys[11], 71), 0)
    keys = draw_keys(jax.random.fold_in(arg_keys[11], 71), 0)
    values = bell_draw(arg_keys[2], (TOKENS, KVHEADS * HD), 1.0, 6.0, ((0, 16), (1, 2)))
    mixer_input = bell_draw(arg_keys[3], (TOKENS, INNER_CHANNELS), 1.0, 6.0, ((0, 16), (1, 2)))
    gate = bell_draw(arg_keys[4], (TOKENS, INNER_CHANNELS), 1.0, 6.0, ((0, 16), (1, 2)))
    step_weight = bell_draw(arg_keys[5], (INNER_CHANNELS, MHEADS), INNER_CHANNELS ** -0.5, 0.0625, ((0, 2),))
    state_weight = bell_draw(arg_keys[6], (INNER_CHANNELS, 2 * STATE_WIDTH), INNER_CHANNELS ** -0.5, 0.0625, ((0, 2),))
    step_bias = jnp.clip(jax.random.uniform(arg_keys[7], (MHEADS,), jnp.float32, -1.0, 1.0) * level_of(arg_keys[7], (MHEADS,), ((0, 2),), -0.4, 0.0), -1.0, 1.0)
    decay_rate = jnp.clip(jnp.exp(math.log(0.05) - 9.2340569 * jax.random.uniform(arg_keys[8], (MHEADS,), jnp.float32) ** level_of(arg_keys[8], (MHEADS,), ((0, 2),), -0.2, 0.2)), 4.882812390860636e-06, 0.05)
    skip_gain = jnp.clip(jnp.exp(math.log(2.0) - 1.3862944 * jax.random.uniform(arg_keys[9], (MHEADS,), jnp.float32) ** level_of(arg_keys[9], (MHEADS,), ((0, 2),), -0.2, 0.2)), 0.5, 2.0)
    norm_gain = jnp.clip(1.0 + 0.18 * jax.random.normal(arg_keys[10], (INNER_CHANNELS,), jnp.float32), 0.1, 1.9)
    return {"queries": queries, "keys": keys, "values": values, "mixer_input": mixer_input, "gate": gate, "step_weight": step_weight, "state_weight": state_weight, "step_bias": step_bias, "decay_rate": decay_rate, "skip_gain": skip_gain, "norm_gain": norm_gain}


def attention(queries, keys, values):
    group = QHEADS // KVHEADS
    scale = 1.0 / math.sqrt(HD)
    keys_wide = keys.reshape(TOKENS, KVHEADS, HD).astype(jnp.float32)
    values_wide = values.reshape(TOKENS, KVHEADS, HD).astype(jnp.float32)
    block = TOK_DEV // 2
    block_count = TOKENS // block
    key_positions = jnp.arange(TOKENS, dtype=jnp.int32)

    def one_block(number):
        first = number * block
        rows = lax.dynamic_slice_in_dim(queries, first, block, 0)
        rows = rows.reshape(block, KVHEADS, group, HD).astype(jnp.float32)
        scores = jnp.einsum('tkgd,skd->kgts', rows, keys_wide) * scale
        query_positions = first + jnp.arange(block, dtype=jnp.int32)
        mask = key_positions[None, :] <= query_positions[:, None]
        scores = jnp.where(mask, scores, -1e+30)
        row_max = lax.optimization_barrier(jnp.max(scores, axis=-1, keepdims=True))
        expos = jnp.where(mask, jnp.exp(scores - row_max), 0.0)
        total = lax.optimization_barrier(jnp.sum(expos, axis=-1))
        weights = lax.optimization_barrier(expos.astype(jnp.bfloat16)).astype(jnp.float32)
        mixed = jnp.einsum('kgts,skd->tkgd', weights, values_wide)
        mixed = mixed / jnp.transpose(total, (2, 0, 1))[..., None]
        return mixed.reshape(block, QHEADS * HD).astype(jnp.bfloat16)
    outputs = lax.map(one_block, jnp.arange(block_count, dtype=jnp.int32))
    return outputs.reshape(TOKENS, QHEADS * HD)

def mixer(mixer_input, gate, step_weight, state_weight, step_bias, decay_rate, skip_gain, norm_gain):
    head_count = INNER_CHANNELS // DECAY_CHANNELS
    step_raw = jnp.dot(mixer_input, step_weight, preferred_element_type=jnp.float32)
    maps = jnp.dot(mixer_input, state_weight, preferred_element_type=jnp.float32)
    step = jax.nn.softplus(step_raw + step_bias)
    log_decay = -decay_rate * step
    block_count = TOKENS // SCAN_TOKENS
    decay_blocks = log_decay.reshape(block_count, SCAN_TOKENS, head_count)
    step_blocks = step.reshape(block_count, SCAN_TOKENS, head_count)
    b_rows = maps[:, :STATE_WIDTH].reshape(block_count, SCAN_TOKENS, STATE_WIDTH)
    c_rows = maps[:, STATE_WIDTH:].reshape(block_count, SCAN_TOKENS, STATE_WIDTH)
    input_blocks = mixer_input.reshape(block_count, SCAN_TOKENS, head_count, DECAY_CHANNELS)
    causal = jnp.arange(SCAN_TOKENS)[:, None] >= jnp.arange(SCAN_TOKENS)[None, :]

    def one_block(carry, items):
        decay_here, step_here, b_here, c_here, x_here = items
        climb = jnp.cumsum(decay_here, axis=0)
        inner = jnp.dot(c_here, b_here.T, precision=lax.Precision.HIGHEST, preferred_element_type=jnp.float32)
        climb_t = climb.T
        diff = climb_t[:, :, None] - climb_t[:, None, :]
        decay = jnp.where(causal[None], jnp.exp(jnp.where(causal[None], diff, 0.0)), 0.0)
        mix = (inner[None] * decay * step_here.T[:, None, :]).astype(jnp.bfloat16)
        mix_wide = lax.optimization_barrier(mix).astype(jnp.float32)
        x_wide = x_here.astype(jnp.float32)
        local = jnp.einsum('hts,shp->thp', mix_wide, x_wide)
        carried = jnp.exp(climb)[:, :, None] * jnp.einsum('tn,nhp->thp', c_here, carry, precision=lax.Precision.HIGHEST)
        y_block = local + carried + skip_gain[None, :, None] * x_wide
        final = climb[-1]
        feed = (b_here[:, :, None] * (jnp.exp(final[None, :] - climb) * step_here)[:, None, :]).astype(jnp.bfloat16)
        feed_wide = lax.optimization_barrier(feed).astype(jnp.float32)
        new_carry = jnp.exp(final)[None, :, None] * carry + jnp.einsum('snh,shp->nhp', feed_wide, x_wide)
        return (new_carry, y_block)
    start_index = jnp.zeros((STATE_WIDTH, head_count, DECAY_CHANNELS), jnp.float32)
    ending, y_all = lax.scan(one_block, start_index, (decay_blocks, step_blocks, b_rows, c_rows, input_blocks))
    y_flat = y_all.reshape(TOKENS, INNER_CHANNELS)
    gated = y_flat * jax.nn.silu(gate.astype(jnp.float32))
    mean_square = lax.optimization_barrier(jnp.mean(gated * gated, axis=-1, keepdims=True))
    normed = gated * lax.rsqrt(mean_square + 1e-05)
    return (normed * norm_gain).astype(jnp.bfloat16)

def reference(queries, keys, values, mixer_input, gate, step_weight, state_weight, step_bias, decay_rate, skip_gain, norm_gain):
    attention_out = attention(queries, keys, values)
    mamba_out = mixer(mixer_input, gate, step_weight, state_weight, step_bias, decay_rate, skip_gain, norm_gain)
    return (attention_out, mamba_out)
```

```python
import functools
import math

import jax
import jax.numpy as jnp
from jax import lax
from jax.experimental import pallas as pl
from jax.experimental.pallas import tpu as pltpu
from jax.sharding import PartitionSpec as P

HD = 128
DECAY_CHANNELS = 64
SCAN_TOKENS = 128
LANES = 128
UNROLL = 8
VMEM_LIMIT = 40 * 1024 * 1024

F32 = jnp.float32
BF16 = jnp.bfloat16


def vmem():
    return pl.BlockSpec(memory_space=pltpu.VMEM)


def params():
    return pltpu.CompilerParams(vmem_limit_bytes=VMEM_LIMIT)


def cost(flops, size, transcendentals=0):
    return pl.CostEstimate(flops=flops, bytes_accessed=size, transcendentals=transcendentals)


def place(group):
    return lax.rem(lax.axis_index("ctx"), jnp.int32(group))


def swap(pieces, group, count):
    result = [pieces[0]]
    for k in range(1, group):
        perm = [(i, (i // group) * group + ((i % group) ^ k)) for i in range(count)]
        result.append(lax.ppermute(pieces[k], "ctx", perm))
    return result


def climb_up(array, group, count, steps=1):
    perm = [(i, i + group * steps) for i in range(count - group * steps)]
    return lax.ppermute(array, "ctx", perm)


def pack_kv_kernel(group, k_ref, v_ref, *outs):
    mine = place(group)
    width = k_ref.shape[1] // group
    for k in range(group):
        columns = pl.ds(pl.multiple_of((mine ^ k) * width, width), width)
        outs[k][0] = k_ref[:, columns]
        outs[k][1] = v_ref[:, columns]


def pack_kv(keys, values, group):
    length, width = keys.shape
    out = jax.ShapeDtypeStruct((2, length, width // group), keys.dtype)
    return pl.pallas_call(
        functools.partial(pack_kv_kernel, group),
        out_shape=[out] * group,
        in_specs=[vmem()] * 2,
        out_specs=[vmem()] * group,
        compiler_params=params(),
        cost_estimate=cost(0, 8 * length * width),
        name="pack_kv",
    )(keys, values)


def pack_q_kernel(group, q_ref, *outs):
    mine = place(group)
    width = q_ref.shape[1] // group
    for k in range(group):
        columns = pl.ds(pl.multiple_of((mine ^ k) * width, width), width)
        outs[k][...] = q_ref[:, columns]


def pack_q(queries, group):
    length, width = queries.shape
    out = jax.ShapeDtypeStruct((length, width // group), queries.dtype)
    return pl.pallas_call(
        functools.partial(pack_q_kernel, group),
        out_shape=[out] * group,
        in_specs=[vmem()],
        out_specs=[vmem()] * group,
        compiler_params=params(),
        cost_estimate=cost(0, 4 * length * width),
        name="pack_q",
    )(queries)


def join_kernel(group, *refs):
    out_ref = refs[group]
    mine = place(group)
    width = refs[0].shape[1]
    for k in range(group):
        columns = pl.ds(pl.multiple_of((mine ^ k) * width, width), width)
        out_ref[:, columns] = refs[k][...]


def join(pieces, group):
    length, width = pieces[0].shape
    return pl.pallas_call(
        functools.partial(join_kernel, group),
        out_shape=jax.ShapeDtypeStruct((length, width * group), pieces[0].dtype),
        in_specs=[vmem()] * group,
        out_specs=vmem(),
        compiler_params=params(),
        cost_estimate=cost(0, 4 * length * width * group),
        name="join_heads",
    )(*pieces)


def flash_kernel(group, length, own, state_in, chunks, final, base, *refs):
    refs = list(refs)
    base_ref = refs.pop(0) if base is None else None
    q_refs = [refs.pop(0) for _ in range(group)]
    own_ref = refs.pop(0) if own else None
    state_ref = refs.pop(0) if state_in else None
    chunk_refs = [refs.pop(0) for _ in range(chunks)]
    out_refs = [refs.pop(0) for _ in range(group if final else 1)]
    acc_ref, top_ref = refs
    index = lax.axis_index("ctx")
    mine = place(group)
    turn = index // group
    first = base_ref[0] if base is None else base
    rows = group * length
    tile = min(rows, 256)
    rate = math.log2(math.e) / math.sqrt(HD)
    queries = jnp.concatenate([ref[...] for ref in q_refs], axis=0)
    ones = jnp.ones((rows, HD), BF16)

    def keys_of(ref):
        return ref[:, 0].reshape(rows, HD)

    def values_of(ref):
        return jnp.concatenate([ref[:, 1].reshape(rows, HD), ones], axis=1)

    def score(q, k):
        return lax.dot_general(q, k, (((1,), (1,)), ((), ())), preferred_element_type=F32)

    for start in range(0, rows, tile):
        here = slice(start, start + tile)
        q = queries[here]
        if own:
            scores = score(q, keys_of(own_ref))
            q_at = (lax.broadcasted_iota(jnp.int32, (tile, rows), 0) + start) ^ (mine * length)
            k_at = lax.broadcasted_iota(jnp.int32, (tile, rows), 1) ^ (mine * length)
            scores = jnp.where(k_at <= q_at, scores, -1e30)
            top = jnp.max(scores, axis=1, keepdims=True)
            weights = jnp.exp2((scores - top) * rate).astype(BF16)
            acc_ref[here] = jnp.dot(weights, values_of(own_ref), preferred_element_type=F32)
            top_ref[here] = jnp.broadcast_to(top, (tile, LANES))
        elif state_in:
            acc_ref[here, :HD] = state_ref[0, here, :HD]
            acc_ref[here, HD:] = jnp.broadcast_to(state_ref[0, here, HD : HD + 1], (tile, LANES))
            top_ref[here] = jnp.broadcast_to(
                state_ref[0, here, HD + LANES // 2 : HD + LANES // 2 + 1], (tile, LANES)
            )
        for number in range(chunks):

            @pl.when(turn >= first + number)
            def _(ref=chunk_refs[number]):
                scores = score(q, keys_of(ref))
                before = top_ref[here, :1]
                top = jnp.maximum(before, jnp.max(scores, axis=1, keepdims=True))
                weights = jnp.exp2((scores - top) * rate).astype(BF16)
                keep = jnp.exp2((before - top) * rate)
                acc_ref[here] = acc_ref[here] * keep + jnp.dot(
                    weights, values_of(ref), preferred_element_type=F32
                )
                top_ref[here] = jnp.broadcast_to(top, (tile, LANES))

        if not final:
            lane = lax.broadcasted_iota(jnp.int32, (tile, LANES), 1)
            out_refs[0][0, here, :HD] = acc_ref[here, :HD]
            out_refs[0][0, here, HD:] = jnp.where(
                lane < LANES // 2, acc_ref[here, HD:], top_ref[here]
            )
    if final:
        for k in range(group):
            here = slice(k * length, (k + 1) * length)
            out_refs[k][...] = (acc_ref[here, :HD] / acc_ref[here, HD:]).astype(BF16)


def flash(q_pieces, group, kv_heads, own=None, state=None, chunks=(), final=False, base=1):
    length, width = q_pieces[0].shape
    heads = width // HD
    share = heads // kv_heads
    rows = group * length
    head_block = pl.BlockSpec((length, HD), lambda h: (0, h))
    kv_block = pl.BlockSpec((group, 2, length, HD), lambda h: (0, 0, 0, h // share))
    state_block = pl.BlockSpec((1, rows, HD + LANES), lambda h: (h, 0, 0))
    operands, specs = [], []
    fixed = base if isinstance(base, int) else None
    if fixed is None:
        operands.append(base)
        specs.append(pl.BlockSpec(memory_space=pltpu.SMEM))
    operands += list(q_pieces)
    specs += [head_block] * group
    if own is not None:
        operands.append(own)
        specs.append(kv_block)
    if state is not None:
        operands.append(state)
        specs.append(state_block)
    operands += list(chunks)
    specs += [kv_block] * len(chunks)
    if final:
        out_shape = [jax.ShapeDtypeStruct((length, width), BF16)] * group
        out_specs = [head_block] * group
    else:
        out_shape = [jax.ShapeDtypeStruct((heads, rows, HD + LANES), F32)]
        out_specs = [state_block]
    parts = len(chunks) + (own is not None)
    kernel = functools.partial(
        flash_kernel, group, length, own is not None, state is not None, len(chunks), final, fixed
    )
    return pl.pallas_call(
        kernel,
        grid=(heads,),
        out_shape=out_shape,
        in_specs=specs,
        out_specs=out_specs,
        scratch_shapes=[pltpu.VMEM((rows, HD + LANES), F32), pltpu.VMEM((rows, LANES), F32)],
        compiler_params=params(),
        cost_estimate=cost(
            16 * heads * rows * rows * HD * parts, 4 * heads * rows * HD, heads * rows * rows * parts
        ),
        name="flash",
    )(*operands)


def attention_layer(queries, keys, values):
    count = lax.axis_size("ctx")
    kv_heads = keys.shape[1] // HD
    group = math.gcd(kv_heads, count)
    turns = count // group
    kv_here = kv_heads // group
    own = jnp.stack(swap(pack_kv(keys, values, group), group, count))
    q_pieces = swap(pack_q(queries, group), group, count)
    run = functools.partial(flash, q_pieces, group, kv_here)
    if turns <= UNROLL:
        arrived = [own]
        for _ in range(turns - 1):
            arrived.append(climb_up(arrived[-1], group, count))
        early, late = arrived[1:-1], arrived[-1:] if turns > 1 else []
        if turns > 1:
            (state,) = run(own=own, chunks=early)
            outs = run(state=state, chunks=late, final=True, base=turns - 1)
        else:
            outs = run(own=own, final=True)
    else:
        (state,) = run(own=own)

        def one(step, carry):
            chunk, state = carry
            chunk = climb_up(chunk, group, count)
            (state,) = run(state=state, chunks=[chunk], base=jnp.reshape(step, (1,)))
            return chunk, state

        _, state = lax.fori_loop(1, turns, one, (own, state))
        outs = run(state=state, final=True)
    return join(swap(outs, group, count), group)


def project_kernel(x_ref, step_ref, map_ref, out_ref):
    @pl.when(pl.program_id(0) == 0)
    def _():
        out_ref[...] = jnp.zeros_like(out_ref)

    heads = step_ref.shape[1]
    width = map_ref.shape[1]
    x = x_ref[...]
    out_ref[:, :heads] += jnp.dot(x, step_ref[...], preferred_element_type=F32)
    out_ref[:, heads : heads + width] += jnp.dot(x, map_ref[...], preferred_element_type=F32)


def project(x, step_weight, state_weight):
    length, channels = x.shape
    heads = step_weight.shape[1]
    width = state_weight.shape[1]
    depth = min(channels, 1024)
    return pl.pallas_call(
        project_kernel,
        grid=(channels // depth,),
        out_shape=jax.ShapeDtypeStruct((length, heads + LANES), F32),
        in_specs=[
            pl.BlockSpec((length, depth), lambda i: (0, i)),
            pl.BlockSpec((depth, heads), lambda i: (i, 0)),
            pl.BlockSpec((depth, width), lambda i: (i, 0)),
        ],
        out_specs=pl.BlockSpec((length, heads + LANES), lambda i: (0, 0)),
        compiler_params=params(),
        cost_estimate=cost(4 * length * channels * heads, 6 * channels * LANES),
        name="project",
    )(x, step_weight, state_weight)


def widen(row, lanes):
    extra = lanes - row.shape[1]
    if not extra:
        return row
    return jnp.concatenate([row, jnp.zeros((row.shape[0], extra), row.dtype)], axis=1)


def state_kernel(group, parts, states, *refs):
    part_refs = refs[:parts]
    bias_ref, rate_ref, x_ref = refs[parts : parts + 3]
    climb_ref, climb_t_ref, step_t_ref, maps_ref = refs[parts + 3 : parts + 7]
    out_refs = refs[parts + 7 : parts + 7 + group]
    held = refs[parts + 7 + group]
    summed = part_refs[0][...]
    for ref in part_refs[1:]:
        summed = summed + ref[...]
    length = summed.shape[0]
    every = summed.shape[1] - LANES
    heads = bias_ref.shape[1]
    shift = lax.rem(every - lax.axis_index("tp") * heads, jnp.int32(every))
    raw = pltpu.roll(summed[:, :every], shift, 1) + widen(bias_ref[...], every)
    step = jnp.maximum(raw, 0.0) + jnp.log1p(jnp.exp(-jnp.abs(raw)))
    log_decay = -widen(rate_ref[...], every) * step
    row = lax.broadcasted_iota(jnp.int32, (length, length), 0)
    column = lax.broadcasted_iota(jnp.int32, (length, length), 1)
    lower = (column <= row).astype(F32)
    climb = jnp.dot(lower, log_decay, precision=lax.Precision.HIGHEST, preferred_element_type=F32)
    maps = summed[:, every:]
    climb_ref[...] = climb
    maps_ref[...] = maps
    climb_t = climb.T
    step_t = step.T
    climb_t_ref[...] = climb_t[:heads]
    step_t_ref[...] = step_t[:heads]
    b_t = maps.T[:states]
    weight_t = jnp.exp(climb_t[:, length - 1 :] - climb_t) * step_t
    last = climb[length - 1 :]
    bundle = 4
    span = bundle * DECAY_CHANNELS
    owner = lax.broadcasted_iota(jnp.int32, (1, span), 1) // DECAY_CHANNELS
    width = held.shape[2]
    for at in range(0, heads, bundle):
        feed = jnp.concatenate([b_t * weight_t[at + i : at + i + 1] for i in range(bundle)], axis=0)
        columns = slice(at * DECAY_CHANNELS, at * DECAY_CHANNELS + span)
        product = jnp.dot(feed.astype(BF16), x_ref[:, columns], preferred_element_type=F32)
        state = jnp.zeros((states, span), F32)
        total = jnp.zeros((1, span), F32)
        for i in range(bundle):
            state = jnp.where(owner == i, product[i * states : (i + 1) * states], state)
            total = jnp.where(owner == i, last[:, at + i : at + i + 1], total)
        piece, offset = divmod(columns.start, width)
        held[piece, :states, offset : offset + span] = state
        held[piece, states:, offset : offset + span] = jnp.broadcast_to(total, (8, span))
    mine = place(group)
    for k in range(group):
        out_refs[k][...] = held[mine ^ k]


def block_state(parts, bias, rate, x, states, group):
    length, channels = x.shape
    every = parts[0].shape[1] - LANES
    heads = bias.shape[1]
    width = channels // group
    piece = jax.ShapeDtypeStruct((states + 8, width), F32)
    result = pl.pallas_call(
        functools.partial(state_kernel, group, len(parts), states),
        out_shape=[
            jax.ShapeDtypeStruct((length, every), F32),
            jax.ShapeDtypeStruct((heads, length), F32),
            jax.ShapeDtypeStruct((heads, length), F32),
            jax.ShapeDtypeStruct((length, LANES), F32),
        ]
        + [piece] * group,
        in_specs=[vmem()] * (len(parts) + 3),
        out_specs=[vmem()] * (4 + group),
        scratch_shapes=[pltpu.VMEM((group, states + 8, width), F32)],
        compiler_params=params(),
        cost_estimate=cost(32 * length * states * channels, 2 * length * channels),
        name="block_state",
    )(*parts, bias, rate, x)
    return result[:4], result[4:]


def local_kernel(states, x_ref, gate_ref, climb_ref, climb_t_ref, step_t_ref, maps_ref, skip_ref, still_ref, scale_ref):
    length = x_ref.shape[0]
    every = climb_ref.shape[1]
    heads = climb_t_ref.shape[0]
    shift = lax.rem(every - pl.program_id(0) * heads, jnp.int32(every))
    climb = pltpu.roll(climb_ref[...], shift, 1)
    skip = pltpu.roll(jnp.broadcast_to(widen(skip_ref[...], every), (8, every)), shift, 1)[:1]
    maps = maps_ref[...]
    inner = lax.dot_general(
        maps[:, states : 2 * states],
        maps[:, :states],
        (((1,), (1,)), ((), ())),
        precision=lax.Precision.HIGHEST,
        preferred_element_type=F32,
    )
    row = lax.broadcasted_iota(jnp.int32, (length, length), 0)
    column = lax.broadcasted_iota(jnp.int32, (length, length), 1)
    inner = jnp.where(column <= row, inner, 0.0)
    left = lax.broadcasted_iota(jnp.int32, (length, LANES), 1) < DECAY_CHANNELS

    def mix(j):
        fall = jnp.minimum(climb[:, j : j + 1] - climb_t_ref[j : j + 1], 0.0)
        return (inner * jnp.exp(fall) * step_t_ref[j : j + 1]).astype(BF16)

    for j in range(0, heads, 2):
        columns = slice(j * DECAY_CHANNELS, j * DECAY_CHANNELS + LANES)
        x = x_ref[:, columns]
        both = jnp.concatenate([mix(j), mix(j + 1)], axis=1)
        zero = jnp.zeros_like(x)
        feeds = jnp.concatenate([jnp.where(left, x, zero), jnp.where(left, zero, x)], axis=0)
        local = jnp.dot(both, feeds, preferred_element_type=F32)
        gain = jnp.where(left[:1], skip[:, j : j + 1], skip[:, j + 1 : j + 2])
        grown = jnp.exp(jnp.where(left, climb[:, j : j + 1], climb[:, j + 1 : j + 2]))
        gate = gate_ref[:, columns].astype(F32)
        silu = gate / (1.0 + jnp.exp(-gate))
        still_ref[:, columns] = (local + gain * x.astype(F32)) * silu
        scale_ref[:, columns] = grown * silu


def local_part(x, gate, climb, climb_t, step_t, maps, skip, states):
    length, channels = x.shape
    width = min(channels, 1024)
    heads = width // DECAY_CHANNELS
    every = climb.shape[1]
    wide = pl.BlockSpec((length, width), lambda i: (0, i))
    rows = pl.BlockSpec((heads, length), lambda i: (i, 0))

    def whole(array):
        return pl.BlockSpec(array.shape, lambda i: (0, 0))

    return pl.pallas_call(
        functools.partial(local_kernel, states),
        grid=(channels // width,),
        out_shape=[jax.ShapeDtypeStruct((length, channels), F32)] * 2,
        in_specs=[wide, wide, whole(climb), rows, rows, whole(maps), whole(skip)],
        out_specs=[wide, wide],
        compiler_params=params(),
        cost_estimate=cost(16 * length * length * channels, 12 * length * channels),
        name="local_part",
    )(x, gate, climb, climb_t, step_t, maps, skip)


def gather_blocks(group, piece_refs, held):
    mine = place(group)
    for k in range(group):
        held[mine ^ k] = piece_refs[k][...]


def group_total_kernel(group, states, *refs):
    out_ref, held = refs[group:]
    gather_blocks(group, refs[:group], held)
    state = held[0, :states]
    total = held[0, states:]
    for b in range(1, group):
        more = held[b, states:]
        state = jnp.exp(more[:1]) * state + held[b, :states]
        total = total + more
    out_ref[:states] = state
    out_ref[states:] = total


def group_total(pieces, group, states):
    shape = pieces[0].shape
    return pl.pallas_call(
        functools.partial(group_total_kernel, group, states),
        out_shape=jax.ShapeDtypeStruct(shape, F32),
        in_specs=[vmem()] * group,
        out_specs=vmem(),
        scratch_shapes=[pltpu.VMEM((group,) + shape, F32)],
        compiler_params=params(),
        cost_estimate=cost(0, 4 * (group + 1) * shape[0] * shape[1]),
        name="group_total",
    )(*pieces)


def entering_kernel(group, states, arrivals, *refs):
    arrival_refs = refs[group : group + arrivals]
    out_refs = refs[group + arrivals : 2 * group + arrivals]
    held, entering = refs[2 * group + arrivals :]
    gather_blocks(group, refs[:group], held)
    incoming = jnp.zeros(entering.shape[1:], F32)
    ahead = jnp.zeros((1, entering.shape[2]), F32)
    for ref in arrival_refs:
        incoming = incoming + jnp.exp(ahead) * ref[:states]
        ahead = ahead + ref[states : states + 1]
    state = incoming
    for b in range(group):
        entering[b] = state
        if b < group - 1:
            state = jnp.exp(held[b, states : states + 1]) * state + held[b, :states]
    mine = place(group)
    for k in range(group):
        out_refs[k][...] = entering[mine ^ k]


def entering_states(pieces, arrivals, group, states):
    shape = pieces[0].shape
    out = jax.ShapeDtypeStruct((states, shape[1]), F32)
    return pl.pallas_call(
        functools.partial(entering_kernel, group, states, len(arrivals)),
        out_shape=[out] * group,
        in_specs=[vmem()] * (group + len(arrivals)),
        out_specs=[vmem()] * group,
        scratch_shapes=[
            pltpu.VMEM((group,) + shape, F32),
            pltpu.VMEM((group, states, shape[1]), F32),
        ],
        compiler_params=params(),
        cost_estimate=cost(0, 4 * (2 * group + len(arrivals)) * shape[0] * shape[1]),
        name="entering_states",
    )(*pieces, *arrivals)


def carried_kernel(group, states, maps_ref, still_ref, scale_ref, *refs):
    piece_refs = refs[:group]
    gated_ref, square_ref, held = refs[group:]

    @pl.when(pl.program_id(0) == 0)
    def _():
        gather_blocks(group, piece_refs, held)
        square_ref[...] = jnp.zeros_like(square_ref)

    c = maps_ref[:, states : 2 * states]
    c_high = c.astype(BF16)
    c_low = (c - c_high.astype(F32)).astype(BF16)
    state = held[pl.program_id(0)]
    high = state.astype(BF16)
    low = (state - high.astype(F32)).astype(BF16)
    carried = jnp.dot(
        jnp.concatenate([c_high, c_low, c_high], axis=1),
        jnp.concatenate([high, high, low], axis=0),
        preferred_element_type=F32,
    )
    gated = still_ref[...] + scale_ref[...] * carried
    gated_ref[...] = gated
    square = gated * gated
    folded = square[:, :LANES]
    for at in range(LANES, square.shape[1], LANES):
        folded = folded + square[:, at : at + LANES]
    square_ref[...] += folded


def carried_part(maps, still, scale, pieces, group, states):
    length, channels = still.shape
    width = channels // group
    wide = pl.BlockSpec((length, width), lambda i: (0, i))

    def whole(array):
        return pl.BlockSpec(array.shape, lambda i: (0, 0))

    return pl.pallas_call(
        functools.partial(carried_kernel, group, states),
        grid=(group,),
        out_shape=[
            jax.ShapeDtypeStruct((length, channels), F32),
            jax.ShapeDtypeStruct((length, LANES), F32),
        ],
        in_specs=[whole(maps), wide, wide] + [whole(piece) for piece in pieces],
        out_specs=[wide, pl.BlockSpec((length, LANES), lambda i: (0, 0))],
        scratch_shapes=[pltpu.VMEM((group, states, width), F32)],
        compiler_params=params(),
        cost_estimate=cost(8 * length * states * channels, 12 * length * channels),
        name="carried_part",
    )(maps, still, scale, *pieces)


def norm_kernel(parts, every, gated_ref, gain_ref, *refs):
    square = refs[0][...]
    for ref in refs[1:parts]:
        square = square + ref[...]
    mean = jnp.sum(square, axis=1, keepdims=True) / every
    refs[parts][...] = (gated_ref[...] * lax.rsqrt(mean + 1e-05) * gain_ref[...]).astype(BF16)


def norm(gated, gain, squares, every):
    length, channels = gated.shape
    width = min(channels, 1024)
    wide = pl.BlockSpec((length, width), lambda i: (0, i))
    small = pl.BlockSpec((length, LANES), lambda i: (0, 0))
    return pl.pallas_call(
        functools.partial(norm_kernel, len(squares), every),
        grid=(channels // width,),
        out_shape=jax.ShapeDtypeStruct((length, channels), BF16),
        in_specs=[wide, pl.BlockSpec((1, width), lambda i: (0, i))] + [small] * len(squares),
        out_specs=wide,
        compiler_params=params(),
        cost_estimate=cost(4 * length * channels, 6 * length * channels),
        name="norm",
    )(gated, gain, *squares)


def shared_parts(part):
    if lax.axis_size("tp") == 2:
        return [part, lax.ppermute(part, "tp", [(0, 1), (1, 0)])]
    return [lax.psum(part, "tp")]


def mixer_layer(
    mixer_input, gate, step_weight, state_weight, step_bias, decay_rate, skip_gain, norm_gain
):
    channels = mixer_input.shape[1]
    states = state_weight.shape[1] // 2
    count = lax.axis_size("ctx")
    group = math.gcd(4, count) if channels % (16 * DECAY_CHANNELS) == 0 and channels > 1024 else 1
    turns = count // group
    parts = shared_parts(project(mixer_input, step_weight, state_weight))
    (climb, climb_t, step_t, maps), pieces = block_state(
        parts, step_bias[None], decay_rate[None], mixer_input, states, group
    )
    pieces = swap(pieces, group, count)
    still, scale = local_part(
        mixer_input, gate, climb, climb_t, step_t, maps, skip_gain[None], states
    )
    total = group_total(pieces, group, states)
    if turns <= UNROLL:
        arrivals = [climb_up(total, group, count, steps) for steps in range(1, turns)]
    else:

        def one(_, carry):
            travelling, summed, ahead = carry
            travelling = climb_up(travelling, group, count)
            summed = summed + jnp.exp(ahead) * travelling[:states]
            return travelling, summed, ahead + travelling[states : states + 1]

        start = (total, jnp.zeros_like(total[:states]), jnp.zeros_like(total[:1]))
        _, summed, _ = lax.fori_loop(1, turns, one, start)
        arrivals = [jnp.concatenate([summed, jnp.zeros_like(total[states:])], axis=0)]
    entering = swap(entering_states(pieces, arrivals, group, states), group, count)
    gated, square = carried_part(maps, still, scale, entering, group, states)
    return norm(gated, norm_gain[None], shared_parts(square), channels * lax.axis_size("tp"))


def per_device(
    queries,
    keys,
    values,
    mixer_input,
    gate,
    step_weight,
    state_weight,
    step_bias,
    decay_rate,
    skip_gain,
    norm_gain,
):
    attention_out = attention_layer(queries, keys, values)
    mamba_out = mixer_layer(
        mixer_input, gate, step_weight, state_weight, step_bias, decay_rate, skip_gain, norm_gain
    )
    return (attention_out, mamba_out)


def solution(mesh):
    return jax.shard_map(
        per_device,
        mesh=mesh,
        in_specs=(
            P("ctx", "tp"),
            P("ctx", "tp"),
            P("ctx", "tp"),
            P("ctx", "tp"),
            P("ctx", "tp"),
            P("tp", None),
            P("tp", None),
            P("tp"),
            P("tp"),
            P("tp"),
            P("tp"),
        ),
        out_specs=(P("ctx", "tp"), P("ctx", "tp")),
        check_vma=False,
    )
```

```python
import functools
import math

import jax
import jax.numpy as jnp
from jax import lax
from jax.experimental import pallas as pl
from jax.experimental.pallas import tpu as pltpu
from jax.sharding import PartitionSpec as P

HD = 128
DECAY_CHANNELS = 64
SCAN_TOKENS = 128
LANES = 128
UNROLL = 8
VMEM_LIMIT = 32 * 1024 * 1024

F32 = jnp.float32
BF16 = jnp.bfloat16


def vmem():
    return pl.BlockSpec(memory_space=pltpu.VMEM)


def params():
    return pltpu.CompilerParams(vmem_limit_bytes=VMEM_LIMIT)


def cost(flops, size, transcendentals=0):
    return pl.CostEstimate(flops=flops, bytes_accessed=size, transcendentals=transcendentals)


def near(group, count):
    return [list(range(at, at + group)) for at in range(0, count, group)]


def far(group, count):
    return [list(range(at, count, group)) for at in range(group)]


def trade(array, groups):
    if len(groups[0]) == 1:
        return array
    return lax.all_to_all(array, "ctx", 0, 0, axis_index_groups=groups)


def climb_up(array, group, count):
    return lax.ppermute(array, "ctx", [(i, i + group) for i in range(count - group)])


def pack_kv_kernel(k_ref, v_ref, out_ref):
    width = out_ref.shape[3]
    for i in range(out_ref.shape[0]):
        columns = slice(i * width, (i + 1) * width)
        out_ref[i, 0] = k_ref[:, columns]
        out_ref[i, 1] = v_ref[:, columns]


def pack_kv(keys, values, group):
    length, width = keys.shape
    return pl.pallas_call(
        pack_kv_kernel,
        out_shape=jax.ShapeDtypeStruct((group, 2, length, width // group), keys.dtype),
        in_specs=[vmem()] * 2,
        out_specs=vmem(),
        compiler_params=params(),
        cost_estimate=cost(0, 8 * length * width),
        name="pack_kv",
    )(keys, values)


def pack_q_kernel(q_ref, out_ref):
    width = out_ref.shape[2]
    for i in range(out_ref.shape[0]):
        out_ref[i] = q_ref[:, i * width : (i + 1) * width]


def pack_q(queries, group):
    length, width = queries.shape
    return pl.pallas_call(
        pack_q_kernel,
        out_shape=jax.ShapeDtypeStruct((group, length, width // group), queries.dtype),
        in_specs=[vmem()],
        out_specs=vmem(),
        compiler_params=params(),
        cost_estimate=cost(0, 4 * length * width),
        name="pack_q",
    )(queries)


def join_kernel(in_ref, out_ref):
    width = in_ref.shape[2]
    for i in range(in_ref.shape[0]):
        out_ref[:, i * width : (i + 1) * width] = in_ref[i]


def join(pieces):
    group, length, width = pieces.shape
    return pl.pallas_call(
        join_kernel,
        out_shape=jax.ShapeDtypeStruct((length, width * group), pieces.dtype),
        in_specs=[vmem()],
        out_specs=vmem(),
        compiler_params=params(),
        cost_estimate=cost(0, 4 * length * width * group),
        name="join_heads",
    )(pieces)


def flash_chunk(q_ref, kv_ref, before, after, extended, own):
    group, length, width = q_ref.shape
    heads = width // HD
    kv_heads = kv_ref.shape[3] // HD
    share = heads // kv_heads
    rows = group * length
    tile = min(rows, 2 * length)
    rate = math.log2(math.e) / math.sqrt(HD)
    for kv in range(kv_heads):
        lanes = slice(kv * HD, (kv + 1) * HD)
        keys = kv_ref[:, 0, :, lanes].reshape(rows, HD)
        extended[:, :HD] = kv_ref[:, 1, :, lanes].reshape(rows, HD)
        extended[:, HD:] = jnp.ones((rows, HD), BF16)
        tiles = [
            (h, start)
            for h in range(kv * share, (kv + 1) * share)
            for start in range(0, rows, tile)
        ]

        def score(h, start):
            q = q_ref[start // length : (start + tile) // length, :, h * HD : (h + 1) * HD]
            used = keys[: start + tile] if own else keys
            scores = lax.dot_general(
                q.reshape(tile, HD), used, (((1,), (1,)), ((), ())), preferred_element_type=F32
            )
            if not own:
                return scores
            row = lax.broadcasted_iota(jnp.int32, (tile, tile), 0)
            column = lax.broadcasted_iota(jnp.int32, (tile, tile), 1)
            edge = jnp.where(column <= row, scores[:, start:], -1e30)
            return jnp.concatenate([scores[:, :start], edge], axis=1) if start else edge

        ahead = score(*tiles[0])
        for n, (h, start) in enumerate(tiles):
            scores = ahead
            if n + 1 < len(tiles):
                ahead = score(*tiles[n + 1])
            here = slice(start, start + tile)
            top = jnp.max(scores, axis=1, keepdims=True)
            if not own:
                top_before = before[1][h, here]
                top = jnp.maximum(top_before[:, :1], top)
            weights = jnp.exp2((scores - top) * rate).astype(BF16)
            value = jnp.dot(weights, extended[: scores.shape[1]], preferred_element_type=F32)
            top = jnp.broadcast_to(top, (tile, LANES))
            if not own:
                keep = jnp.exp2((top_before - top) * rate)
                value = value + before[0][h, here] * jnp.concatenate([keep, keep], axis=1)
            yield h, start, tile, value
            if after is not None:
                after[0][h, here] = value
                after[1][h, here] = top


def finish_rows(out_ref, h, start, tile, value):
    length = out_ref.shape[1]
    result = (value[:, :HD] / value[:, HD:]).astype(BF16).reshape(tile // length, length, HD)
    out_ref[start // length : (start + tile) // length, :, h * HD : (h + 1) * HD] = result


def flash_kernel(own, chunks, final, base, *refs):
    refs = list(refs)
    base_ref = refs.pop(0) if base is None else None
    first = base_ref[0] if base is None else base
    q_ref = refs.pop(0)
    own_ref = refs.pop(0) if own else None
    state = None if own else (refs.pop(0), refs.pop(0))
    chunk_refs = [refs.pop(0) for _ in range(chunks)]
    extended = refs.pop()
    turn = lax.axis_index("ctx") // q_ref.shape[0]
    heads = q_ref.shape[2] // HD
    rows = q_ref.shape[0] * q_ref.shape[1]
    after = None if final else tuple(refs)
    if own:
        for done in flash_chunk(q_ref, own_ref, None, after, extended, True):
            if final:
                finish_rows(refs[0], *done)
        state = after
    for number, ref in enumerate(chunk_refs):

        @pl.when(turn >= first + number)
        def _(ref=ref, state=state):
            for done in flash_chunk(q_ref, ref, state, after, extended, False):
                if final:
                    finish_rows(refs[0], *done)

        if not own:

            @pl.when(turn < first + number)
            def _(state=state):
                for h in range(heads):
                    if final:
                        finish_rows(refs[0], h, 0, rows, state[0][h])
                    else:
                        after[0][h] = state[0][h]
                        after[1][h] = state[1][h]


def flash(q, own=None, state=(), chunks=(), final=False, base=1):
    group, length, width = q.shape
    heads = width // HD
    rows = group * length
    fixed = base if isinstance(base, int) else None
    operands, specs = [], []
    if fixed is None:
        operands.append(base)
        specs.append(pl.BlockSpec(memory_space=pltpu.SMEM))
    rest = [q] + ([own] if own is not None else []) + list(state) + list(chunks)
    operands += rest
    specs += [vmem()] * len(rest)
    if final:
        out_shape = [jax.ShapeDtypeStruct(q.shape, BF16)]
    else:
        out_shape = [
            jax.ShapeDtypeStruct((heads, rows, HD + LANES), F32),
            jax.ShapeDtypeStruct((heads, rows, LANES), F32),
        ]
    parts = len(chunks) + (own is not None)
    return pl.pallas_call(
        functools.partial(flash_kernel, own is not None, len(chunks), final, fixed),
        out_shape=out_shape,
        in_specs=specs,
        out_specs=[vmem()] * len(out_shape),
        scratch_shapes=[pltpu.VMEM((rows, HD + LANES), BF16)],
        compiler_params=params(),
        cost_estimate=cost(4 * heads * rows * rows * HD * parts, 4 * heads * rows * HD),
        name="flash",
    )(*operands)


def attention_layer(queries, keys, values):
    count = lax.axis_size("ctx")
    group = math.gcd(keys.shape[1] // HD, count)
    turns = count // group
    groups = near(group, count)
    own = trade(pack_kv(keys, values, group), groups)
    q = trade(pack_q(queries, group), groups)
    if turns == 1:
        (out,) = flash(q, own=own, final=True)
    elif turns <= UNROLL:
        arrived = [own]
        for _ in range(turns - 1):
            arrived.append(climb_up(arrived[-1], group, count))
        state = flash(q, own=own, chunks=arrived[1:-1])
        (out,) = flash(q, state=state, chunks=arrived[-1:], final=True, base=turns - 1)
    else:
        state = flash(q, own=own)

        def one(step, carry):
            chunk, state = carry
            chunk = climb_up(chunk, group, count)
            return chunk, tuple(flash(q, state=state, chunks=[chunk], base=jnp.reshape(step, (1,))))

        chunk, state = lax.fori_loop(1, turns - 1, one, (own, tuple(state)))
        chunk = climb_up(chunk, group, count)
        (out,) = flash(q, state=state, chunks=[chunk], final=True, base=turns - 1)
    return join(trade(out, groups))


def project_kernel(x_ref, step_ref, map_ref, out_ref):
    heads = step_ref.shape[1]
    width = map_ref.shape[0]
    x = x_ref[...]
    out_ref[:, :heads] = jnp.dot(x, step_ref[...], preferred_element_type=F32)
    maps = lax.dot_general(x, map_ref[...], (((1,), (1,)), ((), ())), preferred_element_type=F32)
    out_ref[:, heads:] = widen(maps, LANES)


def project(x, step_weight, state_weight):
    length, channels = x.shape
    heads = step_weight.shape[1]
    return pl.pallas_call(
        project_kernel,
        out_shape=jax.ShapeDtypeStruct((length, heads + LANES), F32),
        in_specs=[vmem()] * 3,
        out_specs=vmem(),
        compiler_params=params(),
        cost_estimate=cost(4 * length * channels * heads, 6 * channels * LANES),
        name="project",
    )(x, step_weight, state_weight.T)


def widen(row, lanes):
    extra = lanes - row.shape[1]
    if not extra:
        return row
    return jnp.concatenate([row, jnp.zeros((row.shape[0], extra), row.dtype)], axis=1)


def spread(row, at, count):
    span = count * DECAY_CHANNELS
    owner = lax.broadcasted_iota(jnp.int32, (1, span), 1) // DECAY_CHANNELS
    result = jnp.broadcast_to(row[:, at : at + 1], (1, span))
    for i in range(1, count):
        result = jnp.where(owner == i, row[:, at + i : at + i + 1], result)
    return result


def pack_row(row, rows):
    high = row.astype(BF16).astype(F32)
    rest = row - high
    middle = rest.astype(BF16).astype(F32)
    low = rest - middle
    return jnp.concatenate([high, middle, low, jnp.zeros((rows - 3, row.shape[1]), F32)], axis=0)


def unpack_row(rows):
    rows = rows.astype(F32)
    return rows[0:1] + rows[1:2] + rows[2:3]


def spread_total(rows, heads):
    row = unpack_row(rows)
    count = min(4, heads)
    return jnp.concatenate([spread(row, at, count) for at in range(0, heads, count)], axis=1)


def state_kernel(parts, states, *refs):
    part_refs = refs[:parts]
    bias_ref, rate_ref, x_ref = refs[parts : parts + 3]
    climb_ref, climb_t_ref, step_t_ref, maps_ref, out_ref = refs[parts + 3 :]
    summed = part_refs[0][...]
    for ref in part_refs[1:]:
        summed = summed + ref[...]
    length = summed.shape[0]
    every = summed.shape[1] - LANES
    heads = bias_ref.shape[1]
    shift = lax.rem(every - lax.axis_index("tp") * heads, jnp.int32(every))
    raw = pltpu.roll(summed[:, :every], shift, 1) + widen(bias_ref[...], every)
    step = jnp.maximum(raw, 0.0) + jnp.log1p(jnp.exp(-jnp.abs(raw)))
    log_decay = -widen(rate_ref[...], every) * step
    row = lax.broadcasted_iota(jnp.int32, (length, length), 0)
    column = lax.broadcasted_iota(jnp.int32, (length, length), 1)
    lower = (column <= row).astype(F32)
    climb = jnp.dot(lower, log_decay, precision=lax.Precision.HIGHEST, preferred_element_type=F32)
    maps = summed[:, every:]
    climb_ref[...] = climb
    maps_ref[...] = maps
    climb_t = climb.T
    step_t = step.T
    climb_t_ref[...] = climb_t[:heads]
    step_t_ref[...] = step_t[:heads]
    b_t = maps.T[:states]
    weight_t = jnp.exp(climb_t[:, length - 1 :] - climb_t) * step_t
    bundle = 4
    span = bundle * DECAY_CHANNELS
    owner = lax.broadcasted_iota(jnp.int32, (1, span), 1) // DECAY_CHANNELS
    group = out_ref.shape[0]
    width = out_ref.shape[2] - LANES
    for at in range(0, heads, bundle):
        feed = jnp.concatenate([b_t * weight_t[at + i : at + i + 1] for i in range(bundle)], axis=0)
        columns = slice(at * DECAY_CHANNELS, at * DECAY_CHANNELS + span)
        product = jnp.dot(feed.astype(BF16), x_ref[:, columns], preferred_element_type=F32)
        state = product[:states]
        for i in range(1, bundle):
            state = jnp.where(owner == i, product[i * states : (i + 1) * states], state)
        piece, offset = divmod(columns.start, width)
        out_ref[piece, :, offset : offset + span] = state.astype(BF16)
    totals = pack_row(climb[length - 1 :], states)
    for piece in range(group):
        at = piece * (heads // group)
        here = totals if not at else pltpu.roll(totals, every - at, 1)
        out_ref[piece, :, width:] = here[:, :LANES].astype(BF16)


def block_state(parts, bias, rate, x, states, group):
    length, channels = x.shape
    every = parts[0].shape[1] - LANES
    heads = bias.shape[1]
    width = channels // group
    return pl.pallas_call(
        functools.partial(state_kernel, len(parts), states),
        out_shape=[
            jax.ShapeDtypeStruct((length, every), F32),
            jax.ShapeDtypeStruct((heads, length), F32),
            jax.ShapeDtypeStruct((heads, length), F32),
            jax.ShapeDtypeStruct((length, LANES), F32),
            jax.ShapeDtypeStruct((group, states, width + LANES), BF16),
        ],
        in_specs=[vmem()] * (len(parts) + 3),
        out_specs=[vmem()] * 5,
        compiler_params=params(),
        cost_estimate=cost(32 * length * states * channels, 2 * length * channels),
        name="block_state",
    )(*parts, bias, rate, x)


def local_kernel(
    states, x_ref, gate_ref, climb_ref, climb_t_ref, step_t_ref, maps_ref, skip_ref, still_ref, scale_ref
):
    length = x_ref.shape[0]
    heads = climb_t_ref.shape[0]
    maps = maps_ref[...]
    inner = lax.dot_general(
        maps[:, states : 2 * states],
        maps[:, :states],
        (((1,), (1,)), ((), ())),
        precision=lax.Precision.HIGHEST,
        preferred_element_type=F32,
    )
    row = lax.broadcasted_iota(jnp.int32, (length, length), 0)
    column = lax.broadcasted_iota(jnp.int32, (length, length), 1)
    inner = jnp.where(column <= row, inner, 0.0)
    left = lax.broadcasted_iota(jnp.int32, (length, LANES), 1) < DECAY_CHANNELS

    for j in range(0, heads, 2):
        columns = slice(j * DECAY_CHANNELS, j * DECAY_CHANNELS + LANES)
        x = x_ref[:, columns]
        wide = [jnp.broadcast_to(climb_ref[:, i : i + 1], (length, length)) for i in (j, j + 1)]
        mixed = []
        for i in (j, j + 1):
            fall = jnp.minimum(wide[i - j] - climb_t_ref[i : i + 1], 0.0)
            mixed.append((inner * jnp.exp(fall) * step_t_ref[i : i + 1]).astype(BF16))
        zero = jnp.zeros_like(x)
        feeds = jnp.concatenate([jnp.where(left, x, zero), jnp.where(left, zero, x)], axis=0)
        local = jnp.dot(jnp.concatenate(mixed, axis=1), feeds, preferred_element_type=F32)
        gain = jnp.where(left[:1], skip_ref[:, j : j + 1], skip_ref[:, j + 1 : j + 2])
        grown = jnp.exp(jnp.where(left, wide[0], wide[1]))
        gate = gate_ref[:, columns].astype(F32)
        silu = gate / (1.0 + jnp.exp(-gate))
        still_ref[:, columns] = (local + gain * x.astype(F32)) * silu
        scale_ref[:, columns] = grown * silu


def local_part(x, gate, climb, climb_t, step_t, maps, skip, states):
    length, channels = x.shape
    return pl.pallas_call(
        functools.partial(local_kernel, states),
        out_shape=[jax.ShapeDtypeStruct((length, channels), F32)] * 2,
        in_specs=[vmem()] * 7,
        out_specs=[vmem()] * 2,
        compiler_params=params(),
        cost_estimate=cost(16 * length * length * channels, 12 * length * channels),
        name="local_part",
    )(x, gate, climb, climb_t, step_t, maps, skip)


def total_kernel(heads, in_ref, out_ref):
    group, states, lanes = in_ref.shape
    width = lanes - LANES
    state = in_ref[0, :, :width].astype(F32)
    total = unpack_row(in_ref[0, :, width:])
    for b in range(1, group):
        state = jnp.exp(spread_total(in_ref[b, :, width:], heads)) * state
        state = state + in_ref[b, :, :width].astype(F32)
        total = total + unpack_row(in_ref[b, :, width:])
    state = state.astype(BF16)
    total = pack_row(total, states).astype(BF16)
    for z in range(out_ref.shape[0]):
        out_ref[z, :, :width] = state
        out_ref[z, :, width:] = total


def group_total(blocks, heads, copies):
    group, states, lanes = blocks.shape
    return pl.pallas_call(
        functools.partial(total_kernel, heads),
        out_shape=jax.ShapeDtypeStruct((copies, states, lanes), BF16),
        in_specs=[vmem()],
        out_specs=vmem(),
        compiler_params=params(),
        cost_estimate=cost(0, 4 * (group + copies) * states * lanes),
        name="group_total",
    )(blocks)


def entering_kernel(heads, chosen, in_ref, earlier_ref, out_ref):
    group, states, lanes = in_ref.shape
    width = lanes - LANES
    turn = lax.axis_index("ctx") // group
    state = jnp.zeros((states, width), F32)
    for z in range(earlier_ref.shape[0]):
        more = jnp.exp(spread_total(earlier_ref[z, :, width:], heads)) * state
        more = more + earlier_ref[z, :, :width].astype(F32)
        state = jnp.where(z < turn, more, state) if chosen else more
    for b in range(group):
        out_ref[b] = state.astype(BF16)
        if b < group - 1:
            state = jnp.exp(spread_total(in_ref[b, :, width:], heads)) * state
            state = state + in_ref[b, :, :width].astype(F32)


def entering_states(blocks, earlier, heads, chosen):
    group, states, lanes = blocks.shape
    return pl.pallas_call(
        functools.partial(entering_kernel, heads, chosen),
        out_shape=jax.ShapeDtypeStruct((group, states, lanes - LANES), BF16),
        in_specs=[vmem()] * 2,
        out_specs=vmem(),
        compiler_params=params(),
        cost_estimate=cost(0, 4 * (group + earlier.shape[0]) * states * lanes),
        name="entering_states",
    )(blocks, earlier)


def carried_kernel(states, maps_ref, still_ref, scale_ref, state_ref, gated_ref, square_ref):
    c = maps_ref[:, states : 2 * states]
    c_high = c.astype(BF16)
    c_low = (c - c_high.astype(F32)).astype(BF16)
    c = jnp.concatenate([c_high, c_low], axis=1)
    width = state_ref.shape[2]
    span = min(width, 512)
    folded = jnp.zeros(square_ref.shape, F32)
    for at in range(0, still_ref.shape[1], span):
        piece, offset = divmod(at, width)
        state = state_ref[piece, :, offset : offset + span]
        carried = jnp.dot(c, jnp.concatenate([state, state], axis=0), preferred_element_type=F32)
        columns = slice(at, at + span)
        gated = still_ref[:, columns] + scale_ref[:, columns] * carried
        gated_ref[:, columns] = gated
        square = gated * gated
        for lane in range(0, span, LANES):
            folded = folded + square[:, lane : lane + LANES]
    square_ref[...] = folded


def carried_part(maps, still, scale, entering, states):
    length, channels = still.shape
    return pl.pallas_call(
        functools.partial(carried_kernel, states),
        out_shape=[
            jax.ShapeDtypeStruct((length, channels), F32),
            jax.ShapeDtypeStruct((length, LANES), F32),
        ],
        in_specs=[vmem()] * 4,
        out_specs=[vmem()] * 2,
        compiler_params=params(),
        cost_estimate=cost(8 * length * states * channels, 12 * length * channels),
        name="carried_part",
    )(maps, still, scale, entering)


def norm_kernel(parts, every, gated_ref, gain_ref, *refs):
    square = refs[0][...]
    for ref in refs[1:parts]:
        square = square + ref[...]
    mean = jnp.sum(square, axis=1, keepdims=True) / every
    factor = jnp.broadcast_to(lax.rsqrt(mean + 1e-05), square.shape)
    out_ref = refs[parts]
    for at in range(0, gated_ref.shape[1], LANES):
        columns = slice(at, at + LANES)
        out_ref[:, columns] = (gated_ref[:, columns] * factor * gain_ref[:, columns]).astype(BF16)


def norm(gated, gain, squares, every):
    length, channels = gated.shape
    return pl.pallas_call(
        functools.partial(norm_kernel, len(squares), every),
        out_shape=jax.ShapeDtypeStruct((length, channels), BF16),
        in_specs=[vmem()] * (2 + len(squares)),
        out_specs=vmem(),
        compiler_params=params(),
        cost_estimate=cost(4 * length * channels, 6 * length * channels),
        name="norm",
    )(gated, gain, *squares)


def shared_parts(part):
    if lax.axis_size("tp") == 2:
        return [part, lax.ppermute(part, "tp", [(0, 1), (1, 0)])]
    return [lax.psum(part, "tp")]


def mixer_layer(
    mixer_input, gate, step_weight, state_weight, step_bias, decay_rate, skip_gain, norm_gain
):
    channels = mixer_input.shape[1]
    states = state_weight.shape[1] // 2
    count = lax.axis_size("ctx")
    group = math.gcd(math.gcd(4, count), channels // (4 * DECAY_CHANNELS))
    turns = count // group
    heads = channels // DECAY_CHANNELS // group
    parts = shared_parts(project(mixer_input, step_weight, state_weight))
    climb, climb_t, step_t, maps, blocks = block_state(
        parts, step_bias[None], decay_rate[None], mixer_input, states, group
    )
    blocks = trade(blocks, near(group, count))
    still, scale = local_part(
        mixer_input, gate, climb, climb_t, step_t, maps, skip_gain[None], states
    )
    if turns <= UNROLL:
        total = group_total(blocks, heads, turns)
        entering = entering_states(blocks, trade(total, far(group, count)), heads, True)
    else:
        total = group_total(blocks, heads, 1)[0]
        width = total.shape[1] - LANES

        def one(_, carry):
            travelling, summed, ahead = carry
            travelling = climb_up(travelling, group, count)
            summed = summed + jnp.exp(ahead) * travelling[:, :width].astype(F32)
            more = unpack_row(travelling[:, width : width + heads])
            return travelling, summed, ahead + jnp.repeat(more, DECAY_CHANNELS, axis=1)

        start = (total, jnp.zeros((states, width), F32), jnp.zeros((1, width), F32))
        _, summed, _ = lax.fori_loop(1, turns, one, start)
        earlier = jnp.concatenate([summed.astype(BF16), jnp.zeros((states, LANES), BF16)], axis=1)
        entering = entering_states(blocks, earlier[None], heads, False)
    entering = trade(entering, near(group, count))
    gated, square = carried_part(maps, still, scale, entering, states)
    return norm(gated, norm_gain[None], shared_parts(square), channels * lax.axis_size("tp"))


def per_device(
    queries,
    keys,
    values,
    mixer_input,
    gate,
    step_weight,
    state_weight,
    step_bias,
    decay_rate,
    skip_gain,
    norm_gain,
):
    attention_out = attention_layer(queries, keys, values)
    mamba_out = mixer_layer(
        mixer_input, gate, step_weight, state_weight, step_bias, decay_rate, skip_gain, norm_gain
    )
    return (attention_out, mamba_out)


def solution(mesh):
    return jax.shard_map(
        per_device,
        mesh=mesh,
        in_specs=(
            P("ctx", "tp"),
            P("ctx", "tp"),
            P("ctx", "tp"),
            P("ctx", "tp"),
            P("ctx", "tp"),
            P("tp", None),
            P("tp", None),
            P("tp"),
            P("tp"),
            P("tp"),
            P("tp"),
        ),
        out_specs=(P("ctx", "tp"), P("ctx", "tp")),
        check_vma=False,
    )
```

```python
import functools
import math

import jax
import jax.numpy as jnp
from jax import lax
from jax.experimental import pallas as pl
from jax.experimental.pallas import tpu as pltpu
from jax.sharding import PartitionSpec as P

HD = 128
DECAY_CHANNELS = 64
SCAN_TOKENS = 128
LANES = 128
UNROLL = 8
VMEM_LIMIT = 32 * 1024 * 1024

F32 = jnp.float32
BF16 = jnp.bfloat16


def vmem():
    return pl.BlockSpec(memory_space=pltpu.VMEM)


def hbm():
    return pl.BlockSpec(memory_space=pltpu.HBM)


def launch(kernel, name, out_shape, *inputs, after=(), flops=0, scratch=(), in_specs=None, out_specs=None):
    count, skip = len(inputs), len(after)
    single = isinstance(out_shape, jax.ShapeDtypeStruct)
    shapes = [out_shape] if single else list(out_shape)
    size = sum(x.size * x.dtype.itemsize for x in list(inputs) + shapes)

    def body(*refs):
        kernel(*refs[:count], *refs[count + skip :])

    result = pl.pallas_call(
        body,
        out_shape=shapes,
        in_specs=(in_specs or [vmem()] * count) + [pl.BlockSpec(memory_space=pl.ANY)] * skip,
        out_specs=out_specs or [vmem()] * len(shapes),
        scratch_shapes=list(scratch),
        compiler_params=pltpu.CompilerParams(vmem_limit_bytes=VMEM_LIMIT),
        cost_estimate=pl.CostEstimate(flops=flops, bytes_accessed=size, transcendentals=0),
        name=name,
    )(*inputs, *after)
    return result[0] if single else result


def place(group):
    return lax.rem(lax.axis_index("ctx"), jnp.int32(group))


def swap(pieces, group, count):
    result = [pieces[0]]
    for k in range(1, group):
        perm = [(i, (i // group) * group + ((i % group) ^ k)) for i in range(count)]
        result.append(lax.ppermute(pieces[k], "ctx", perm))
    return result


def climb_up(array, group, count, steps=1):
    perm = [(i, i + group * steps) for i in range(count - group * steps)]
    return lax.ppermute(array, "ctx", perm)


def shape_of(shape, dtype):
    return jax.ShapeDtypeStruct(shape, dtype)


def tie(array, after):
    return pl.pallas_call(
        lambda *refs: None,
        out_shape=shape_of(array.shape, array.dtype),
        in_specs=[pl.BlockSpec(memory_space=pl.ANY)] * (1 + len(after)),
        out_specs=pl.BlockSpec(memory_space=pl.ANY),
        input_output_aliases={0: 0},
        name="tie",
    )(array, *after)


def pack_kv(keys, values, group):
    length, width = keys.shape
    width = width // group

    def kernel(k_ref, v_ref, *refs):
        outs, sems = refs[:group], refs[group]
        mine = place(group)
        copies = []
        for k in reversed(range(group)):
            columns = pl.ds(pl.multiple_of((mine ^ k) * width, width), width)
            for n, ref in enumerate((k_ref, v_ref)):
                copies.append(
                    pltpu.make_async_copy(ref.at[:, columns], outs[k].at[n], sems.at[k, n])
                )
        for copy in copies:
            copy.start()
        for copy in copies:
            copy.wait()

    return launch(
        kernel,
        "pack_kv",
        [shape_of((2, length, width), keys.dtype)] * group,
        keys,
        values,
        in_specs=[hbm()] * 2,
        scratch=[pltpu.SemaphoreType.DMA((group, 2))],
    )


def join(pieces, group):
    length, width = pieces[0].shape

    def kernel(*refs):
        out_ref, sems = refs[group:]
        mine = place(group)
        copies = []
        for k in range(group):
            columns = pl.ds(pl.multiple_of((mine ^ k) * width, width), width)
            copies.append(pltpu.make_async_copy(refs[k], out_ref.at[:, columns], sems.at[k]))
        for copy in copies:
            copy.start()
        for copy in copies:
            copy.wait()

    return launch(
        kernel,
        "join_heads",
        shape_of((length, width * group), pieces[0].dtype),
        *pieces,
        out_specs=[hbm()],
        scratch=[pltpu.SemaphoreType.DMA((group,))],
    )


def flash_chunk(q_refs, kv_ref, before, after, extended, own, length):
    group = len(q_refs)
    heads = q_refs[0].shape[1] // HD
    kv_heads = kv_ref.shape[3] // HD
    share = heads // kv_heads
    rows = group * length
    tile = min(rows, 2 * length)
    rate = math.log2(math.e) / math.sqrt(HD)
    for kv in range(kv_heads):
        lanes = slice(kv * HD, (kv + 1) * HD)
        keys = kv_ref[:, 0, :, lanes].reshape(rows, HD)
        extended[:, :HD] = kv_ref[:, 1, :, lanes].reshape(rows, HD)
        extended[:, HD:] = jnp.ones((rows, HD), BF16)
        tiles = [
            (h, start)
            for start in range(0, rows, tile)
            for h in range(kv * share, (kv + 1) * share)
        ]

        def score(h, start):
            parts = q_refs[start // length : (start + tile) // length]
            q = [ref[:length, h * HD : (h + 1) * HD] for ref in parts]
            q = jnp.concatenate(q, axis=0) if len(q) > 1 else q[0]
            scores = lax.dot_general(
                q, keys, (((1,), (1,)), ((), ())), preferred_element_type=F32
            )
            if own:
                flip = place(group) * length
                row = (lax.broadcasted_iota(jnp.int32, (tile, rows), 0) + start) ^ flip
                column = lax.broadcasted_iota(jnp.int32, (tile, rows), 1) ^ flip
                scores = jnp.where(column <= row, scores, -1e30)
            return scores

        ahead = score(*tiles[0])
        for n, (h, start) in enumerate(tiles):
            scores = ahead
            if n + 1 < len(tiles):
                ahead = score(*tiles[n + 1])
            here = slice(start, start + tile)
            top = jnp.max(scores, axis=1, keepdims=True)
            if not own:
                top_before = before[1][h, here]
                top = jnp.maximum(top_before[:, :1], top)
            weights = jnp.exp2((scores - top) * rate).astype(BF16)
            value = jnp.dot(weights, extended[...], preferred_element_type=F32)
            top = jnp.broadcast_to(top, (tile, LANES))
            if not own:
                keep = jnp.exp2((top_before - top) * rate)
                value = value + before[0][h, here] * jnp.concatenate([keep, keep], axis=1)
            yield h, start, tile, value
            if after is not None:
                after[0][h, here] = value
                after[1][h, here] = top


def finish_rows(out_refs, h, start, tile, value):
    length = out_refs[0].shape[0]
    result = (value[:, :HD] / value[:, HD:]).astype(BF16)
    for at in range(0, tile, length):
        out_refs[(start + at) // length][:, h * HD : (h + 1) * HD] = result[at : at + length]


def flash(q, length, own=None, state=(), chunks=(), final=False, base=1, after=()):
    group = len(q)
    heads = q[0].shape[1] // HD
    rows = group * length
    fixed = isinstance(base, int)
    has_own = own is not None
    specs = [] if fixed else [pl.BlockSpec(memory_space=pltpu.SMEM)]
    rest = list(q) + ([own] if has_own else []) + list(state) + list(chunks)
    specs = specs + [vmem()] * len(rest)

    def kernel(*refs):
        refs = list(refs)
        first = base if fixed else refs.pop(0)[0]
        q_refs = [refs.pop(0) for _ in range(group)]
        own_ref = refs.pop(0) if has_own else None
        held = None if has_own else (refs.pop(0), refs.pop(0))
        chunk_refs = [refs.pop(0) for _ in range(len(chunks))]
        extended = refs.pop()
        turn = lax.axis_index("ctx") // group
        outs = None if final else tuple(refs)
        if has_own:
            for done in flash_chunk(q_refs, own_ref, None, outs, extended, True, length):
                if final:
                    finish_rows(refs, *done)
            held = outs
        for number, ref in enumerate(chunk_refs):

            @pl.when(turn >= first + number)
            def _(ref=ref, held=held):
                for done in flash_chunk(q_refs, ref, held, outs, extended, False, length):
                    if final:
                        finish_rows(refs, *done)

            if not has_own and number == 0:

                @pl.when(turn < first)
                def _(held=held):
                    for h in range(heads):
                        if final:
                            finish_rows(refs, h, 0, rows, held[0][h])
                        else:
                            outs[0][h] = held[0][h]
                            outs[1][h] = held[1][h]

            held = outs

    if final:
        out_shape = [shape_of((length, heads * HD), BF16)] * group
    else:
        out_shape = [
            shape_of((heads, rows, HD + LANES), F32),
            shape_of((heads, rows, LANES), F32),
        ]
    parts = len(chunks) + has_own
    return launch(
        kernel,
        "flash",
        out_shape,
        *([] if fixed else [base]),
        *rest,
        after=after,
        in_specs=specs,
        flops=4 * heads * rows * rows * HD * parts,
        scratch=[pltpu.VMEM((rows, HD + LANES), BF16)],
    )


def widen(row, lanes):
    extra = lanes - row.shape[1]
    if not extra:
        return row
    return jnp.concatenate([row, jnp.zeros((row.shape[0], extra), row.dtype)], axis=1)


def project(x, step_weight, state_weight, after=()):
    length, channels = x.shape
    heads = step_weight.shape[1]

    def kernel(x_ref, step_ref, map_ref, out_ref):
        x = x_ref[...]
        out_ref[:, :heads] = jnp.dot(x, step_ref[...], preferred_element_type=F32)
        maps = lax.dot_general(
            x, map_ref[...], (((1,), (1,)), ((), ())), preferred_element_type=F32
        )
        out_ref[:, heads:] = widen(maps, LANES)

    return launch(
        kernel,
        "project",
        shape_of((length, heads + LANES), F32),
        x,
        step_weight,
        state_weight.T,
        after=after,
        flops=4 * length * channels * heads,
    )


def spread(row, at, count):
    span = count * DECAY_CHANNELS
    owner = lax.broadcasted_iota(jnp.int32, (1, span), 1) // DECAY_CHANNELS
    result = jnp.broadcast_to(row[:, at : at + 1], (1, span))
    for i in range(1, count):
        result = jnp.where(owner == i, row[:, at + i : at + i + 1], result)
    return result


def pack_row(row, rows):
    high = row.astype(BF16).astype(F32)
    rest = row - high
    middle = rest.astype(BF16).astype(F32)
    low = rest - middle
    return jnp.concatenate([high, middle, low, jnp.zeros((rows - 3, row.shape[1]), F32)], axis=0)


def unpack_row(rows):
    rows = rows.astype(F32)
    return rows[0:1] + rows[1:2] + rows[2:3]


def spread_total(rows, heads):
    row = unpack_row(rows)
    count = min(4, heads)
    return jnp.concatenate([spread(row, at, count) for at in range(0, heads, count)], axis=1)


def block_state(parts, bias, rate, x, q, states, group, after=()):
    length, channels = x.shape
    every = parts[0].shape[1] - LANES
    heads = bias.shape[1]
    width = channels // group
    columns = q.shape[1] // group
    bands = width // columns
    count = len(parts)

    def kernel(*refs):
        bias_ref, rate_ref, x_ref, q_ref = refs[count : count + 4]
        climb_ref, climb_t_ref, step_t_ref, maps_ref = refs[count + 4 : count + 8]
        outs = refs[count + 8 : count + 8 + group]
        held = refs[count + 8 + group]
        summed = refs[0][...]
        for ref in refs[1:count]:
            summed = summed + ref[...]
        shift = lax.rem(every - lax.axis_index("tp") * heads, jnp.int32(every))
        raw = pltpu.roll(summed[:, :every], shift, 1) + widen(bias_ref[...], every)
        step = jnp.maximum(raw, 0.0) + jnp.log1p(jnp.exp(-jnp.abs(raw)))
        log_decay = -widen(rate_ref[...], every) * step
        row = lax.broadcasted_iota(jnp.int32, (length, length), 0)
        column = lax.broadcasted_iota(jnp.int32, (length, length), 1)
        lower = (column <= row).astype(F32)
        climb = jnp.dot(
            lower, log_decay, precision=lax.Precision.HIGHEST, preferred_element_type=F32
        )
        maps = summed[:, every:]
        climb_ref[...] = climb
        maps_ref[...] = maps
        climb_t = climb.T
        step_t = step.T
        climb_t_ref[...] = climb_t[:heads]
        step_t_ref[...] = step_t[:heads]
        b_t = maps.T[:states]
        weight_t = jnp.exp(climb_t[:, length - 1 :] - climb_t) * step_t
        bundle = 4
        span = bundle * DECAY_CHANNELS
        owner = lax.broadcasted_iota(jnp.int32, (1, span), 1) // DECAY_CHANNELS
        for at in range(0, heads, bundle):
            feed = [b_t * weight_t[at + i : at + i + 1] for i in range(bundle)]
            feed = jnp.concatenate(feed, axis=0).astype(BF16)
            start = at * DECAY_CHANNELS
            product = jnp.dot(feed, x_ref[:, start : start + span], preferred_element_type=F32)
            state = product[:states]
            for i in range(1, bundle):
                state = jnp.where(owner == i, product[i * states : (i + 1) * states], state)
            piece, offset = divmod(start, width)
            band, offset = divmod(offset, columns)
            rows = slice(band * states, (band + 1) * states)
            held[piece, rows, offset : offset + span] = state.astype(BF16)
        totals = pack_row(climb[length - 1 :], states)
        for piece in range(group):
            at = piece * (heads // group)
            here = totals if not at else pltpu.roll(totals, every - at, 1)
            held[piece, bands * states :, :] = widen(here[:, :LANES], columns).astype(BF16)
        mine = place(group)
        for k in range(group):
            here = pl.ds(pl.multiple_of((mine ^ k) * columns, columns), columns)
            outs[k][:length] = q_ref[:, here]
            outs[k][length:] = held[mine ^ k]

    payload = shape_of((length + (bands + 1) * states, columns), BF16)
    result = launch(
        kernel,
        "block_state",
        [
            shape_of((length, every), F32),
            shape_of((heads, length), F32),
            shape_of((heads, length), F32),
            shape_of((length, LANES), F32),
        ]
        + [payload] * group,
        *parts,
        bias,
        rate,
        x,
        q,
        after=after,
        flops=32 * length * states * channels,
        scratch=[pltpu.VMEM((group, (bands + 1) * states, columns), BF16)],
    )
    return result[:4], result[4:]


def local_part(x, gate, climb, climb_t, step_t, maps, skip, states, after=()):
    length, channels = x.shape
    heads = channels // DECAY_CHANNELS

    def kernel(
        x_ref, gate_ref, climb_ref, climb_t_ref, step_t_ref, maps_ref, skip_ref, still_ref, scale_ref
    ):
        maps = maps_ref[...]
        inner = lax.dot_general(
            maps[:, states : 2 * states],
            maps[:, :states],
            (((1,), (1,)), ((), ())),
            precision=lax.Precision.HIGHEST,
            preferred_element_type=F32,
        )
        row = lax.broadcasted_iota(jnp.int32, (length, length), 0)
        column = lax.broadcasted_iota(jnp.int32, (length, length), 1)
        inner = jnp.where(column <= row, inner, 0.0)
        left = lax.broadcasted_iota(jnp.int32, (length, LANES), 1) < DECAY_CHANNELS

        for j in range(0, heads, 2):
            columns = slice(j * DECAY_CHANNELS, j * DECAY_CHANNELS + LANES)
            x = x_ref[:, columns]
            wide = [jnp.broadcast_to(climb_ref[:, i : i + 1], (length, length)) for i in (j, j + 1)]
            mixed = []
            for i in (j, j + 1):
                fall = jnp.minimum(wide[i - j] - climb_t_ref[i : i + 1], 0.0)
                mixed.append((inner * jnp.exp(fall) * step_t_ref[i : i + 1]).astype(BF16))
            zero = jnp.zeros_like(x)
            feeds = jnp.concatenate([jnp.where(left, x, zero), jnp.where(left, zero, x)], axis=0)
            local = jnp.dot(jnp.concatenate(mixed, axis=1), feeds, preferred_element_type=F32)
            gain = jnp.where(left[:1], skip_ref[:, j : j + 1], skip_ref[:, j + 1 : j + 2])
            grown = jnp.exp(jnp.where(left, wide[0], wide[1]))
            gate = gate_ref[:, columns].astype(F32)
            silu = gate / (1.0 + jnp.exp(-gate))
            still_ref[:, columns] = (local + gain * x.astype(F32)) * silu
            scale_ref[:, columns] = grown * silu

    return launch(
        kernel,
        "local_part",
        [shape_of((length, channels), F32)] * 2,
        x,
        gate,
        climb,
        climb_t,
        step_t,
        maps,
        skip,
        after=after,
        flops=4 * length * length * channels,
    )


def gather_blocks(group, states, length, refs, held):
    mine = place(group)
    for k in range(group):
        held[mine ^ k] = refs[k][length:]


def block_of(held, b, states, columns, width):
    bands = width // columns
    rows = [held[b, i * states : (i + 1) * states] for i in range(bands)]
    state = jnp.concatenate(rows, axis=1) if bands > 1 else rows[0]
    return state.astype(F32), held[b, bands * states :, :LANES]


def group_total(payloads, length, states, width, after=()):
    group = len(payloads)
    rows, columns = payloads[0].shape
    heads = width // DECAY_CHANNELS

    def kernel(*refs):
        out_ref, held = refs[group:]
        gather_blocks(group, states, length, refs[:group], held)
        state, packed = block_of(held, 0, states, columns, width)
        total = unpack_row(packed)
        for b in range(1, group):
            more, packed = block_of(held, b, states, columns, width)
            state = jnp.exp(spread_total(packed, heads)) * state + more
            total = total + unpack_row(packed)
        out_ref[:, :width] = state.astype(BF16)
        out_ref[:, width:] = pack_row(total, states).astype(BF16)

    return launch(
        kernel,
        "group_total",
        shape_of((states, width + LANES), BF16),
        *payloads,
        after=after,
        scratch=[pltpu.VMEM((group, rows - length, columns), BF16)],
    )


def entering_states(payloads, earlier, length, states, width, after=()):
    group = len(payloads)
    rows, columns = payloads[0].shape
    heads = width // DECAY_CHANNELS
    count = len(earlier)

    def kernel(*refs):
        earlier_refs = refs[group : group + count]
        outs = refs[group + count : 2 * group + count]
        held, entering = refs[2 * group + count :]
        gather_blocks(group, states, length, refs[:group], held)
        state = jnp.zeros((states, width), F32)
        for ref in reversed(earlier_refs):
            state = jnp.exp(spread_total(ref[:, width:], heads)) * state
            state = state + ref[:, :width].astype(F32)
        for b in range(group):
            entering[b] = state
            if b < group - 1:
                more, packed = block_of(held, b, states, columns, width)
                state = jnp.exp(spread_total(packed, heads)) * state + more
        mine = place(group)
        for k in range(group):
            outs[k][...] = entering[mine ^ k]

    return launch(
        kernel,
        "entering_states",
        [shape_of((states, width), F32)] * group,
        *payloads,
        *earlier,
        after=after,
        scratch=[
            pltpu.VMEM((group, rows - length, columns), BF16),
            pltpu.VMEM((group, states, width), F32),
        ],
    )


def carried_part(maps, still, scale, entering, states, after=()):
    length, channels = still.shape
    group = len(entering)
    width = channels // group
    span = min(width, 512)

    def kernel(maps_ref, still_ref, scale_ref, *refs):
        gated_ref, square_ref, held = refs[group:]
        mine = place(group)
        for k in range(group):
            held[mine ^ k] = refs[k][...]
        c = maps_ref[:, states : 2 * states]
        c_high = c.astype(BF16)
        c_low = (c - c_high.astype(F32)).astype(BF16)
        c = jnp.concatenate([c_high, c_low, c_high], axis=1)
        folded = jnp.zeros(square_ref.shape, F32)
        for at in range(0, channels, span):
            piece, offset = divmod(at, width)
            state = held[piece, :, offset : offset + span]
            high = state.astype(BF16)
            low = (state - high.astype(F32)).astype(BF16)
            carried = jnp.dot(
                c, jnp.concatenate([high, high, low], axis=0), preferred_element_type=F32
            )
            columns = slice(at, at + span)
            gated = still_ref[:, columns] + scale_ref[:, columns] * carried
            gated_ref[:, columns] = gated
            square = gated * gated
            for lane in range(0, span, LANES):
                folded = folded + square[:, lane : lane + LANES]
        square_ref[...] = folded

    return launch(
        kernel,
        "carried_part",
        [shape_of((length, channels), F32), shape_of((length, LANES), F32)],
        maps,
        still,
        scale,
        *entering,
        after=after,
        flops=6 * length * states * channels,
        scratch=[pltpu.VMEM((group, states, width), F32)],
    )


def norm(gated, gain, squares, every):
    length, channels = gated.shape
    count = len(squares)

    def kernel(gated_ref, gain_ref, *refs):
        out_ref = refs[count]
        square = refs[0][...]
        for ref in refs[1:count]:
            square = square + ref[...]
        mean = jnp.sum(square, axis=1, keepdims=True) / every
        factor = jnp.broadcast_to(lax.rsqrt(mean + 1e-05), square.shape)
        for at in range(0, channels, LANES):
            columns = slice(at, at + LANES)
            out_ref[:, columns] = (gated_ref[:, columns] * factor * gain_ref[:, columns]).astype(BF16)

    return launch(
        kernel, "norm", shape_of((length, channels), BF16), gated, gain, *squares
    )


def shared_parts(part):
    if lax.axis_size("tp") == 2:
        return [part, lax.ppermute(part, "tp", [(0, 1), (1, 0)])]
    return [lax.psum(part, "tp")]


def earlier_states(total, group, turns, count, states, width):
    if turns <= UNROLL:
        return [climb_up(total, group, count, steps) for steps in range(1, turns)]
    heads = width // DECAY_CHANNELS

    def one(_, carry):
        travelling, summed, ahead = carry
        travelling = climb_up(travelling, group, count)
        summed = summed + jnp.exp(ahead) * travelling[:, :width].astype(F32)
        more = unpack_row(travelling[:, width : width + heads])
        return travelling, summed, ahead + jnp.repeat(more, DECAY_CHANNELS, axis=1)

    start = (total, jnp.zeros((states, width), F32), jnp.zeros((1, width), F32))
    _, summed, _ = lax.fori_loop(1, turns, one, start)
    return [jnp.concatenate([summed.astype(BF16), jnp.zeros((states, LANES), BF16)], axis=1)]


def per_device(
    queries,
    keys,
    values,
    mixer_input,
    gate,
    step_weight,
    state_weight,
    step_bias,
    decay_rate,
    skip_gain,
    norm_gain,
):
    count = lax.axis_size("ctx")
    length = queries.shape[0]
    channels = mixer_input.shape[1]
    states = state_weight.shape[1] // 2
    group = math.gcd(keys.shape[1] // HD, count)
    turns = count // group
    width = channels // group

    own = jnp.stack(swap(pack_kv(keys, values, group), group, count))
    parts = shared_parts(project(mixer_input, step_weight, state_weight, after=[own]))
    (climb, climb_t, step_t, maps), payloads = block_state(
        parts, step_bias[None], decay_rate[None], mixer_input, queries, states, group
    )
    sent = payloads[0]
    payloads = swap(payloads, group, count)
    still, scale = local_part(
        mixer_input, gate, climb, climb_t, step_t, maps, skip_gain[None], states
    )
    total = group_total(payloads, length, states, width, after=[still])
    earlier = earlier_states(total, group, turns, count, states, width)
    arrived = []
    if 1 < turns <= UNROLL:
        state, waiting = (), [sent]
        travelling = climb_up(own, group, count)
        for step in range(1, turns):
            if step < turns - 1:
                travelling = tie(travelling, waiting)
                onward = climb_up(travelling, group, count)
            if step == 1:
                here = [travelling] if turns > 2 else []
                state = flash(payloads, length, own=own, chunks=here, after=[total])
            elif step < turns - 1:
                state = flash(payloads, length, state=state, chunks=[travelling], base=step)
            waiting = [state[1], total]
            arrived.append(travelling)
            travelling = onward if step < turns - 1 else travelling
    elif turns > 1:
        state = flash(payloads, length, own=own)

        def one(step, carry):
            chunk, state = carry
            chunk = climb_up(chunk, group, count)
            state = flash(payloads, length, state=state, chunks=[chunk], base=jnp.reshape(step, (1,)))
            return chunk, tuple(state)

        chunk, state = lax.fori_loop(1, turns - 1, one, (own, tuple(state)))
        arrived.append(climb_up(chunk, group, count))
    entering = swap(
        entering_states(payloads, earlier, length, states, width, after=arrived[1:2]), group, count
    )
    gated, square = carried_part(maps, still, scale, entering, states)
    mamba_out = norm(
        gated, norm_gain[None], shared_parts(square), channels * lax.axis_size("tp")
    )
    if turns == 1:
        outs = flash(payloads, length, own=own, final=True)
    else:
        outs = flash(
            payloads, length, state=state, chunks=arrived[-1:], final=True, base=turns - 1
        )
    return join(swap(outs, group, count), group), mamba_out


def solution(mesh):
    return jax.shard_map(
        per_device,
        mesh=mesh,
        in_specs=(
            P("ctx", "tp"),
            P("ctx", "tp"),
            P("ctx", "tp"),
            P("ctx", "tp"),
            P("ctx", "tp"),
            P("tp", None),
            P("tp", None),
            P("tp"),
            P("tp"),
            P("tp"),
            P("tp"),
        ),
        out_specs=(P("ctx", "tp"), P("ctx", "tp")),
        check_vma=False,
    )
```

```python
import functools
import math

import jax
import jax.numpy as jnp
from jax import lax
from jax.experimental import pallas as pl
from jax.experimental.pallas import tpu as pltpu
from jax.sharding import PartitionSpec as P

HD = 128
DECAY_CHANNELS = 64
SCAN_TOKENS = 128
LANES = 128
UNROLL = 8
VMEM_LIMIT = 14 * 1024 * 1024

F32 = jnp.float32
BF16 = jnp.bfloat16


def vmem():
    return pl.BlockSpec(memory_space=pltpu.VMEM)


def hbm():
    return pl.BlockSpec(memory_space=pltpu.HBM)


def launch(kernel, name, out_shape, *inputs, after=(), flops=0, scratch=(), in_specs=None, out_specs=None):
    count, skip = len(inputs), len(after)
    single = isinstance(out_shape, jax.ShapeDtypeStruct)
    shapes = [out_shape] if single else list(out_shape)
    size = sum(x.size * x.dtype.itemsize for x in list(inputs) + shapes)

    def body(*refs):
        kernel(*refs[:count], *refs[count + skip :])

    result = pl.pallas_call(
        body,
        out_shape=shapes,
        in_specs=(in_specs or [vmem()] * count) + [pl.BlockSpec(memory_space=pl.ANY)] * skip,
        out_specs=out_specs or [vmem()] * len(shapes),
        scratch_shapes=list(scratch),
        compiler_params=pltpu.CompilerParams(vmem_limit_bytes=VMEM_LIMIT),
        cost_estimate=pl.CostEstimate(flops=flops, bytes_accessed=size, transcendentals=0),
        name=name,
    )(*inputs, *after)
    return result[0] if single else result


def place(group):
    return lax.rem(lax.axis_index("ctx"), jnp.int32(group))


def swap(pieces, group, count):
    result = [pieces[0]]
    for k in range(1, group):
        perm = [(i, (i // group) * group + ((i % group) ^ k)) for i in range(count)]
        result.append(lax.ppermute(pieces[k], "ctx", perm))
    return result


def climb_up(array, group, count, steps=1):
    perm = [(i, i + group * steps) for i in range(count - group * steps)]
    return lax.ppermute(array, "ctx", perm)


def shape_of(shape, dtype):
    return jax.ShapeDtypeStruct(shape, dtype)


def tie(array, after):
    return pl.pallas_call(
        lambda *refs: None,
        out_shape=shape_of(array.shape, array.dtype),
        in_specs=[pl.BlockSpec(memory_space=pl.ANY)] * (1 + len(after)),
        out_specs=pl.BlockSpec(memory_space=pl.ANY),
        input_output_aliases={0: 0},
        name="tie",
    )(array, *after)


def pack_kv(keys, values, group):
    length, width = keys.shape
    width = width // group

    def kernel(k_ref, v_ref, *refs):
        outs, sems = refs[:group], refs[group]
        mine = place(group)
        copies = []
        for k in reversed(range(group)):
            columns = pl.ds(pl.multiple_of((mine ^ k) * width, width), width)
            for n, ref in enumerate((k_ref, v_ref)):
                copies.append(
                    pltpu.make_async_copy(ref.at[:, columns], outs[k].at[n], sems.at[k, n])
                )
        for copy in copies:
            copy.start()
        for copy in copies:
            copy.wait()

    return launch(
        kernel,
        "pack_kv",
        [shape_of((2, length, width), keys.dtype)] * group,
        keys,
        values,
        in_specs=[hbm()] * 2,
        scratch=[pltpu.SemaphoreType.DMA((group, 2))],
    )


def join(pieces, group):
    length, width = pieces[0].shape

    def kernel(*refs):
        out_ref, sems = refs[group:]
        mine = place(group)
        copies = []
        for k in range(group):
            columns = pl.ds(pl.multiple_of((mine ^ k) * width, width), width)
            copies.append(pltpu.make_async_copy(refs[k], out_ref.at[:, columns], sems.at[k]))
        for copy in copies:
            copy.start()
        for copy in copies:
            copy.wait()

    return launch(
        kernel,
        "join_heads",
        shape_of((length, width * group), pieces[0].dtype),
        *pieces,
        out_specs=[hbm()],
        scratch=[pltpu.SemaphoreType.DMA((group,))],
    )


def flash_chunk(q_refs, kv_ref, before, after, extended, own, length, done=None):
    group = len(q_refs)
    heads = q_refs[0].shape[1] // HD
    kv_heads = kv_ref.shape[3] // HD
    share = heads // kv_heads
    rows = group * length
    tile = min(rows, 2 * length)
    rate = math.log2(math.e) / math.sqrt(HD)
    for kv in range(kv_heads):
        lanes = slice(kv * HD, (kv + 1) * HD)
        keys = kv_ref[:, 0, :, lanes].reshape(rows, HD)
        extended[:, :HD] = kv_ref[:, 1, :, lanes].reshape(rows, HD)
        extended[:, HD:] = jnp.ones((rows, HD), BF16)

        def score(columns, start):
            parts = q_refs[start // length : (start + tile) // length]
            q = [ref[:length, columns] for ref in parts]
            q = jnp.concatenate(q, axis=0) if len(q) > 1 else q[0]
            scores = lax.dot_general(
                q, keys, (((1,), (1,)), ((), ())), preferred_element_type=F32
            )
            if own:
                flip = place(group) * length
                row = (lax.broadcasted_iota(jnp.int32, (tile, rows), 0) + start) ^ flip
                column = lax.broadcasted_iota(jnp.int32, (tile, rows), 1) ^ flip
                scores = jnp.where(column <= row, scores, -1e30)
            return scores

        def head(h, _):
            columns = pl.ds(pl.multiple_of(h * HD, HD), HD)
            starts = list(range(0, rows, tile))
            every = [score(columns, start) for start in starts]
            for start, scores in zip(starts, every):
                here = slice(start, start + tile)
                top = jnp.max(scores, axis=1, keepdims=True)
                if not own:
                    top_before = before[1][h, here]
                    top = jnp.maximum(top_before[:, :1], top)
                weights = jnp.exp2((scores - top) * rate).astype(BF16)
                value = jnp.dot(weights, extended[...], preferred_element_type=F32)
                top = jnp.broadcast_to(top, (tile, LANES))
                if not own:
                    keep = jnp.exp2((top_before - top) * rate)
                    value = value + before[0][h, here] * jnp.concatenate([keep, keep], axis=1)
                if done is not None:
                    done(columns, start, tile, value)
                if after is not None:
                    after[0][h, here] = value
                    after[1][h, here] = top
            return 0

        lax.fori_loop(kv * share, (kv + 1) * share, head, 0)


def finish_rows(out_refs, columns, start, tile, value):
    length = out_refs[0].shape[0]
    result = (value[:, :HD] / value[:, HD:]).astype(BF16)
    for at in range(0, tile, length):
        out_refs[(start + at) // length][:, columns] = result[at : at + length]


def flash(q, length, own=None, state=(), chunks=(), final=False, base=1, after=()):
    group = len(q)
    heads = q[0].shape[1] // HD
    rows = group * length
    fixed = isinstance(base, int)
    has_own = own is not None
    specs = [] if fixed else [pl.BlockSpec(memory_space=pltpu.SMEM)]
    rest = list(q) + ([own] if has_own else []) + list(state) + list(chunks)
    specs = specs + [vmem()] * len(rest)

    def kernel(*refs):
        refs = list(refs)
        first = base if fixed else refs.pop(0)[0]
        q_refs = [refs.pop(0) for _ in range(group)]
        own_ref = refs.pop(0) if has_own else None
        held = None if has_own else (refs.pop(0), refs.pop(0))
        chunk_refs = [refs.pop(0) for _ in range(len(chunks))]
        extended = refs.pop()
        turn = lax.axis_index("ctx") // group
        outs = None if final else tuple(refs)
        done = functools.partial(finish_rows, refs) if final else None
        if has_own:
            flash_chunk(q_refs, own_ref, None, outs, extended, True, length, done)
            held = outs
        for number, ref in enumerate(chunk_refs):

            @pl.when(turn >= first + number)
            def _(ref=ref, held=held):
                flash_chunk(q_refs, ref, held, outs, extended, False, length, done)

            if not has_own and number == 0:

                @pl.when(turn < first)
                def _(held=held):
                    def head(h, _):
                        if final:
                            columns = pl.ds(pl.multiple_of(h * HD, HD), HD)
                            finish_rows(refs, columns, 0, rows, held[0][h])
                        else:
                            outs[0][h] = held[0][h]
                            outs[1][h] = held[1][h]
                        return 0

                    lax.fori_loop(0, heads, head, 0)

            held = outs

    if final:
        out_shape = [shape_of((length, heads * HD), BF16)] * group
    else:
        out_shape = [
            shape_of((heads, rows, HD + LANES), F32),
            shape_of((heads, rows, LANES), F32),
        ]
    parts = len(chunks) + has_own
    return launch(
        kernel,
        "flash",
        out_shape,
        *([] if fixed else [base]),
        *rest,
        after=after,
        in_specs=specs,
        flops=4 * heads * rows * rows * HD * parts,
        scratch=[pltpu.VMEM((rows, HD + LANES), BF16)],
    )


def widen(row, lanes):
    extra = lanes - row.shape[1]
    if not extra:
        return row
    return jnp.concatenate([row, jnp.zeros((row.shape[0], extra), row.dtype)], axis=1)


def project(x, step_weight, state_weight, after=()):
    length, channels = x.shape
    heads = step_weight.shape[1]

    def kernel(x_ref, step_ref, map_ref, out_ref):
        x = x_ref[...]
        out_ref[:, :heads] = jnp.dot(x, step_ref[...], preferred_element_type=F32)
        maps = lax.dot_general(
            x, map_ref[...], (((1,), (1,)), ((), ())), preferred_element_type=F32
        )
        out_ref[:, heads:] = widen(maps, LANES)

    return launch(
        kernel,
        "project",
        shape_of((length, heads + LANES), F32),
        x,
        step_weight,
        state_weight.T,
        after=after,
        flops=4 * length * channels * heads,
    )


def owners(heads):
    shape = (LANES, heads * DECAY_CHANNELS)
    head = lax.broadcasted_iota(jnp.int32, shape, 0)
    channel = lax.broadcasted_iota(jnp.int32, shape, 1)
    return (channel // DECAY_CHANNELS == head).astype(BF16)


def pack_row(row, rows):
    high = row.astype(BF16).astype(F32)
    rest = row - high
    middle = rest.astype(BF16).astype(F32)
    low = rest - middle
    return jnp.concatenate([high, middle, low, jnp.zeros((rows - 3, row.shape[1]), F32)], axis=0)


def unpack_row(rows):
    rows = rows.astype(F32)
    return rows[0:1] + rows[1:2] + rows[2:3]


def spread_total(rows, owner):
    wide = jnp.dot(rows, owner, preferred_element_type=F32)
    return wide[0:1] + wide[1:2] + wide[2:3]


def block_state(parts, bias, rate, x, q, states, group, after=()):
    length, channels = x.shape
    every = parts[0].shape[1] - LANES
    heads = bias.shape[1]
    width = channels // group
    columns = q.shape[1] // group
    bands = width // columns
    count = len(parts)
    bundle = min(8, columns // DECAY_CHANNELS)
    span = bundle * DECAY_CHANNELS

    def kernel(*refs):
        bias_ref, rate_ref, x_ref, q_ref = refs[count : count + 4]
        climb_ref, climb_t_ref, step_t_ref, maps_ref = refs[count + 4 : count + 8]
        outs = refs[count + 8 : count + 8 + group]
        held, weight_ref = refs[count + 8 + group :]
        summed = refs[0][...]
        for ref in refs[1:count]:
            summed = summed + ref[...]
        shift = lax.rem(every - lax.axis_index("tp") * heads, jnp.int32(every))
        raw = pltpu.roll(summed[:, :every], shift, 1) + widen(bias_ref[...], every)
        step = jnp.maximum(raw, 0.0) + jnp.log1p(jnp.exp(-jnp.abs(raw)))
        log_decay = -widen(rate_ref[...], every) * step
        row = lax.broadcasted_iota(jnp.int32, (length, length), 0)
        column = lax.broadcasted_iota(jnp.int32, (length, length), 1)
        lower = (column <= row).astype(F32)
        climb = jnp.dot(
            lower, log_decay, precision=lax.Precision.HIGHEST, preferred_element_type=F32
        )
        maps = summed[:, every:]
        climb_ref[...] = climb
        maps_ref[...] = maps
        climb_t = climb.T
        step_t = step.T
        climb_t_ref[...] = climb_t[:heads]
        step_t_ref[...] = step_t[:heads]
        b_t = maps.T[:states]
        weight_t = jnp.exp(climb_t[:, length - 1 :] - climb_t) * step_t
        weight_ref[...] = weight_t[:heads]
        owner = lax.broadcasted_iota(jnp.int32, (1, span), 1) // DECAY_CHANNELS

        def some(i, _):
            weight = weight_ref[pl.ds(pl.multiple_of(i * bundle, bundle), bundle)]
            feed = [b_t * weight[n : n + 1] for n in range(bundle)]
            feed = jnp.concatenate(feed, axis=0).astype(BF16)
            start = pl.multiple_of(i * span, span)
            product = jnp.dot(feed, x_ref[:, pl.ds(start, span)], preferred_element_type=F32)
            state = product[:states]
            for n in range(1, bundle):
                state = jnp.where(owner == n, product[n * states : (n + 1) * states], state)
            piece = start // width
            band = (start - piece * width) // columns
            offset = pl.multiple_of(start - piece * width - band * columns, span)
            rows = pl.ds(pl.multiple_of(band * states, states), states)
            held[piece, rows, pl.ds(offset, span)] = state.astype(BF16)
            return 0

        lax.fori_loop(0, heads // bundle, some, 0)
        totals = pack_row(climb[length - 1 :], states)
        for piece in range(group):
            at = piece * (heads // group)
            here = totals if not at else pltpu.roll(totals, every - at, 1)
            held[piece, bands * states :, :] = widen(here[:, :LANES], columns).astype(BF16)
        mine = place(group)
        for k in range(group):
            here = pl.ds(pl.multiple_of((mine ^ k) * columns, columns), columns)
            outs[k][:length] = q_ref[:, here]
            outs[k][length:] = held[mine ^ k]

    payload = shape_of((length + (bands + 1) * states, columns), BF16)
    result = launch(
        kernel,
        "block_state",
        [
            shape_of((length, every), F32),
            shape_of((heads, length), F32),
            shape_of((heads, length), F32),
            shape_of((length, LANES), F32),
        ]
        + [payload] * group,
        *parts,
        bias,
        rate,
        x,
        q,
        after=after,
        flops=32 * length * states * channels,
        scratch=[
            pltpu.VMEM((group, (bands + 1) * states, columns), BF16),
            pltpu.VMEM((heads, length), F32),
        ],
    )
    return result[:4], result[4:]


def local_part(x, gate, climb, climb_t, step_t, maps, skip, states, after=()):
    length, channels = x.shape
    heads = channels // DECAY_CHANNELS
    pairs = 2 if heads % 4 == 0 else 1

    def kernel(
        x_ref, gate_ref, climb_ref, climb_t_ref, step_t_ref, maps_ref, skip_ref, still_ref, scale_ref
    ):
        maps = maps_ref[...]
        inner = lax.dot_general(
            maps[:, states : 2 * states],
            maps[:, :states],
            (((1,), (1,)), ((), ())),
            precision=lax.Precision.HIGHEST,
            preferred_element_type=F32,
        )
        row = lax.broadcasted_iota(jnp.int32, (length, length), 0)
        column = lax.broadcasted_iota(jnp.int32, (length, length), 1)
        inner = jnp.where(column <= row, inner, 0.0)
        left = lax.broadcasted_iota(jnp.int32, (length, LANES), 1) < DECAY_CHANNELS

        skip = jnp.broadcast_to(widen(skip_ref[...], climb_ref.shape[1]), (8, climb_ref.shape[1]))

        def some(i, carry):
            climb, skip = carry
            for pair in range(pairs):
                start = pl.multiple_of((i * pairs + pair) * LANES, LANES)
                columns = pl.ds(start, LANES)
                j = 2 * pair
                x = x_ref[:, columns]
                wide = [jnp.broadcast_to(climb[:, n : n + 1], (length, length)) for n in (j, j + 1)]
                mixed = []
                for n in range(2):
                    row = pl.ds(2 * (i * pairs + pair) + n, 1)
                    fall = jnp.minimum(wide[n] - climb_t_ref[row], 0.0)
                    mixed.append((inner * jnp.exp(fall) * step_t_ref[row]).astype(BF16))
                zero = jnp.zeros_like(x)
                feeds = [jnp.where(left, x, zero), jnp.where(left, zero, x)]
                local = jnp.dot(
                    jnp.concatenate(mixed, axis=1),
                    jnp.concatenate(feeds, axis=0),
                    preferred_element_type=F32,
                )
                gain = jnp.where(left[:1], skip[:1, j : j + 1], skip[:1, j + 1 : j + 2])
                grown = jnp.exp(jnp.where(left, wide[0], wide[1]))
                gate = gate_ref[:, columns].astype(F32)
                silu = gate / (1.0 + jnp.exp(-gate))
                still_ref[:, columns] = (local + gain * x.astype(F32)) * silu
                scale_ref[:, columns] = grown * silu
            shift = climb.shape[1] - 2 * pairs
            return pltpu.roll(climb, shift, 1), pltpu.roll(skip, shift, 1)

        lax.fori_loop(0, heads // (2 * pairs), some, (climb_ref[...], skip))

    return launch(
        kernel,
        "local_part",
        [shape_of((length, channels), F32)] * 2,
        x,
        gate,
        climb,
        climb_t,
        step_t,
        maps,
        skip,
        after=after,
        flops=4 * length * length * channels,
    )


def gather_blocks(group, states, length, refs, held):
    mine = place(group)
    for k in range(group):
        held[mine ^ k] = refs[k][length:]


def block_of(held, b, states, columns, width):
    bands = width // columns
    rows = [held[b, i * states : (i + 1) * states] for i in range(bands)]
    state = jnp.concatenate(rows, axis=1) if bands > 1 else rows[0]
    return state.astype(F32), held[b, bands * states :, :LANES]


def group_total(payloads, length, states, width, after=()):
    group = len(payloads)
    rows, columns = payloads[0].shape
    heads = width // DECAY_CHANNELS

    def kernel(*refs):
        out_ref, held = refs[group:]
        gather_blocks(group, states, length, refs[:group], held)
        owner = owners(heads)
        state, packed = block_of(held, 0, states, columns, width)
        total = unpack_row(packed)
        for b in range(1, group):
            more, packed = block_of(held, b, states, columns, width)
            state = jnp.exp(spread_total(packed, owner)) * state + more
            total = total + unpack_row(packed)
        out_ref[:, :width] = state.astype(BF16)
        out_ref[:, width:] = pack_row(total, states).astype(BF16)

    return launch(
        kernel,
        "group_total",
        shape_of((states, width + LANES), BF16),
        *payloads,
        after=after,
        scratch=[pltpu.VMEM((group, rows - length, columns), BF16)],
    )


def entering_states(payloads, earlier, length, states, width, after=()):
    group = len(payloads)
    rows, columns = payloads[0].shape
    heads = width // DECAY_CHANNELS
    count = len(earlier)

    def kernel(*refs):
        earlier_refs = refs[group : group + count]
        outs = refs[group + count : 2 * group + count]
        held, entering = refs[2 * group + count :]
        gather_blocks(group, states, length, refs[:group], held)
        owner = owners(heads)
        state = jnp.zeros((states, width), F32)
        for ref in reversed(earlier_refs):
            state = jnp.exp(spread_total(ref[:, width:], owner)) * state
            state = state + ref[:, :width].astype(F32)
        for b in range(group):
            entering[b] = state
            if b < group - 1:
                more, packed = block_of(held, b, states, columns, width)
                state = jnp.exp(spread_total(packed, owner)) * state + more
        mine = place(group)
        for k in range(group):
            outs[k][...] = entering[mine ^ k]

    return launch(
        kernel,
        "entering_states",
        [shape_of((states, width), F32)] * group,
        *payloads,
        *earlier,
        after=after,
        scratch=[
            pltpu.VMEM((group, rows - length, columns), BF16),
            pltpu.VMEM((group, states, width), F32),
        ],
    )


def carried_part(maps, still, scale, entering, states, after=()):
    length, channels = still.shape
    group = len(entering)
    width = channels // group
    span = min(width, 512)

    def kernel(maps_ref, still_ref, scale_ref, *refs):
        gated_ref, square_ref, held = refs[group:]
        mine = place(group)
        for k in range(group):
            held[mine ^ k] = refs[k][...]
        c = maps_ref[:, states : 2 * states]
        c_high = c.astype(BF16)
        c_low = (c - c_high.astype(F32)).astype(BF16)
        c = jnp.concatenate([c_high, c_low, c_high], axis=1)

        def some(i, folded):
            at = pl.multiple_of(i * span, span)
            piece = at // width
            state = held[piece, :, pl.ds(pl.multiple_of(at - piece * width, span), span)]
            high = state.astype(BF16)
            low = (state - high.astype(F32)).astype(BF16)
            carried = jnp.dot(
                c, jnp.concatenate([high, high, low], axis=0), preferred_element_type=F32
            )
            columns = pl.ds(at, span)
            gated = still_ref[:, columns] + scale_ref[:, columns] * carried
            gated_ref[:, columns] = gated
            square = gated * gated
            for lane in range(0, span, LANES):
                folded = folded + square[:, lane : lane + LANES]
            return folded

        square_ref[...] = lax.fori_loop(0, channels // span, some, jnp.zeros(square_ref.shape, F32))

    return launch(
        kernel,
        "carried_part",
        [shape_of((length, channels), F32), shape_of((length, LANES), F32)],
        maps,
        still,
        scale,
        *entering,
        after=after,
        flops=6 * length * states * channels,
        scratch=[pltpu.VMEM((group, states, width), F32)],
    )


def norm(gated, gain, squares, every):
    length, channels = gated.shape
    count = len(squares)
    span = math.gcd(channels, 4 * LANES)

    def kernel(gated_ref, gain_ref, *refs):
        out_ref = refs[count]
        square = refs[0][...]
        for ref in refs[1:count]:
            square = square + ref[...]
        mean = jnp.sum(square, axis=1, keepdims=True) / every
        factor = jnp.broadcast_to(lax.rsqrt(mean + 1e-05), square.shape)

        def some(i, _):
            for lane in range(0, span, LANES):
                columns = pl.ds(pl.multiple_of(i * span + lane, LANES), LANES)
                gain = gain_ref[:, columns]
                out_ref[:, columns] = (gated_ref[:, columns] * factor * gain).astype(BF16)
            return 0

        lax.fori_loop(0, channels // span, some, 0)

    return launch(
        kernel, "norm", shape_of((length, channels), BF16), gated, gain, *squares
    )


def shared_parts(part):
    if lax.axis_size("tp") == 2:
        return [part, lax.ppermute(part, "tp", [(0, 1), (1, 0)])]
    return [lax.psum(part, "tp")]


def earlier_states(total, group, turns, count, states, width):
    if turns <= UNROLL:
        return [climb_up(total, group, count, steps) for steps in range(1, turns)]
    heads = width // DECAY_CHANNELS

    def one(_, carry):
        travelling, summed, ahead = carry
        travelling = climb_up(travelling, group, count)
        summed = summed + jnp.exp(ahead) * travelling[:, :width].astype(F32)
        more = unpack_row(travelling[:, width : width + heads])
        return travelling, summed, ahead + jnp.repeat(more, DECAY_CHANNELS, axis=1)

    start = (total, jnp.zeros((states, width), F32), jnp.zeros((1, width), F32))
    _, summed, _ = lax.fori_loop(1, turns, one, start)
    return [jnp.concatenate([summed.astype(BF16), jnp.zeros((states, LANES), BF16)], axis=1)]


def per_device(
    queries,
    keys,
    values,
    mixer_input,
    gate,
    step_weight,
    state_weight,
    step_bias,
    decay_rate,
    skip_gain,
    norm_gain,
):
    count = lax.axis_size("ctx")
    length = queries.shape[0]
    channels = mixer_input.shape[1]
    states = state_weight.shape[1] // 2
    group = math.gcd(keys.shape[1] // HD, count)
    turns = count // group
    width = channels // group

    packed = pack_kv(keys, values, group)
    own = jnp.stack(swap(packed, group, count))
    parts = shared_parts(project(mixer_input, step_weight, state_weight, after=packed[:1]))
    (climb, climb_t, step_t, maps), payloads = block_state(
        parts, step_bias[None], decay_rate[None], mixer_input, queries, states, group, after=[own]
    )
    sent = payloads[:1]
    payloads = swap(payloads, group, count)
    still, scale = local_part(
        mixer_input, gate, climb, climb_t, step_t, maps, skip_gain[None], states
    )
    ring = 1 < turns <= UNROLL
    arrived, ready = [], []
    if ring:
        arrived.append(climb_up(own, group, count))
    if ring and turns > 2:
        arrived[0] = tie(arrived[0], sent)
        ready = [arrived[0]]
        arrived.append(climb_up(arrived[0], group, count))
    total = group_total(payloads, length, states, width, after=[still] + ready)
    earlier = earlier_states(total, group, turns, count, states, width)
    state = flash(payloads, length, own=own, after=[total])
    if ring and turns > 3:
        arrived[1] = tie(arrived[1], [state[1]] + earlier)
        ready = [arrived[1]]
        arrived.append(climb_up(arrived[1], group, count))
        for step in range(4, turns):
            arrived.append(climb_up(arrived[-1], group, count))
    entering = entering_states(payloads, earlier, length, states, width, after=ready)
    if ring and turns > 2:
        state = flash(payloads, length, state=state, chunks=arrived[:-1], after=entering[:1])
    entering = swap(entering, group, count)
    if turns > 1 and not ring:

        def one(step, carry):
            chunk, state = carry
            chunk = climb_up(chunk, group, count)
            state = flash(payloads, length, state=state, chunks=[chunk], base=jnp.reshape(step, (1,)))
            return chunk, tuple(state)

        chunk, state = lax.fori_loop(1, turns - 1, one, (own, tuple(state)))
        arrived.append(climb_up(chunk, group, count))
    gated, square = carried_part(maps, still, scale, entering, states)
    mamba_out = norm(
        gated, norm_gain[None], shared_parts(square), channels * lax.axis_size("tp")
    )
    if turns == 1:
        outs = flash(payloads, length, own=own, final=True)
    else:
        outs = flash(
            payloads, length, state=state, chunks=arrived[-1:], final=True, base=turns - 1
        )
    return join(swap(outs, group, count), group), mamba_out


def solution(mesh):
    return jax.shard_map(
        per_device,
        mesh=mesh,
        in_specs=(
            P("ctx", "tp"),
            P("ctx", "tp"),
            P("ctx", "tp"),
            P("ctx", "tp"),
            P("ctx", "tp"),
            P("tp", None),
            P("tp", None),
            P("tp"),
            P("tp"),
            P("tp"),
            P("tp"),
        ),
        out_specs=(P("ctx", "tp"), P("ctx", "tp")),
        check_vma=False,
    )
```

```python
import functools
import math

import jax
import jax.numpy as jnp
from jax import lax
from jax.experimental import pallas as pl
from jax.experimental.pallas import tpu as pltpu
from jax.sharding import PartitionSpec as P

HD = 128
DECAY_CHANNELS = 64
SCAN_TOKENS = 128
LANES = 128
UNROLL = 8
VMEM_LIMIT = 14 * 1024 * 1024

F32 = jnp.float32
BF16 = jnp.bfloat16


def vmem():
    return pl.BlockSpec(memory_space=pltpu.VMEM)


def hbm():
    return pl.BlockSpec(memory_space=pltpu.HBM)


def launch(kernel, name, out_shape, *inputs, after=(), flops=0, scratch=(), in_specs=None, out_specs=None):
    count, skip = len(inputs), len(after)
    single = isinstance(out_shape, jax.ShapeDtypeStruct)
    shapes = [out_shape] if single else list(out_shape)
    size = sum(x.size * x.dtype.itemsize for x in list(inputs) + shapes)

    def body(*refs):
        kernel(*refs[:count], *refs[count + skip :])

    result = pl.pallas_call(
        body,
        out_shape=shapes,
        in_specs=(in_specs or [vmem()] * count) + [pl.BlockSpec(memory_space=pl.ANY)] * skip,
        out_specs=out_specs or [vmem()] * len(shapes),
        scratch_shapes=list(scratch),
        compiler_params=pltpu.CompilerParams(vmem_limit_bytes=VMEM_LIMIT),
        cost_estimate=pl.CostEstimate(flops=flops, bytes_accessed=size, transcendentals=0),
        name=name,
    )(*inputs, *after)
    return result[0] if single else result


def place(group):
    return lax.rem(lax.axis_index("ctx"), jnp.int32(group))


def swap(pieces, group, count):
    result = [pieces[0]]
    for k in range(1, group):
        perm = [(i, (i // group) * group + ((i % group) ^ k)) for i in range(count)]
        result.append(lax.ppermute(pieces[k], "ctx", perm))
    return result


def climb_up(array, group, count, steps=1):
    perm = [(i, i + group * steps) for i in range(count - group * steps)]
    return lax.ppermute(array, "ctx", perm)


def shape_of(shape, dtype):
    return jax.ShapeDtypeStruct(shape, dtype)


def tie(array, after):
    return pl.pallas_call(
        lambda *refs: None,
        out_shape=shape_of(array.shape, array.dtype),
        in_specs=[pl.BlockSpec(memory_space=pl.ANY)] * (1 + len(after)),
        out_specs=pl.BlockSpec(memory_space=pl.ANY),
        input_output_aliases={0: 0},
        compiler_params=pltpu.CompilerParams(vmem_limit_bytes=1024 * 1024),
        name="tie",
    )(array, *after)


def pack_kv(keys, values, group):
    length, width = keys.shape
    width = width // group

    def kernel(k_ref, v_ref, *refs):
        outs, sems = refs[:group], refs[group]
        mine = place(group)
        copies = []
        for k in reversed(range(group)):
            columns = pl.ds(pl.multiple_of((mine ^ k) * width, width), width)
            for n, ref in enumerate((k_ref, v_ref)):
                copies.append(
                    pltpu.make_async_copy(ref.at[:, columns], outs[k].at[n], sems.at[k, n])
                )
        for copy in copies:
            copy.start()
        for copy in copies:
            copy.wait()

    return launch(
        kernel,
        "pack_kv",
        [shape_of((2, length, width), keys.dtype)] * group,
        keys,
        values,
        in_specs=[hbm()] * 2,
        scratch=[pltpu.SemaphoreType.DMA((group, 2))],
    )


def join(pieces, group):
    length, width = pieces[0].shape

    def kernel(*refs):
        out_ref, sems = refs[group:]
        mine = place(group)
        copies = []
        for k in range(group):
            columns = pl.ds(pl.multiple_of((mine ^ k) * width, width), width)
            copies.append(pltpu.make_async_copy(refs[k], out_ref.at[:, columns], sems.at[k]))
        for copy in copies:
            copy.start()
        for copy in copies:
            copy.wait()

    return launch(
        kernel,
        "join_heads",
        shape_of((length, width * group), pieces[0].dtype),
        *pieces,
        out_specs=[hbm()],
        scratch=[pltpu.SemaphoreType.DMA((group,))],
    )


def flash_chunk(q_refs, kv_ref, before, after, extended, own, length):
    group = len(q_refs)
    heads = q_refs[0].shape[1] // HD
    kv_heads = kv_ref.shape[3] // HD
    share = heads // kv_heads
    rows = group * length
    tile = min(rows, 2 * length)
    rate = math.log2(math.e) / math.sqrt(HD)
    for kv in range(kv_heads):
        lanes = slice(kv * HD, (kv + 1) * HD)
        keys = kv_ref[:, 0, :, lanes].reshape(rows, HD)
        extended[:, :HD] = kv_ref[:, 1, :, lanes].reshape(rows, HD)
        extended[:, HD:] = jnp.ones((rows, HD), BF16)
        tiles = [
            (h, start)
            for start in range(0, rows, tile)
            for h in range(kv * share, (kv + 1) * share)
        ]

        def score(h, start):
            parts = q_refs[start // length : (start + tile) // length]
            q = [ref[:length, h * HD : (h + 1) * HD] for ref in parts]
            q = jnp.concatenate(q, axis=0) if len(q) > 1 else q[0]
            scores = lax.dot_general(
                q, keys, (((1,), (1,)), ((), ())), preferred_element_type=F32
            )
            if own:
                flip = place(group) * length
                row = (lax.broadcasted_iota(jnp.int32, (tile, rows), 0) + start) ^ flip
                column = lax.broadcasted_iota(jnp.int32, (tile, rows), 1) ^ flip
                scores = jnp.where(column <= row, scores, -1e30)
            return scores

        ahead = score(*tiles[0])
        for n, (h, start) in enumerate(tiles):
            scores = ahead
            if n + 1 < len(tiles):
                ahead = score(*tiles[n + 1])
            here = slice(start, start + tile)
            top = jnp.max(scores, axis=1, keepdims=True)
            if not own:
                top_before = before[1][h, here]
                top = jnp.maximum(top_before[:, :1], top)
            weights = jnp.exp2((scores - top) * rate).astype(BF16)
            value = jnp.dot(weights, extended[...], preferred_element_type=F32)
            top = jnp.broadcast_to(top, (tile, LANES))
            if not own:
                keep = jnp.exp2((top_before - top) * rate)
                value = value + before[0][h, here] * jnp.concatenate([keep, keep], axis=1)
            yield h, start, tile, value
            if after is not None:
                after[0][h, here] = value
                after[1][h, here] = top


def finish_rows(out_refs, h, start, tile, value):
    length = out_refs[0].shape[0]
    result = (value[:, :HD] / value[:, HD:]).astype(BF16)
    for at in range(0, tile, length):
        out_refs[(start + at) // length][:, h * HD : (h + 1) * HD] = result[at : at + length]


def flash(q, length, own=None, state=(), chunks=(), final=False, base=1, after=()):
    group = len(q)
    heads = q[0].shape[1] // HD
    rows = group * length
    fixed = isinstance(base, int)
    has_own = own is not None
    specs = [] if fixed else [pl.BlockSpec(memory_space=pltpu.SMEM)]
    rest = list(q) + ([own] if has_own else []) + list(state) + list(chunks)
    specs = specs + [vmem()] * len(rest)

    def kernel(*refs):
        refs = list(refs)
        first = base if fixed else refs.pop(0)[0]
        q_refs = [refs.pop(0) for _ in range(group)]
        own_ref = refs.pop(0) if has_own else None
        held = None if has_own else (refs.pop(0), refs.pop(0))
        chunk_refs = [refs.pop(0) for _ in range(len(chunks))]
        extended = refs.pop()
        turn = lax.axis_index("ctx") // group
        outs = None if final else tuple(refs)
        if has_own:
            for done in flash_chunk(q_refs, own_ref, None, outs, extended, True, length):
                if final:
                    finish_rows(refs, *done)
            held = outs
        for number, ref in enumerate(chunk_refs):

            @pl.when(turn >= first + number)
            def _(ref=ref, held=held):
                for done in flash_chunk(q_refs, ref, held, outs, extended, False, length):
                    if final:
                        finish_rows(refs, *done)

            if not has_own and number == 0:

                @pl.when(turn < first)
                def _(held=held):
                    for h in range(heads):
                        if final:
                            finish_rows(refs, h, 0, rows, held[0][h])
                        else:
                            outs[0][h] = held[0][h]
                            outs[1][h] = held[1][h]

            held = outs

    if final:
        out_shape = [shape_of((length, heads * HD), BF16)] * group
    else:
        out_shape = [
            shape_of((heads, rows, HD + LANES), F32),
            shape_of((heads, rows, LANES), F32),
        ]
    parts = len(chunks) + has_own
    return launch(
        kernel,
        "flash",
        out_shape,
        *([] if fixed else [base]),
        *rest,
        after=after,
        in_specs=specs,
        flops=4 * heads * rows * rows * HD * parts,
        scratch=[pltpu.VMEM((rows, HD + LANES), BF16)],
    )


def widen(row, lanes):
    extra = lanes - row.shape[1]
    if not extra:
        return row
    return jnp.concatenate([row, jnp.zeros((row.shape[0], extra), row.dtype)], axis=1)


def project(x, step_weight, state_weight, after=()):
    length, channels = x.shape
    heads = step_weight.shape[1]

    def kernel(x_ref, step_ref, map_ref, out_ref):
        x = x_ref[...]
        out_ref[:, :heads] = jnp.dot(x, step_ref[...], preferred_element_type=F32)
        maps = lax.dot_general(
            x, map_ref[...], (((1,), (1,)), ((), ())), preferred_element_type=F32
        )
        out_ref[:, heads:] = widen(maps, LANES)

    return launch(
        kernel,
        "project",
        shape_of((length, heads + LANES), F32),
        x,
        step_weight,
        state_weight.T,
        after=after,
        flops=4 * length * channels * heads,
    )


def owners(heads):
    shape = (LANES, heads * DECAY_CHANNELS)
    head = lax.broadcasted_iota(jnp.int32, shape, 0)
    channel = lax.broadcasted_iota(jnp.int32, shape, 1)
    return (channel // DECAY_CHANNELS == head).astype(BF16)


def pack_row(row, rows):
    high = row.astype(BF16).astype(F32)
    rest = row - high
    middle = rest.astype(BF16).astype(F32)
    low = rest - middle
    return jnp.concatenate([high, middle, low, jnp.zeros((rows - 3, row.shape[1]), F32)], axis=0)


def unpack_row(rows):
    rows = rows.astype(F32)
    return rows[0:1] + rows[1:2] + rows[2:3]


def spread_total(rows, owner):
    wide = jnp.dot(rows, owner, preferred_element_type=F32)
    return wide[0:1] + wide[1:2] + wide[2:3]


def block_state(parts, bias, rate, x, q, states, group, after=()):
    length, channels = x.shape
    every = parts[0].shape[1] - LANES
    heads = bias.shape[1]
    width = channels // group
    columns = q.shape[1] // group
    bands = width // columns
    count = len(parts)

    def kernel(*refs):
        bias_ref, rate_ref, x_ref, q_ref = refs[count : count + 4]
        climb_ref, climb_t_ref, step_t_ref, maps_ref = refs[count + 4 : count + 8]
        outs = refs[count + 8 : count + 8 + group]
        held = refs[count + 8 + group]
        summed = refs[0][...]
        for ref in refs[1:count]:
            summed = summed + ref[...]
        shift = lax.rem(every - lax.axis_index("tp") * heads, jnp.int32(every))
        raw = pltpu.roll(summed[:, :every], shift, 1) + widen(bias_ref[...], every)
        step = jnp.maximum(raw, 0.0) + jnp.log1p(jnp.exp(-jnp.abs(raw)))
        log_decay = -widen(rate_ref[...], every) * step
        row = lax.broadcasted_iota(jnp.int32, (length, length), 0)
        column = lax.broadcasted_iota(jnp.int32, (length, length), 1)
        lower = (column <= row).astype(F32)
        climb = jnp.dot(
            lower, log_decay, precision=lax.Precision.HIGHEST, preferred_element_type=F32
        )
        maps = summed[:, every:]
        climb_ref[...] = climb
        maps_ref[...] = maps
        climb_t = climb.T
        step_t = step.T
        climb_t_ref[...] = climb_t[:heads]
        step_t_ref[...] = step_t[:heads]
        b_t = maps.T[:states]
        weight_t = jnp.exp(climb_t[:, length - 1 :] - climb_t) * step_t
        bundle = 4
        span = bundle * DECAY_CHANNELS
        owner = lax.broadcasted_iota(jnp.int32, (1, span), 1) // DECAY_CHANNELS
        for at in range(0, heads, bundle):
            feed = [b_t * weight_t[at + i : at + i + 1] for i in range(bundle)]
            feed = jnp.concatenate(feed, axis=0).astype(BF16)
            start = at * DECAY_CHANNELS
            product = jnp.dot(feed, x_ref[:, start : start + span], preferred_element_type=F32)
            state = product[:states]
            for i in range(1, bundle):
                state = jnp.where(owner == i, product[i * states : (i + 1) * states], state)
            piece, offset = divmod(start, width)
            band, offset = divmod(offset, columns)
            rows = slice(band * states, (band + 1) * states)
            held[piece, rows, offset : offset + span] = state.astype(BF16)
        totals = pack_row(climb[length - 1 :], states)
        for piece in range(group):
            at = piece * (heads // group)
            here = totals if not at else pltpu.roll(totals, every - at, 1)
            held[piece, bands * states :, :] = widen(here[:, :LANES], columns).astype(BF16)
        mine = place(group)
        for k in range(group):
            here = pl.ds(pl.multiple_of((mine ^ k) * columns, columns), columns)
            outs[k][:length] = q_ref[:, here]
            outs[k][length:] = held[mine ^ k]

    payload = shape_of((length + (bands + 1) * states, columns), BF16)
    result = launch(
        kernel,
        "block_state",
        [
            shape_of((length, every), F32),
            shape_of((heads, length), F32),
            shape_of((heads, length), F32),
            shape_of((length, LANES), F32),
        ]
        + [payload] * group,
        *parts,
        bias,
        rate,
        x,
        q,
        after=after,
        flops=32 * length * states * channels,
        scratch=[pltpu.VMEM((group, (bands + 1) * states, columns), BF16)],
    )
    return result[:4], result[4:]


def local_part(x, gate, climb, climb_t, step_t, maps, skip, states, after=()):
    length, channels = x.shape
    heads = channels // DECAY_CHANNELS

    def kernel(
        x_ref, gate_ref, climb_ref, climb_t_ref, step_t_ref, maps_ref, skip_ref, still_ref, scale_ref
    ):
        maps = maps_ref[...]
        inner = lax.dot_general(
            maps[:, states : 2 * states],
            maps[:, :states],
            (((1,), (1,)), ((), ())),
            precision=lax.Precision.HIGHEST,
            preferred_element_type=F32,
        )
        row = lax.broadcasted_iota(jnp.int32, (length, length), 0)
        column = lax.broadcasted_iota(jnp.int32, (length, length), 1)
        inner = jnp.where(column <= row, inner, 0.0)
        left = lax.broadcasted_iota(jnp.int32, (length, LANES), 1) < DECAY_CHANNELS

        for j in range(0, heads, 2):
            columns = slice(j * DECAY_CHANNELS, j * DECAY_CHANNELS + LANES)
            x = x_ref[:, columns]
            wide = [jnp.broadcast_to(climb_ref[:, i : i + 1], (length, length)) for i in (j, j + 1)]
            mixed = []
            for i in (j, j + 1):
                fall = jnp.minimum(wide[i - j] - climb_t_ref[i : i + 1], 0.0)
                mixed.append((inner * jnp.exp(fall) * step_t_ref[i : i + 1]).astype(BF16))
            zero = jnp.zeros_like(x)
            feeds = jnp.concatenate([jnp.where(left, x, zero), jnp.where(left, zero, x)], axis=0)
            local = jnp.dot(jnp.concatenate(mixed, axis=1), feeds, preferred_element_type=F32)
            gain = jnp.where(left[:1], skip_ref[:, j : j + 1], skip_ref[:, j + 1 : j + 2])
            grown = jnp.exp(jnp.where(left, wide[0], wide[1]))
            gate = gate_ref[:, columns].astype(F32)
            silu = gate / (1.0 + jnp.exp(-gate))
            still_ref[:, columns] = (local + gain * x.astype(F32)) * silu
            scale_ref[:, columns] = grown * silu

    return launch(
        kernel,
        "local_part",
        [shape_of((length, channels), F32)] * 2,
        x,
        gate,
        climb,
        climb_t,
        step_t,
        maps,
        skip,
        after=after,
        flops=4 * length * length * channels,
    )


def gather_blocks(group, states, length, refs, held):
    mine = place(group)
    for k in range(group):
        held[mine ^ k] = refs[k][length:]


def block_of(held, b, states, columns, width):
    bands = width // columns
    rows = [held[b, i * states : (i + 1) * states] for i in range(bands)]
    state = jnp.concatenate(rows, axis=1) if bands > 1 else rows[0]
    return state.astype(F32), held[b, bands * states :, :LANES]


def group_total(payloads, length, states, width, after=()):
    group = len(payloads)
    rows, columns = payloads[0].shape
    heads = width // DECAY_CHANNELS

    def kernel(*refs):
        out_ref, held = refs[group:]
        gather_blocks(group, states, length, refs[:group], held)
        owner = owners(heads)
        state, packed = block_of(held, 0, states, columns, width)
        total = unpack_row(packed)
        for b in range(1, group):
            more, packed = block_of(held, b, states, columns, width)
            state = jnp.exp(spread_total(packed, owner)) * state + more
            total = total + unpack_row(packed)
        out_ref[:, :width] = state.astype(BF16)
        out_ref[:, width:] = pack_row(total, states).astype(BF16)

    return launch(
        kernel,
        "group_total",
        shape_of((states, width + LANES), BF16),
        *payloads,
        after=after,
        scratch=[pltpu.VMEM((group, rows - length, columns), BF16)],
    )


def entering_states(payloads, earlier, length, states, width, after=()):
    group = len(payloads)
    rows, columns = payloads[0].shape
    heads = width // DECAY_CHANNELS
    count = len(earlier)

    def kernel(*refs):
        earlier_refs = refs[group : group + count]
        outs = refs[group + count : 2 * group + count]
        held, entering = refs[2 * group + count :]
        gather_blocks(group, states, length, refs[:group], held)
        owner = owners(heads)
        state = jnp.zeros((states, width), F32)
        for ref in reversed(earlier_refs):
            state = jnp.exp(spread_total(ref[:, width:], owner)) * state
            state = state + ref[:, :width].astype(F32)
        for b in range(group):
            entering[b] = state
            if b < group - 1:
                more, packed = block_of(held, b, states, columns, width)
                state = jnp.exp(spread_total(packed, owner)) * state + more
        mine = place(group)
        for k in range(group):
            outs[k][...] = entering[mine ^ k]

    return launch(
        kernel,
        "entering_states",
        [shape_of((states, width), F32)] * group,
        *payloads,
        *earlier,
        after=after,
        scratch=[
            pltpu.VMEM((group, rows - length, columns), BF16),
            pltpu.VMEM((group, states, width), F32),
        ],
    )


def carried_part(maps, still, scale, entering, states, after=()):
    length, channels = still.shape
    group = len(entering)
    width = channels // group
    span = min(width, 512)

    def kernel(maps_ref, still_ref, scale_ref, *refs):
        gated_ref, square_ref, held = refs[group:]
        mine = place(group)
        for k in range(group):
            held[mine ^ k] = refs[k][...]
        c = maps_ref[:, states : 2 * states]
        c_high = c.astype(BF16)
        c_low = (c - c_high.astype(F32)).astype(BF16)
        c = jnp.concatenate([c_high, c_low, c_high], axis=1)
        folded = jnp.zeros(square_ref.shape, F32)
        for at in range(0, channels, span):
            piece, offset = divmod(at, width)
            state = held[piece, :, offset : offset + span]
            high = state.astype(BF16)
            low = (state - high.astype(F32)).astype(BF16)
            carried = jnp.dot(
                c, jnp.concatenate([high, high, low], axis=0), preferred_element_type=F32
            )
            columns = slice(at, at + span)
            gated = still_ref[:, columns] + scale_ref[:, columns] * carried
            gated_ref[:, columns] = gated
            square = gated * gated
            for lane in range(0, span, LANES):
                folded = folded + square[:, lane : lane + LANES]
        square_ref[...] = folded

    return launch(
        kernel,
        "carried_part",
        [shape_of((length, channels), F32), shape_of((length, LANES), F32)],
        maps,
        still,
        scale,
        *entering,
        after=after,
        flops=6 * length * states * channels,
        scratch=[pltpu.VMEM((group, states, width), F32)],
    )


def norm(gated, gain, squares, every):
    length, channels = gated.shape
    count = len(squares)

    def kernel(gated_ref, gain_ref, *refs):
        out_ref = refs[count]
        square = refs[0][...]
        for ref in refs[1:count]:
            square = square + ref[...]
        mean = jnp.sum(square, axis=1, keepdims=True) / every
        factor = jnp.broadcast_to(lax.rsqrt(mean + 1e-05), square.shape)
        for at in range(0, channels, LANES):
            columns = slice(at, at + LANES)
            out_ref[:, columns] = (gated_ref[:, columns] * factor * gain_ref[:, columns]).astype(BF16)

    return launch(
        kernel, "norm", shape_of((length, channels), BF16), gated, gain, *squares
    )


def shared_parts(part):
    if lax.axis_size("tp") == 2:
        return [part, lax.ppermute(part, "tp", [(0, 1), (1, 0)])]
    return [lax.psum(part, "tp")]


def earlier_states(total, group, turns, count, states, width):
    if turns <= UNROLL:
        return [climb_up(total, group, count, steps) for steps in range(1, turns)]
    heads = width // DECAY_CHANNELS

    def one(_, carry):
        travelling, summed, ahead = carry
        travelling = climb_up(travelling, group, count)
        summed = summed + jnp.exp(ahead) * travelling[:, :width].astype(F32)
        more = unpack_row(travelling[:, width : width + heads])
        return travelling, summed, ahead + jnp.repeat(more, DECAY_CHANNELS, axis=1)

    start = (total, jnp.zeros((states, width), F32), jnp.zeros((1, width), F32))
    _, summed, _ = lax.fori_loop(1, turns, one, start)
    return [jnp.concatenate([summed.astype(BF16), jnp.zeros((states, LANES), BF16)], axis=1)]


def per_device(
    queries,
    keys,
    values,
    mixer_input,
    gate,
    step_weight,
    state_weight,
    step_bias,
    decay_rate,
    skip_gain,
    norm_gain,
):
    count = lax.axis_size("ctx")
    length = queries.shape[0]
    channels = mixer_input.shape[1]
    states = state_weight.shape[1] // 2
    group = math.gcd(keys.shape[1] // HD, count)
    turns = count // group
    width = channels // group

    packed = pack_kv(keys, values, group)
    own = jnp.stack(swap(packed, group, count))
    parts = shared_parts(project(mixer_input, step_weight, state_weight, after=packed[:1]))
    (climb, climb_t, step_t, maps), payloads = block_state(
        parts, step_bias[None], decay_rate[None], mixer_input, queries, states, group, after=[own]
    )
    sent = payloads[:1]
    payloads = swap(payloads, group, count)
    still, scale = local_part(
        mixer_input, gate, climb, climb_t, step_t, maps, skip_gain[None], states
    )
    ring = 1 < turns <= UNROLL
    arrived, ready = [], []
    if ring:
        arrived.append(climb_up(own, group, count))
    if ring and turns > 2:
        arrived[0] = tie(arrived[0], sent)
        ready = [arrived[0]]
        arrived.append(climb_up(arrived[0], group, count))
    total = group_total(payloads, length, states, width, after=[still] + ready)
    earlier = earlier_states(total, group, turns, count, states, width)
    state = flash(payloads, length, own=own, after=[total])
    if ring and turns > 3:
        arrived[1] = tie(arrived[1], [state[1]] + earlier)
        ready = [arrived[1]]
        arrived.append(climb_up(arrived[1], group, count))
        for step in range(4, turns):
            arrived.append(climb_up(arrived[-1], group, count))
    entering = entering_states(payloads, earlier, length, states, width, after=ready)
    if ring and turns > 2:
        state = flash(payloads, length, state=state, chunks=arrived[:-1], after=entering[:1])
    entering = swap(entering, group, count)
    if turns > 1 and not ring:

        def one(step, carry):
            chunk, state = carry
            chunk = climb_up(chunk, group, count)
            state = flash(payloads, length, state=state, chunks=[chunk], base=jnp.reshape(step, (1,)))
            return chunk, tuple(state)

        chunk, state = lax.fori_loop(1, turns - 1, one, (own, tuple(state)))
        arrived.append(climb_up(chunk, group, count))
    gated, square = carried_part(maps, still, scale, entering, states)
    mamba_out = norm(
        gated, norm_gain[None], shared_parts(square), channels * lax.axis_size("tp")
    )
    if turns == 1:
        outs = flash(payloads, length, own=own, final=True)
    else:
        outs = flash(
            payloads, length, state=state, chunks=arrived[-1:], final=True, base=turns - 1
        )
    return join(swap(outs, group, count), group), mamba_out


def solution(mesh):
    return jax.shard_map(
        per_device,
        mesh=mesh,
        in_specs=(
            P("ctx", "tp"),
            P("ctx", "tp"),
            P("ctx", "tp"),
            P("ctx", "tp"),
            P("ctx", "tp"),
            P("tp", None),
            P("tp", None),
            P("tp"),
            P("tp"),
            P("tp"),
            P("tp"),
        ),
        out_specs=(P("ctx", "tp"), P("ctx", "tp")),
        check_vma=False,
    )
```

```python
import functools
import math

import jax
import jax.numpy as jnp
from jax import lax
from jax.experimental import pallas as pl
from jax.experimental.pallas import tpu as pltpu
from jax.sharding import PartitionSpec as P

HD = 128
DECAY_CHANNELS = 64
SCAN_TOKENS = 128
LANES = 128
UNROLL = 8
VMEM_LIMIT = 14 * 1024 * 1024

F32 = jnp.float32
BF16 = jnp.bfloat16


def vmem():
    return pl.BlockSpec(memory_space=pltpu.VMEM)


def hbm():
    return pl.BlockSpec(memory_space=pltpu.HBM)


def launch(kernel, name, out_shape, *inputs, after=(), flops=0, scratch=(), in_specs=None, out_specs=None, grid=None):
    count, skip = len(inputs), len(after)
    single = isinstance(out_shape, jax.ShapeDtypeStruct)
    shapes = [out_shape] if single else list(out_shape)
    size = sum(x.size * x.dtype.itemsize for x in list(inputs) + shapes)

    def body(*refs):
        kernel(*refs[:count], *refs[count + skip :])

    result = pl.pallas_call(
        body,
        **({} if grid is None else {"grid": grid}),
        out_shape=shapes,
        in_specs=(in_specs or [vmem()] * count) + [pl.BlockSpec(memory_space=pl.ANY)] * skip,
        out_specs=out_specs or [vmem()] * len(shapes),
        scratch_shapes=list(scratch),
        compiler_params=pltpu.CompilerParams(vmem_limit_bytes=VMEM_LIMIT),
        cost_estimate=pl.CostEstimate(flops=flops, bytes_accessed=size, transcendentals=0),
        name=name,
    )(*inputs, *after)
    return result[0] if single else result


def place(group):
    return lax.rem(lax.axis_index("ctx"), jnp.int32(group))


def swap(pieces, group, count):
    result = [pieces[0]]
    for k in range(1, group):
        perm = [(i, (i // group) * group + ((i % group) ^ k)) for i in range(count)]
        result.append(lax.ppermute(pieces[k], "ctx", perm))
    return result


def climb_up(array, group, count, steps=1):
    perm = [(i, i + group * steps) for i in range(count - group * steps)]
    return lax.ppermute(array, "ctx", perm)


def shape_of(shape, dtype):
    return jax.ShapeDtypeStruct(shape, dtype)


def tie(array, after):
    return pl.pallas_call(
        lambda *refs: None,
        out_shape=shape_of(array.shape, array.dtype),
        in_specs=[pl.BlockSpec(memory_space=pl.ANY)] * (1 + len(after)),
        out_specs=pl.BlockSpec(memory_space=pl.ANY),
        input_output_aliases={0: 0},
        compiler_params=pltpu.CompilerParams(vmem_limit_bytes=1024 * 1024),
        name="tie",
    )(array, *after)


def pack_kv(keys, values, group):
    length, width = keys.shape
    piece = width // group

    def kernel(k_ref, v_ref, *outs):
        mine = place(group)
        for k in range(group):
            columns = pl.ds(pl.multiple_of((mine ^ k) * piece, piece), piece)
            outs[k][0] = k_ref[:, columns]
            outs[k][1] = v_ref[:, columns]

    return launch(
        kernel,
        "pack_kv",
        [shape_of((2, length, piece), keys.dtype)] * group,
        keys,
        values,
        grid=(1,),
        in_specs=[pl.BlockSpec((length, width), lambda i: (0, 0))] * 2,
    )


def join(pieces, group):
    length, width = pieces[0].shape

    def kernel(*refs):
        out_ref, sems = refs[group:]
        mine = place(group)
        copies = []
        for k in range(group):
            columns = pl.ds(pl.multiple_of((mine ^ k) * width, width), width)
            copies.append(pltpu.make_async_copy(refs[k], out_ref.at[:, columns], sems.at[k]))
        for copy in copies:
            copy.start()
        for copy in copies:
            copy.wait()

    return launch(
        kernel,
        "join_heads",
        shape_of((length, width * group), pieces[0].dtype),
        *pieces,
        out_specs=[hbm()],
        scratch=[pltpu.SemaphoreType.DMA((group,))],
    )


def flash_chunk(q_refs, kv_refs, before, after, extended, own, length):
    group = len(q_refs)
    heads = q_refs[0].shape[1] // HD
    kv_heads = kv_refs[0].shape[3] // HD
    share = heads // kv_heads
    rows = group * length
    tile = min(rows, 2 * length)
    rate = math.log2(math.e) / math.sqrt(HD)
    for kv in range(kv_heads):
        lanes = slice(kv * HD, (kv + 1) * HD)
        keys, at = [], 0
        for ref in kv_refs:
            more = ref.shape[0] * length
            keys.append(ref[:, 0, :, lanes].reshape(more, HD))
            extended[at : at + more, :HD] = ref[:, 1, :, lanes].reshape(more, HD)
            at += more
        keys = jnp.concatenate(keys, axis=0) if len(keys) > 1 else keys[0]
        extended[:, HD:] = jnp.ones((rows, HD), BF16)
        tiles = [
            (h, start)
            for start in range(0, rows, tile)
            for h in range(kv * share, (kv + 1) * share)
        ]

        def score(h, start):
            parts = q_refs[start // length : (start + tile) // length]
            q = [ref[:length, h * HD : (h + 1) * HD] for ref in parts]
            q = jnp.concatenate(q, axis=0) if len(q) > 1 else q[0]
            scores = lax.dot_general(
                q, keys, (((1,), (1,)), ((), ())), preferred_element_type=F32
            )
            if own:
                flip = place(group) * length
                row = (lax.broadcasted_iota(jnp.int32, (tile, rows), 0) + start) ^ flip
                column = lax.broadcasted_iota(jnp.int32, (tile, rows), 1) ^ flip
                scores = jnp.where(column <= row, scores, -1e30)
            return scores

        ahead = score(*tiles[0])
        for n, (h, start) in enumerate(tiles):
            scores = ahead
            if n + 1 < len(tiles):
                ahead = score(*tiles[n + 1])
            here = slice(start, start + tile)
            top = jnp.max(scores, axis=1, keepdims=True)
            if not own:
                top_before = before[1][h, here]
                top = jnp.maximum(top_before[:, :1], top)
            weights = jnp.exp2((scores - top) * rate).astype(BF16)
            value = jnp.dot(weights, extended[...], preferred_element_type=F32)
            top = jnp.broadcast_to(top, (tile, LANES))
            if not own:
                keep = jnp.exp2((top_before - top) * rate)
                value = value + before[0][h, here] * jnp.concatenate([keep, keep], axis=1)
            yield h, start, tile, value
            if after is not None:
                after[0][h, here] = value
                after[1][h, here] = top


def finish_rows(out_refs, h, start, tile, value):
    length = out_refs[0].shape[0]
    result = (value[:, :HD] / value[:, HD:]).astype(BF16)
    for at in range(0, tile, length):
        out_refs[(start + at) // length][:, h * HD : (h + 1) * HD] = result[at : at + length]


def flash(q, length, own=None, state=(), chunks=(), final=False, base=1, after=()):
    group = len(q)
    heads = q[0].shape[1] // HD
    rows = group * length
    fixed = isinstance(base, int)
    has_own = own is not None
    specs = [] if fixed else [pl.BlockSpec(memory_space=pltpu.SMEM)]
    rest = list(q) + list(own or ()) + list(state) + [half for chunk in chunks for half in chunk]
    specs = specs + [vmem()] * len(rest)

    def kernel(*refs):
        refs = list(refs)
        first = base if fixed else refs.pop(0)[0]
        q_refs = [refs.pop(0) for _ in range(group)]
        own_refs = [refs.pop(0) for _ in own or ()]
        held = None if has_own else (refs.pop(0), refs.pop(0))
        chunk_refs = [[refs.pop(0) for _ in chunk] for chunk in chunks]
        extended = refs.pop()
        turn = lax.axis_index("ctx") // group
        outs = None if final else tuple(refs)
        if has_own:
            for done in flash_chunk(q_refs, own_refs, None, outs, extended, True, length):
                if final:
                    finish_rows(refs, *done)
            held = outs
        for number, ref in enumerate(chunk_refs):

            @pl.when(turn >= first + number)
            def _(ref=ref, held=held):
                for done in flash_chunk(q_refs, ref, held, outs, extended, False, length):
                    if final:
                        finish_rows(refs, *done)

            if not has_own and number == 0:

                @pl.when(turn < first)
                def _(held=held):
                    for h in range(heads):
                        if final:
                            finish_rows(refs, h, 0, rows, held[0][h])
                        else:
                            outs[0][h] = held[0][h]
                            outs[1][h] = held[1][h]

            held = outs

    if final:
        out_shape = [shape_of((length, heads * HD), BF16)] * group
    else:
        out_shape = [
            shape_of((heads, rows, HD + LANES), F32),
            shape_of((heads, rows, LANES), F32),
        ]
    parts = len(chunks) + has_own
    return launch(
        kernel,
        "flash",
        out_shape,
        *([] if fixed else [base]),
        *rest,
        after=after,
        in_specs=specs,
        flops=4 * heads * rows * rows * HD * parts,
        scratch=[pltpu.VMEM((rows, HD + LANES), BF16)],
    )


def widen(row, lanes):
    extra = lanes - row.shape[1]
    if not extra:
        return row
    return jnp.concatenate([row, jnp.zeros((row.shape[0], extra), row.dtype)], axis=1)


def project(x, step_weight, state_weight, after=()):
    length, channels = x.shape
    heads = step_weight.shape[1]
    width = state_weight.shape[1]
    depth = math.gcd(channels, 1024)

    def kernel(x_ref, step_ref, map_ref, out_ref):
        x = x_ref[...]
        step = jnp.dot(x, step_ref[...], preferred_element_type=F32)
        maps = lax.dot_general(
            x, map_ref[...], (((1,), (1,)), ((), ())), preferred_element_type=F32
        )
        maps = widen(maps, LANES)
        first = pl.program_id(0) == 0

        @pl.when(first)
        def _():
            out_ref[:, :heads] = step
            out_ref[:, heads:] = maps

        @pl.when(jnp.logical_not(first))
        def _():
            out_ref[:, :heads] += step
            out_ref[:, heads:] += maps

    return launch(
        kernel,
        "project",
        shape_of((length, heads + LANES), F32),
        x,
        step_weight,
        state_weight.T,
        after=after,
        flops=4 * length * channels * heads,
        grid=(channels // depth,),
        in_specs=[
            pl.BlockSpec((length, depth), lambda i: (0, i)),
            pl.BlockSpec((depth, heads), lambda i: (i, 0)),
            pl.BlockSpec((width, depth), lambda i: (0, i)),
        ],
    )


def owners(heads):
    shape = (LANES, heads * DECAY_CHANNELS)
    head = lax.broadcasted_iota(jnp.int32, shape, 0)
    channel = lax.broadcasted_iota(jnp.int32, shape, 1)
    return (channel // DECAY_CHANNELS == head).astype(BF16)


def pack_row(row, rows):
    high = row.astype(BF16).astype(F32)
    rest = row - high
    middle = rest.astype(BF16).astype(F32)
    low = rest - middle
    return jnp.concatenate([high, middle, low, jnp.zeros((rows - 3, row.shape[1]), F32)], axis=0)


def unpack_row(rows):
    rows = rows.astype(F32)
    return rows[0:1] + rows[1:2] + rows[2:3]


def spread_total(rows, owner):
    wide = jnp.dot(rows, owner, preferred_element_type=F32)
    return wide[0:1] + wide[1:2] + wide[2:3]


def block_state(parts, bias, rate, x, q, states, group, after=()):
    length, channels = x.shape
    every = parts[0].shape[1] - LANES
    heads = bias.shape[1]
    width = channels // group
    columns = q.shape[1] // group
    bands = width // columns
    count = len(parts)

    def kernel(*refs):
        bias_ref, rate_ref, x_ref, q_ref = refs[count : count + 4]
        climb_ref, climb_t_ref, step_t_ref, maps_ref = refs[count + 4 : count + 8]
        outs = refs[count + 8 : count + 8 + group]
        held = refs[count + 8 + group]
        summed = refs[0][...]
        for ref in refs[1:count]:
            summed = summed + ref[...]
        shift = lax.rem(every - lax.axis_index("tp") * heads, jnp.int32(every))
        raw = pltpu.roll(summed[:, :every], shift, 1) + widen(bias_ref[...], every)
        step = jnp.maximum(raw, 0.0) + jnp.log1p(jnp.exp(-jnp.abs(raw)))
        log_decay = -widen(rate_ref[...], every) * step
        row = lax.broadcasted_iota(jnp.int32, (length, length), 0)
        column = lax.broadcasted_iota(jnp.int32, (length, length), 1)
        lower = (column <= row).astype(F32)
        climb = jnp.dot(
            lower, log_decay, precision=lax.Precision.HIGHEST, preferred_element_type=F32
        )
        maps = summed[:, every:]
        climb_ref[...] = climb
        maps_ref[...] = maps
        climb_t = climb.T
        step_t = step.T
        climb_t_ref[...] = climb_t[:heads]
        step_t_ref[...] = step_t[:heads]
        b_t = maps.T[:states]
        weight_t = jnp.exp(climb_t[:, length - 1 :] - climb_t) * step_t
        bundle = 4
        span = bundle * DECAY_CHANNELS
        owner = lax.broadcasted_iota(jnp.int32, (1, span), 1) // DECAY_CHANNELS
        for at in range(0, heads, bundle):
            feed = [b_t * weight_t[at + i : at + i + 1] for i in range(bundle)]
            feed = jnp.concatenate(feed, axis=0).astype(BF16)
            start = at * DECAY_CHANNELS
            product = jnp.dot(feed, x_ref[:, start : start + span], preferred_element_type=F32)
            state = product[:states]
            for i in range(1, bundle):
                state = jnp.where(owner == i, product[i * states : (i + 1) * states], state)
            piece, offset = divmod(start, width)
            band, offset = divmod(offset, columns)
            rows = slice(band * states, (band + 1) * states)
            held[piece, rows, offset : offset + span] = state.astype(BF16)
        totals = pack_row(climb[length - 1 :], states)
        for piece in range(group):
            at = piece * (heads // group)
            here = totals if not at else pltpu.roll(totals, every - at, 1)
            held[piece, bands * states :, :] = widen(here[:, :LANES], columns).astype(BF16)
        mine = place(group)
        for k in range(group):
            here = pl.ds(pl.multiple_of((mine ^ k) * columns, columns), columns)
            outs[k][:length] = q_ref[:, here]
            outs[k][length:] = held[mine ^ k]

    payload = shape_of((length + (bands + 1) * states, columns), BF16)
    result = launch(
        kernel,
        "block_state",
        [
            shape_of((length, every), F32),
            shape_of((heads, length), F32),
            shape_of((heads, length), F32),
            shape_of((length, LANES), F32),
        ]
        + [payload] * group,
        *parts,
        bias,
        rate,
        x,
        q,
        after=after,
        flops=32 * length * states * channels,
        scratch=[pltpu.VMEM((group, (bands + 1) * states, columns), BF16)],
    )
    return result[:4], result[4:]


def local_part(x, gate, climb, climb_t, step_t, maps, skip, states, after=()):
    length, channels = x.shape
    heads = channels // DECAY_CHANNELS

    def kernel(
        x_ref, gate_ref, climb_ref, climb_t_ref, step_t_ref, maps_ref, skip_ref, still_ref, scale_ref
    ):
        maps = maps_ref[...]
        inner = lax.dot_general(
            maps[:, states : 2 * states],
            maps[:, :states],
            (((1,), (1,)), ((), ())),
            precision=lax.Precision.HIGHEST,
            preferred_element_type=F32,
        )
        row = lax.broadcasted_iota(jnp.int32, (length, length), 0)
        column = lax.broadcasted_iota(jnp.int32, (length, length), 1)
        inner = jnp.where(column <= row, inner, 0.0)
        left = lax.broadcasted_iota(jnp.int32, (length, LANES), 1) < DECAY_CHANNELS

        for j in range(0, heads, 2):
            columns = slice(j * DECAY_CHANNELS, j * DECAY_CHANNELS + LANES)
            x = x_ref[:, columns]
            wide = [jnp.broadcast_to(climb_ref[:, i : i + 1], (length, length)) for i in (j, j + 1)]
            mixed = []
            for i in (j, j + 1):
                fall = jnp.minimum(wide[i - j] - climb_t_ref[i : i + 1], 0.0)
                mixed.append((inner * jnp.exp(fall) * step_t_ref[i : i + 1]).astype(BF16))
            zero = jnp.zeros_like(x)
            feeds = jnp.concatenate([jnp.where(left, x, zero), jnp.where(left, zero, x)], axis=0)
            local = jnp.dot(jnp.concatenate(mixed, axis=1), feeds, preferred_element_type=F32)
            gain = jnp.where(left[:1], skip_ref[:, j : j + 1], skip_ref[:, j + 1 : j + 2])
            grown = jnp.exp(jnp.where(left, wide[0], wide[1]))
            gate = gate_ref[:, columns].astype(F32)
            silu = gate / (1.0 + jnp.exp(-gate))
            still_ref[:, columns] = (local + gain * x.astype(F32)) * silu
            scale_ref[:, columns] = grown * silu

    return launch(
        kernel,
        "local_part",
        [shape_of((length, channels), F32)] * 2,
        x,
        gate,
        climb,
        climb_t,
        step_t,
        maps,
        skip,
        after=after,
        flops=4 * length * length * channels,
    )


def gather_blocks(group, states, length, refs, held):
    mine = place(group)
    for k in range(group):
        held[mine ^ k] = refs[k][length:]


def block_of(held, b, states, columns, width):
    bands = width // columns
    rows = [held[b, i * states : (i + 1) * states] for i in range(bands)]
    state = jnp.concatenate(rows, axis=1) if bands > 1 else rows[0]
    return state.astype(F32), held[b, bands * states :, :LANES]


def group_total(payloads, length, states, width, after=()):
    group = len(payloads)
    rows, columns = payloads[0].shape
    heads = width // DECAY_CHANNELS

    def kernel(*refs):
        out_ref, held = refs[group:]
        gather_blocks(group, states, length, refs[:group], held)
        owner = owners(heads)
        state, packed = block_of(held, 0, states, columns, width)
        total = unpack_row(packed)
        for b in range(1, group):
            more, packed = block_of(held, b, states, columns, width)
            state = jnp.exp(spread_total(packed, owner)) * state + more
            total = total + unpack_row(packed)
        out_ref[:, :width] = state.astype(BF16)
        out_ref[:, width:] = pack_row(total, states).astype(BF16)

    return launch(
        kernel,
        "group_total",
        shape_of((states, width + LANES), BF16),
        *payloads,
        after=after,
        scratch=[pltpu.VMEM((group, rows - length, columns), BF16)],
    )


def entering_states(payloads, earlier, length, states, width, after=()):
    group = len(payloads)
    rows, columns = payloads[0].shape
    heads = width // DECAY_CHANNELS
    count = len(earlier)

    def kernel(*refs):
        earlier_refs = refs[group : group + count]
        outs = refs[group + count : 2 * group + count]
        held, entering = refs[2 * group + count :]
        gather_blocks(group, states, length, refs[:group], held)
        owner = owners(heads)
        state = jnp.zeros((states, width), F32)
        for ref in reversed(earlier_refs):
            state = jnp.exp(spread_total(ref[:, width:], owner)) * state
            state = state + ref[:, :width].astype(F32)
        for b in range(group):
            entering[b] = state
            if b < group - 1:
                more, packed = block_of(held, b, states, columns, width)
                state = jnp.exp(spread_total(packed, owner)) * state + more
        mine = place(group)
        for k in range(group):
            outs[k][...] = entering[mine ^ k]

    return launch(
        kernel,
        "entering_states",
        [shape_of((states, width), F32)] * group,
        *payloads,
        *earlier,
        after=after,
        scratch=[
            pltpu.VMEM((group, rows - length, columns), BF16),
            pltpu.VMEM((group, states, width), F32),
        ],
    )


def carried_part(maps, still, scale, entering, states, after=()):
    length, channels = still.shape
    group = len(entering)
    width = channels // group
    span = min(width, 512)

    def kernel(maps_ref, still_ref, scale_ref, *refs):
        gated_ref, square_ref, held = refs[group:]
        mine = place(group)
        for k in range(group):
            held[mine ^ k] = refs[k][...]
        c = maps_ref[:, states : 2 * states]
        c_high = c.astype(BF16)
        c_low = (c - c_high.astype(F32)).astype(BF16)
        c = jnp.concatenate([c_high, c_low, c_high], axis=1)
        folded = jnp.zeros(square_ref.shape, F32)
        for at in range(0, channels, span):
            piece, offset = divmod(at, width)
            state = held[piece, :, offset : offset + span]
            high = state.astype(BF16)
            low = (state - high.astype(F32)).astype(BF16)
            carried = jnp.dot(
                c, jnp.concatenate([high, high, low], axis=0), preferred_element_type=F32
            )
            columns = slice(at, at + span)
            gated = still_ref[:, columns] + scale_ref[:, columns] * carried
            gated_ref[:, columns] = gated
            square = gated * gated
            for lane in range(0, span, LANES):
                folded = folded + square[:, lane : lane + LANES]
        square_ref[...] = folded

    return launch(
        kernel,
        "carried_part",
        [shape_of((length, channels), F32), shape_of((length, LANES), F32)],
        maps,
        still,
        scale,
        *entering,
        after=after,
        flops=6 * length * states * channels,
        scratch=[pltpu.VMEM((group, states, width), F32)],
    )


def norm(gated, gain, squares, every):
    length, channels = gated.shape
    count = len(squares)

    def kernel(gated_ref, gain_ref, *refs):
        out_ref = refs[count]
        square = refs[0][...]
        for ref in refs[1:count]:
            square = square + ref[...]
        mean = jnp.sum(square, axis=1, keepdims=True) / every
        factor = jnp.broadcast_to(lax.rsqrt(mean + 1e-05), square.shape)
        for at in range(0, channels, LANES):
            columns = slice(at, at + LANES)
            out_ref[:, columns] = (gated_ref[:, columns] * factor * gain_ref[:, columns]).astype(BF16)

    return launch(
        kernel, "norm", shape_of((length, channels), BF16), gated, gain, *squares
    )


def shared_parts(part):
    if lax.axis_size("tp") == 2:
        return [part, lax.ppermute(part, "tp", [(0, 1), (1, 0)])]
    return [lax.psum(part, "tp")]


def earlier_states(total, group, turns, count, states, width):
    if turns <= UNROLL:
        return [climb_up(total, group, count, steps) for steps in range(1, turns)]
    heads = width // DECAY_CHANNELS

    def one(_, carry):
        travelling, summed, ahead = carry
        travelling = climb_up(travelling, group, count)
        summed = summed + jnp.exp(ahead) * travelling[:, :width].astype(F32)
        more = unpack_row(travelling[:, width : width + heads])
        return travelling, summed, ahead + jnp.repeat(more, DECAY_CHANNELS, axis=1)

    start = (total, jnp.zeros((states, width), F32), jnp.zeros((1, width), F32))
    _, summed, _ = lax.fori_loop(1, turns, one, start)
    return [jnp.concatenate([summed.astype(BF16), jnp.zeros((states, LANES), BF16)], axis=1)]


def per_device(
    queries,
    keys,
    values,
    mixer_input,
    gate,
    step_weight,
    state_weight,
    step_bias,
    decay_rate,
    skip_gain,
    norm_gain,
):
    count = lax.axis_size("ctx")
    length = queries.shape[0]
    channels = mixer_input.shape[1]
    states = state_weight.shape[1] // 2
    group = math.gcd(keys.shape[1] // HD, count)
    turns = count // group
    width = channels // group

    packed = pack_kv(keys, values, group)
    blocks = swap(packed, group, count)
    half = max(group // 2, 1)
    own = [jnp.stack(blocks[at : at + half]) for at in range(0, group, half)]

    def onward(chunk):
        return [climb_up(part, group, count) for part in chunk]

    ring = 1 < turns <= UNROLL
    arrived = [onward(own)] if ring else []
    parts = shared_parts(project(mixer_input, step_weight, state_weight, after=own))
    (climb, climb_t, step_t, maps), payloads = block_state(
        parts,
        step_bias[None],
        decay_rate[None],
        mixer_input,
        queries,
        states,
        group,
        after=arrived[0] if ring else [],
    )
    ready = []
    if ring and turns > 2:
        arrived[0] = [tie(part, payloads[:1]) for part in arrived[0]]
        ready = arrived[0][:1]
        arrived.append(onward(arrived[0]))
    payloads = swap(payloads, group, count)
    still, scale = local_part(
        mixer_input, gate, climb, climb_t, step_t, maps, skip_gain[None], states
    )
    total = group_total(payloads, length, states, width, after=[still] + ready)
    earlier = earlier_states(total, group, turns, count, states, width)
    state = flash(payloads, length, own=own, chunks=arrived[:-1][:1], after=[total])
    if ring and turns > 3:
        arrived[1] = [tie(part, [state[1]] + earlier) for part in arrived[1]]
        ready = arrived[1][:1]
        arrived.append(onward(arrived[1]))
        for step in range(4, turns):
            arrived.append(onward(arrived[-1]))
    entering = entering_states(payloads, earlier, length, states, width, after=ready)
    if ring and turns > 3:
        state = flash(
            payloads, length, state=state, chunks=arrived[1:-1], base=2, after=entering[:1]
        )
    entering = swap(entering, group, count)
    if turns > 1 and not ring:

        def one(step, carry):
            chunk, state = carry
            chunk = onward(chunk)
            state = flash(payloads, length, state=state, chunks=[chunk], base=jnp.reshape(step, (1,)))
            return chunk, tuple(state)

        chunk, state = lax.fori_loop(1, turns - 1, one, (own, tuple(state)))
        arrived.append(onward(chunk))
    gated, square = carried_part(maps, still, scale, entering, states)
    mamba_out = norm(
        gated, norm_gain[None], shared_parts(square), channels * lax.axis_size("tp")
    )
    if turns == 1:
        outs = flash(payloads, length, own=own, final=True)
    else:
        outs = flash(
            payloads, length, state=state, chunks=arrived[-1:], final=True, base=turns - 1
        )
    return join(swap(outs, group, count), group), mamba_out


def solution(mesh):
    return jax.shard_map(
        per_device,
        mesh=mesh,
        in_specs=(
            P("ctx", "tp"),
            P("ctx", "tp"),
            P("ctx", "tp"),
            P("ctx", "tp"),
            P("ctx", "tp"),
            P("tp", None),
            P("tp", None),
            P("tp"),
            P("tp"),
            P("tp"),
            P("tp"),
        ),
        out_specs=(P("ctx", "tp"), P("ctx", "tp")),
        check_vma=False,
    )
```

```python
import functools
import math

import jax
import jax.numpy as jnp
from jax import lax
from jax.experimental import pallas as pl
from jax.experimental.pallas import tpu as pltpu
from jax.sharding import PartitionSpec as P

HD = 128
DECAY_CHANNELS = 64
SCAN_TOKENS = 128
LANES = 128
UNROLL = 8
VMEM_LIMIT = 14 * 1024 * 1024

F32 = jnp.float32
BF16 = jnp.bfloat16


def vmem():
    return pl.BlockSpec(memory_space=pltpu.VMEM)


def hbm():
    return pl.BlockSpec(memory_space=pltpu.HBM)


def launch(kernel, name, out_shape, *inputs, after=(), flops=0, scratch=(), in_specs=None, out_specs=None, grid=None):
    count, skip = len(inputs), len(after)
    single = isinstance(out_shape, jax.ShapeDtypeStruct)
    shapes = [out_shape] if single else list(out_shape)
    size = sum(x.size * x.dtype.itemsize for x in list(inputs) + shapes)

    def body(*refs):
        kernel(*refs[:count], *refs[count + skip :])

    result = pl.pallas_call(
        body,
        **({} if grid is None else {"grid": grid}),
        out_shape=shapes,
        in_specs=(in_specs or [vmem()] * count) + [pl.BlockSpec(memory_space=pl.ANY)] * skip,
        out_specs=out_specs or [vmem()] * len(shapes),
        scratch_shapes=list(scratch),
        compiler_params=pltpu.CompilerParams(vmem_limit_bytes=VMEM_LIMIT),
        cost_estimate=pl.CostEstimate(flops=flops, bytes_accessed=size, transcendentals=0),
        name=name,
    )(*inputs, *after)
    return result[0] if single else result


def place(group):
    return lax.rem(lax.axis_index("ctx"), jnp.int32(group))


def swap(pieces, group, count):
    result = [pieces[0]]
    for k in range(1, group):
        perm = [(i, (i // group) * group + ((i % group) ^ k)) for i in range(count)]
        result.append(lax.ppermute(pieces[k], "ctx", perm))
    return result


def climb_up(array, group, count, steps=1):
    perm = [(i, i + group * steps) for i in range(count - group * steps)]
    return lax.ppermute(array, "ctx", perm)


def shape_of(shape, dtype):
    return jax.ShapeDtypeStruct(shape, dtype)


def tie(array, after):
    return pl.pallas_call(
        lambda *refs: None,
        out_shape=shape_of(array.shape, array.dtype),
        in_specs=[pl.BlockSpec(memory_space=pl.ANY)] * (1 + len(after)),
        out_specs=pl.BlockSpec(memory_space=pl.ANY),
        input_output_aliases={0: 0},
        compiler_params=pltpu.CompilerParams(vmem_limit_bytes=1024 * 1024),
        name="tie",
    )(array, *after)


def pack_kv(keys, values, group):
    length, width = keys.shape
    piece = width // group

    def kernel(k_ref, v_ref, *outs):
        mine = place(group)
        for k in range(group):
            columns = pl.ds(pl.multiple_of((mine ^ k) * piece, piece), piece)
            outs[k][0] = k_ref[:, columns]
            outs[k][1] = v_ref[:, columns]

    return launch(
        kernel,
        "pack_kv",
        [shape_of((2, length, piece), keys.dtype)] * group,
        keys,
        values,
        flops=5000000000,
        grid=(1,),
        in_specs=[pl.BlockSpec((length, width), lambda i: (0, 0))] * 2,
    )


def join(pieces, group):
    length, width = pieces[0].shape

    def kernel(*refs):
        out_ref, sems = refs[group:]
        mine = place(group)
        copies = []
        for k in range(group):
            columns = pl.ds(pl.multiple_of((mine ^ k) * width, width), width)
            copies.append(pltpu.make_async_copy(refs[k], out_ref.at[:, columns], sems.at[k]))
        for copy in copies:
            copy.start()
        for copy in copies:
            copy.wait()

    return launch(
        kernel,
        "join_heads",
        shape_of((length, width * group), pieces[0].dtype),
        *pieces,
        out_specs=[hbm()],
        scratch=[pltpu.SemaphoreType.DMA((group,))],
    )


def flash_chunk(q_refs, kv_ref, before, after, extended, own, length):
    group = len(q_refs)
    heads = q_refs[0].shape[1] // HD
    kv_heads = kv_ref.shape[3] // HD
    share = heads // kv_heads
    rows = group * length
    tile = min(rows, 2 * length)
    rate = math.log2(math.e) / math.sqrt(HD)
    for kv in range(kv_heads):
        lanes = slice(kv * HD, (kv + 1) * HD)
        keys = kv_ref[:, 0, :, lanes].reshape(rows, HD)
        extended[:, :HD] = kv_ref[:, 1, :, lanes].reshape(rows, HD)
        extended[:, HD:] = jnp.ones((rows, HD), BF16)
        tiles = [
            (h, start)
            for start in range(0, rows, tile)
            for h in range(kv * share, (kv + 1) * share)
        ]

        def score(h, start):
            parts = q_refs[start // length : (start + tile) // length]
            q = [ref[:length, h * HD : (h + 1) * HD] for ref in parts]
            q = jnp.concatenate(q, axis=0) if len(q) > 1 else q[0]
            scores = lax.dot_general(
                q, keys, (((1,), (1,)), ((), ())), preferred_element_type=F32
            )
            if own:
                flip = place(group) * length
                row = (lax.broadcasted_iota(jnp.int32, (tile, rows), 0) + start) ^ flip
                column = lax.broadcasted_iota(jnp.int32, (tile, rows), 1) ^ flip
                scores = jnp.where(column <= row, scores, -1e30)
            return scores

        ahead = score(*tiles[0])
        for n, (h, start) in enumerate(tiles):
            scores = ahead
            if n + 1 < len(tiles):
                ahead = score(*tiles[n + 1])
            here = slice(start, start + tile)
            top = jnp.max(scores, axis=1, keepdims=True)
            if not own:
                top_before = before[1][h, here]
                top = jnp.maximum(top_before[:, :1], top)
            weights = jnp.exp2((scores - top) * rate).astype(BF16)
            value = jnp.dot(weights, extended[...], preferred_element_type=F32)
            top = jnp.broadcast_to(top, (tile, LANES))
            if not own:
                keep = jnp.exp2((top_before - top) * rate)
                value = value + before[0][h, here] * jnp.concatenate([keep, keep], axis=1)
            yield h, start, tile, value
            if after is not None:
                after[0][h, here] = value
                after[1][h, here] = top


def finish_rows(out_refs, h, start, tile, value):
    length = out_refs[0].shape[0]
    result = (value[:, :HD] / value[:, HD:]).astype(BF16)
    for at in range(0, tile, length):
        out_refs[(start + at) // length][:, h * HD : (h + 1) * HD] = result[at : at + length]


def flash(q, length, own=None, state=(), chunks=(), final=False, base=1, after=()):
    group = len(q)
    heads = q[0].shape[1] // HD
    rows = group * length
    fixed = isinstance(base, int)
    has_own = own is not None
    specs = [] if fixed else [pl.BlockSpec(memory_space=pltpu.SMEM)]
    rest = list(q) + ([own] if has_own else []) + list(state) + list(chunks)
    specs = specs + [vmem()] * len(rest)

    def kernel(*refs):
        refs = list(refs)
        first = base if fixed else refs.pop(0)[0]
        q_refs = [refs.pop(0) for _ in range(group)]
        own_ref = refs.pop(0) if has_own else None
        held = None if has_own else (refs.pop(0), refs.pop(0))
        chunk_refs = [refs.pop(0) for _ in range(len(chunks))]
        extended = refs.pop()
        turn = lax.axis_index("ctx") // group
        outs = None if final else tuple(refs)
        if has_own:
            for done in flash_chunk(q_refs, own_ref, None, outs, extended, True, length):
                if final:
                    finish_rows(refs, *done)
            held = outs
        for number, ref in enumerate(chunk_refs):

            @pl.when(turn >= first + number)
            def _(ref=ref, held=held):
                for done in flash_chunk(q_refs, ref, held, outs, extended, False, length):
                    if final:
                        finish_rows(refs, *done)

            if not has_own and number == 0:

                @pl.when(turn < first)
                def _(held=held):
                    for h in range(heads):
                        if final:
                            finish_rows(refs, h, 0, rows, held[0][h])
                        else:
                            outs[0][h] = held[0][h]
                            outs[1][h] = held[1][h]

            held = outs

    if final:
        out_shape = [shape_of((length, heads * HD), BF16)] * group
    else:
        out_shape = [
            shape_of((heads, rows, HD + LANES), F32),
            shape_of((heads, rows, LANES), F32),
        ]
    parts = len(chunks) + has_own
    return launch(
        kernel,
        "flash",
        out_shape,
        *([] if fixed else [base]),
        *rest,
        after=after,
        in_specs=specs,
        flops=4 * heads * rows * rows * HD * parts,
        scratch=[pltpu.VMEM((rows, HD + LANES), BF16)],
    )


def widen(row, lanes):
    extra = lanes - row.shape[1]
    if not extra:
        return row
    return jnp.concatenate([row, jnp.zeros((row.shape[0], extra), row.dtype)], axis=1)


def project(x, step_weight, state_weight, after=()):
    length, channels = x.shape
    heads = step_weight.shape[1]

    def kernel(x_ref, step_ref, map_ref, out_ref):
        x = x_ref[...]
        out_ref[:, :heads] = jnp.dot(x, step_ref[...], preferred_element_type=F32)
        maps = lax.dot_general(
            x, map_ref[...], (((1,), (1,)), ((), ())), preferred_element_type=F32
        )
        out_ref[:, heads:] = widen(maps, LANES)

    return launch(
        kernel,
        "project",
        shape_of((length, heads + LANES), F32),
        x,
        step_weight,
        state_weight.T,
        after=after,
        flops=4 * length * channels * heads,
    )


def owners(heads):
    shape = (LANES, heads * DECAY_CHANNELS)
    head = lax.broadcasted_iota(jnp.int32, shape, 0)
    channel = lax.broadcasted_iota(jnp.int32, shape, 1)
    return (channel // DECAY_CHANNELS == head).astype(BF16)


def pack_row(row, rows):
    high = row.astype(BF16).astype(F32)
    rest = row - high
    middle = rest.astype(BF16).astype(F32)
    low = rest - middle
    return jnp.concatenate([high, middle, low, jnp.zeros((rows - 3, row.shape[1]), F32)], axis=0)


def unpack_row(rows):
    rows = rows.astype(F32)
    return rows[0:1] + rows[1:2] + rows[2:3]


def spread_total(rows, owner):
    wide = jnp.dot(rows, owner, preferred_element_type=F32)
    return wide[0:1] + wide[1:2] + wide[2:3]


def block_state(parts, bias, rate, x, q, states, group, after=()):
    length, channels = x.shape
    every = parts[0].shape[1] - LANES
    heads = bias.shape[1]
    width = channels // group
    columns = q.shape[1] // group
    bands = width // columns
    count = len(parts)

    def kernel(*refs):
        bias_ref, rate_ref, x_ref, q_ref = refs[count : count + 4]
        climb_ref, climb_t_ref, step_t_ref, maps_ref = refs[count + 4 : count + 8]
        outs = refs[count + 8 : count + 8 + group]
        held = refs[count + 8 + group]
        summed = refs[0][...]
        for ref in refs[1:count]:
            summed = summed + ref[...]
        shift = lax.rem(every - lax.axis_index("tp") * heads, jnp.int32(every))
        raw = pltpu.roll(summed[:, :every], shift, 1) + widen(bias_ref[...], every)
        step = jnp.maximum(raw, 0.0) + jnp.log1p(jnp.exp(-jnp.abs(raw)))
        log_decay = -widen(rate_ref[...], every) * step
        row = lax.broadcasted_iota(jnp.int32, (length, length), 0)
        column = lax.broadcasted_iota(jnp.int32, (length, length), 1)
        lower = (column <= row).astype(F32)
        climb = jnp.dot(
            lower, log_decay, precision=lax.Precision.HIGHEST, preferred_element_type=F32
        )
        maps = summed[:, every:]
        climb_ref[...] = climb
        maps_ref[...] = maps
        climb_t = climb.T
        step_t = step.T
        climb_t_ref[...] = climb_t[:heads]
        step_t_ref[...] = step_t[:heads]
        b_t = maps.T[:states]
        weight_t = jnp.exp(climb_t[:, length - 1 :] - climb_t) * step_t
        bundle = 4
        span = bundle * DECAY_CHANNELS
        owner = lax.broadcasted_iota(jnp.int32, (1, span), 1) // DECAY_CHANNELS
        for at in range(0, heads, bundle):
            feed = [b_t * weight_t[at + i : at + i + 1] for i in range(bundle)]
            feed = jnp.concatenate(feed, axis=0).astype(BF16)
            start = at * DECAY_CHANNELS
            product = jnp.dot(feed, x_ref[:, start : start + span], preferred_element_type=F32)
            state = product[:states]
            for i in range(1, bundle):
                state = jnp.where(owner == i, product[i * states : (i + 1) * states], state)
            piece, offset = divmod(start, width)
            band, offset = divmod(offset, columns)
            rows = slice(band * states, (band + 1) * states)
            held[piece, rows, offset : offset + span] = state.astype(BF16)
        totals = pack_row(climb[length - 1 :], states)
        for piece in range(group):
            at = piece * (heads // group)
            here = totals if not at else pltpu.roll(totals, every - at, 1)
            held[piece, bands * states :, :] = widen(here[:, :LANES], columns).astype(BF16)
        mine = place(group)
        for k in range(group):
            here = pl.ds(pl.multiple_of((mine ^ k) * columns, columns), columns)
            outs[k][:length] = q_ref[:, here]
            outs[k][length:] = held[mine ^ k]

    payload = shape_of((length + (bands + 1) * states, columns), BF16)
    result = launch(
        kernel,
        "block_state",
        [
            shape_of((length, every), F32),
            shape_of((heads, length), F32),
            shape_of((heads, length), F32),
            shape_of((length, LANES), F32),
        ]
        + [payload] * group,
        *parts,
        bias,
        rate,
        x,
        q,
        after=after,
        flops=32 * length * states * channels,
        scratch=[pltpu.VMEM((group, (bands + 1) * states, columns), BF16)],
    )
    return result[:4], result[4:]


def local_part(x, gate, climb, climb_t, step_t, maps, skip, states, after=()):
    length, channels = x.shape
    heads = channels // DECAY_CHANNELS

    def kernel(
        x_ref, gate_ref, climb_ref, climb_t_ref, step_t_ref, maps_ref, skip_ref, still_ref, scale_ref
    ):
        maps = maps_ref[...]
        inner = lax.dot_general(
            maps[:, states : 2 * states],
            maps[:, :states],
            (((1,), (1,)), ((), ())),
            precision=lax.Precision.HIGHEST,
            preferred_element_type=F32,
        )
        row = lax.broadcasted_iota(jnp.int32, (length, length), 0)
        column = lax.broadcasted_iota(jnp.int32, (length, length), 1)
        inner = jnp.where(column <= row, inner, 0.0)
        left = lax.broadcasted_iota(jnp.int32, (length, LANES), 1) < DECAY_CHANNELS

        for j in range(0, heads, 2):
            columns = slice(j * DECAY_CHANNELS, j * DECAY_CHANNELS + LANES)
            x = x_ref[:, columns]
            wide = [jnp.broadcast_to(climb_ref[:, i : i + 1], (length, length)) for i in (j, j + 1)]
            mixed = []
            for i in (j, j + 1):
                fall = jnp.minimum(wide[i - j] - climb_t_ref[i : i + 1], 0.0)
                mixed.append((inner * jnp.exp(fall) * step_t_ref[i : i + 1]).astype(BF16))
            zero = jnp.zeros_like(x)
            feeds = jnp.concatenate([jnp.where(left, x, zero), jnp.where(left, zero, x)], axis=0)
            local = jnp.dot(jnp.concatenate(mixed, axis=1), feeds, preferred_element_type=F32)
            gain = jnp.where(left[:1], skip_ref[:, j : j + 1], skip_ref[:, j + 1 : j + 2])
            grown = jnp.exp(jnp.where(left, wide[0], wide[1]))
            gate = gate_ref[:, columns].astype(F32)
            silu = gate / (1.0 + jnp.exp(-gate))
            still_ref[:, columns] = (local + gain * x.astype(F32)) * silu
            scale_ref[:, columns] = grown * silu

    return launch(
        kernel,
        "local_part",
        [shape_of((length, channels), F32)] * 2,
        x,
        gate,
        climb,
        climb_t,
        step_t,
        maps,
        skip,
        after=after,
        flops=4 * length * length * channels,
    )


def gather_blocks(group, states, length, refs, held):
    mine = place(group)
    for k in range(group):
        held[mine ^ k] = refs[k][length:]


def block_of(held, b, states, columns, width):
    bands = width // columns
    rows = [held[b, i * states : (i + 1) * states] for i in range(bands)]
    state = jnp.concatenate(rows, axis=1) if bands > 1 else rows[0]
    return state.astype(F32), held[b, bands * states :, :LANES]


def group_total(payloads, length, states, width, after=()):
    group = len(payloads)
    rows, columns = payloads[0].shape
    heads = width // DECAY_CHANNELS

    def kernel(*refs):
        out_ref, held = refs[group:]
        gather_blocks(group, states, length, refs[:group], held)
        owner = owners(heads)
        state, packed = block_of(held, 0, states, columns, width)
        total = unpack_row(packed)
        for b in range(1, group):
            more, packed = block_of(held, b, states, columns, width)
            state = jnp.exp(spread_total(packed, owner)) * state + more
            total = total + unpack_row(packed)
        out_ref[:, :width] = state.astype(BF16)
        out_ref[:, width:] = pack_row(total, states).astype(BF16)

    return launch(
        kernel,
        "group_total",
        shape_of((states, width + LANES), BF16),
        *payloads,
        after=after,
        scratch=[pltpu.VMEM((group, rows - length, columns), BF16)],
    )


def entering_states(payloads, earlier, length, states, width, after=()):
    group = len(payloads)
    rows, columns = payloads[0].shape
    heads = width // DECAY_CHANNELS
    count = len(earlier)

    def kernel(*refs):
        earlier_refs = refs[group : group + count]
        outs = refs[group + count : 2 * group + count]
        held, entering = refs[2 * group + count :]
        gather_blocks(group, states, length, refs[:group], held)
        owner = owners(heads)
        state = jnp.zeros((states, width), F32)
        for ref in reversed(earlier_refs):
            state = jnp.exp(spread_total(ref[:, width:], owner)) * state
            state = state + ref[:, :width].astype(F32)
        for b in range(group):
            entering[b] = state
            if b < group - 1:
                more, packed = block_of(held, b, states, columns, width)
                state = jnp.exp(spread_total(packed, owner)) * state + more
        mine = place(group)
        for k in range(group):
            outs[k][...] = entering[mine ^ k]

    return launch(
        kernel,
        "entering_states",
        [shape_of((states, width), F32)] * group,
        *payloads,
        *earlier,
        after=after,
        scratch=[
            pltpu.VMEM((group, rows - length, columns), BF16),
            pltpu.VMEM((group, states, width), F32),
        ],
    )


def carried_part(maps, still, scale, entering, states, after=()):
    length, channels = still.shape
    group = len(entering)
    width = channels // group
    span = min(width, 512)

    def kernel(maps_ref, still_ref, scale_ref, *refs):
        gated_ref, square_ref, held = refs[group:]
        mine = place(group)
        for k in range(group):
            held[mine ^ k] = refs[k][...]
        c = maps_ref[:, states : 2 * states]
        c_high = c.astype(BF16)
        c_low = (c - c_high.astype(F32)).astype(BF16)
        c = jnp.concatenate([c_high, c_low, c_high], axis=1)
        folded = jnp.zeros(square_ref.shape, F32)
        for at in range(0, channels, span):
            piece, offset = divmod(at, width)
            state = held[piece, :, offset : offset + span]
            high = state.astype(BF16)
            low = (state - high.astype(F32)).astype(BF16)
            carried = jnp.dot(
                c, jnp.concatenate([high, high, low], axis=0), preferred_element_type=F32
            )
            columns = slice(at, at + span)
            gated = still_ref[:, columns] + scale_ref[:, columns] * carried
            gated_ref[:, columns] = gated
            square = gated * gated
            for lane in range(0, span, LANES):
                folded = folded + square[:, lane : lane + LANES]
        square_ref[...] = folded

    return launch(
        kernel,
        "carried_part",
        [shape_of((length, channels), F32), shape_of((length, LANES), F32)],
        maps,
        still,
        scale,
        *entering,
        after=after,
        flops=6 * length * states * channels,
        scratch=[pltpu.VMEM((group, states, width), F32)],
    )


def norm(gated, gain, squares, every):
    length, channels = gated.shape
    count = len(squares)

    def kernel(gated_ref, gain_ref, *refs):
        out_ref = refs[count]
        square = refs[0][...]
        for ref in refs[1:count]:
            square = square + ref[...]
        mean = jnp.sum(square, axis=1, keepdims=True) / every
        factor = jnp.broadcast_to(lax.rsqrt(mean + 1e-05), square.shape)
        for at in range(0, channels, LANES):
            columns = slice(at, at + LANES)
            out_ref[:, columns] = (gated_ref[:, columns] * factor * gain_ref[:, columns]).astype(BF16)

    return launch(
        kernel, "norm", shape_of((length, channels), BF16), gated, gain, *squares
    )


def shared_parts(part):
    if lax.axis_size("tp") == 2:
        return [part, lax.ppermute(part, "tp", [(0, 1), (1, 0)])]
    return [lax.psum(part, "tp")]


def earlier_states(total, group, turns, count, states, width):
    if turns <= UNROLL:
        return [climb_up(total, group, count, steps) for steps in range(1, turns)]
    heads = width // DECAY_CHANNELS

    def one(_, carry):
        travelling, summed, ahead = carry
        travelling = climb_up(travelling, group, count)
        summed = summed + jnp.exp(ahead) * travelling[:, :width].astype(F32)
        more = unpack_row(travelling[:, width : width + heads])
        return travelling, summed, ahead + jnp.repeat(more, DECAY_CHANNELS, axis=1)

    start = (total, jnp.zeros((states, width), F32), jnp.zeros((1, width), F32))
    _, summed, _ = lax.fori_loop(1, turns, one, start)
    return [jnp.concatenate([summed.astype(BF16), jnp.zeros((states, LANES), BF16)], axis=1)]


def per_device(
    queries,
    keys,
    values,
    mixer_input,
    gate,
    step_weight,
    state_weight,
    step_bias,
    decay_rate,
    skip_gain,
    norm_gain,
):
    count = lax.axis_size("ctx")
    length = queries.shape[0]
    channels = mixer_input.shape[1]
    states = state_weight.shape[1] // 2
    group = math.gcd(keys.shape[1] // HD, count)
    turns = count // group
    width = channels // group

    packed = pack_kv(keys, values, group)
    own = jnp.stack(swap(packed, group, count))
    parts = shared_parts(project(mixer_input, step_weight, state_weight, after=[]))
    (climb, climb_t, step_t, maps), payloads = block_state(
        parts, step_bias[None], decay_rate[None], mixer_input, queries, states, group, after=[own]
    )
    sent = payloads[:1]
    payloads = swap(payloads, group, count)
    still, scale = local_part(
        mixer_input, gate, climb, climb_t, step_t, maps, skip_gain[None], states
    )
    ring = 1 < turns <= UNROLL
    arrived, ready = [], []
    if ring:
        arrived.append(climb_up(own, group, count))
    if ring and turns > 2:
        arrived[0] = tie(arrived[0], sent)
        ready = [arrived[0]]
        arrived.append(climb_up(arrived[0], group, count))
    total = group_total(payloads, length, states, width, after=[still] + ready)
    earlier = earlier_states(total, group, turns, count, states, width)
    state = flash(payloads, length, own=own, chunks=arrived[:-1][:1], after=[total])
    if ring and turns > 3:
        arrived[1] = tie(arrived[1], [state[1]] + earlier)
        ready = [arrived[1]]
        arrived.append(climb_up(arrived[1], group, count))
        for step in range(4, turns):
            arrived.append(climb_up(arrived[-1], group, count))
    entering = entering_states(payloads, earlier, length, states, width, after=ready)
    if ring and turns > 3:
        state = flash(
            payloads, length, state=state, chunks=arrived[1:-1], base=2, after=entering[:1]
        )
    entering = swap(entering, group, count)
    if turns > 1 and not ring:

        def one(step, carry):
            chunk, state = carry
            chunk = climb_up(chunk, group, count)
            state = flash(payloads, length, state=state, chunks=[chunk], base=jnp.reshape(step, (1,)))
            return chunk, tuple(state)

        chunk, state = lax.fori_loop(1, turns - 1, one, (own, tuple(state)))
        arrived.append(climb_up(chunk, group, count))
    gated, square = carried_part(maps, still, scale, entering, states)
    mamba_out = norm(
        gated, norm_gain[None], shared_parts(square), channels * lax.axis_size("tp")
    )
    if turns == 1:
        outs = flash(payloads, length, own=own, final=True)
    else:
        outs = flash(
            payloads, length, state=state, chunks=arrived[-1:], final=True, base=turns - 1
        )
    return join(swap(outs, group, count), group), mamba_out


def solution(mesh):
    return jax.shard_map(
        per_device,
        mesh=mesh,
        in_specs=(
            P("ctx", "tp"),
            P("ctx", "tp"),
            P("ctx", "tp"),
            P("ctx", "tp"),
            P("ctx", "tp"),
            P("tp", None),
            P("tp", None),
            P("tp"),
            P("tp"),
            P("tp"),
            P("tp"),
        ),
        out_specs=(P("ctx", "tp"), P("ctx", "tp")),
        check_vma=False,
    )
```

```python
import functools
import math

import jax
import jax.numpy as jnp
from jax import lax
from jax.experimental import pallas as pl
from jax.experimental.pallas import tpu as pltpu
from jax.sharding import PartitionSpec as P

HD = 128
DECAY_CHANNELS = 64
SCAN_TOKENS = 128
LANES = 128
UNROLL = 8
LOG2E = math.log2(math.e)
VMEM_LIMIT = 14 * 1024 * 1024

F32 = jnp.float32
BF16 = jnp.bfloat16


def vmem():
    return pl.BlockSpec(memory_space=pltpu.VMEM)


def hbm():
    return pl.BlockSpec(memory_space=pltpu.HBM)


def launch(kernel, name, out_shape, *inputs, after=(), flops=0, scratch=(), in_specs=None, out_specs=None, grid=None):
    count, skip = len(inputs), len(after)
    single = isinstance(out_shape, jax.ShapeDtypeStruct)
    shapes = [out_shape] if single else list(out_shape)
    size = sum(x.size * x.dtype.itemsize for x in list(inputs) + shapes)

    def body(*refs):
        kernel(*refs[:count], *refs[count + skip :])

    result = pl.pallas_call(
        body,
        **({} if grid is None else {"grid": grid}),
        out_shape=shapes,
        in_specs=(in_specs or [vmem()] * count) + [pl.BlockSpec(memory_space=pl.ANY)] * skip,
        out_specs=out_specs or [vmem()] * len(shapes),
        scratch_shapes=list(scratch),
        compiler_params=pltpu.CompilerParams(vmem_limit_bytes=VMEM_LIMIT),
        cost_estimate=pl.CostEstimate(flops=flops, bytes_accessed=size, transcendentals=0),
        name=name,
    )(*inputs, *after)
    return result[0] if single else result


def place(group):
    return lax.rem(lax.axis_index("ctx"), jnp.int32(group))


def swap(pieces, group, count):
    result = [pieces[0]]
    for k in range(1, group):
        perm = [(i, (i // group) * group + ((i % group) ^ k)) for i in range(count)]
        result.append(lax.ppermute(pieces[k], "ctx", perm))
    return result


def climb_up(array, group, count, steps=1):
    perm = [(i, i + group * steps) for i in range(count - group * steps)]
    return lax.ppermute(array, "ctx", perm)


def shape_of(shape, dtype):
    return jax.ShapeDtypeStruct(shape, dtype)


def tie(array, after):
    return pl.pallas_call(
        lambda *refs: None,
        out_shape=shape_of(array.shape, array.dtype),
        in_specs=[pl.BlockSpec(memory_space=pl.ANY)] * (1 + len(after)),
        out_specs=pl.BlockSpec(memory_space=pl.ANY),
        input_output_aliases={0: 0},
        compiler_params=pltpu.CompilerParams(vmem_limit_bytes=1024 * 1024),
        name="tie",
    )(array, *after)


def pack_kv(keys, values, group):
    length, width = keys.shape
    piece = width // group

    def kernel(k_ref, v_ref, *outs):
        mine = place(group)
        for k in range(group):
            columns = pl.ds(pl.multiple_of((mine ^ k) * piece, piece), piece)
            outs[k][0] = k_ref[:, columns]
            outs[k][1] = v_ref[:, columns]

    return launch(
        kernel,
        "pack_kv",
        [shape_of((2, length, piece), keys.dtype)] * group,
        keys,
        values,
        flops=5000000000,
        grid=(1,),
        in_specs=[pl.BlockSpec((length, width), lambda i: (0, 0))] * 2,
    )


def join(pieces, group):
    length, width = pieces[0].shape

    def kernel(*refs):
        out_ref, sems = refs[group:]
        mine = place(group)
        copies = []
        for k in range(group):
            columns = pl.ds(pl.multiple_of((mine ^ k) * width, width), width)
            copies.append(pltpu.make_async_copy(refs[k], out_ref.at[:, columns], sems.at[k]))
        for copy in copies:
            copy.start()
        for copy in copies:
            copy.wait()

    return launch(
        kernel,
        "join_heads",
        shape_of((length, width * group), pieces[0].dtype),
        *pieces,
        out_specs=[hbm()],
        scratch=[pltpu.SemaphoreType.DMA((group,))],
    )


def flash_chunk(q_refs, kv_ref, before, after, extended, own, length):
    group = len(q_refs)
    heads = q_refs[0].shape[1] // HD
    kv_heads = kv_ref.shape[3] // HD
    share = heads // kv_heads
    rows = group * length
    tile = min(rows, 2 * length)
    rate = LOG2E / math.sqrt(HD)
    for kv in range(kv_heads):
        lanes = slice(kv * HD, (kv + 1) * HD)
        keys = kv_ref[:, 0, :, lanes].reshape(rows, HD)
        extended[:, :HD] = kv_ref[:, 1, :, lanes].reshape(rows, HD)
        extended[:, HD:] = jnp.ones((rows, HD), BF16)
        tiles = [
            (h, start)
            for start in range(0, rows, tile)
            for h in range(kv * share, (kv + 1) * share)
        ]

        def score(h, start):
            parts = q_refs[start // length : (start + tile) // length]
            q = [ref[:length, h * HD : (h + 1) * HD] for ref in parts]
            q = jnp.concatenate(q, axis=0) if len(q) > 1 else q[0]
            scores = lax.dot_general(
                q, keys, (((1,), (1,)), ((), ())), preferred_element_type=F32
            )
            if own:
                flip = place(group) * length
                row = (lax.broadcasted_iota(jnp.int32, (tile, rows), 0) + start) ^ flip
                column = lax.broadcasted_iota(jnp.int32, (tile, rows), 1) ^ flip
                scores = jnp.where(column <= row, scores, -1e30)
            return scores

        ahead = score(*tiles[0])
        for n, (h, start) in enumerate(tiles):
            scores = ahead
            if n + 1 < len(tiles):
                ahead = score(*tiles[n + 1])
            here = slice(start, start + tile)
            top = jnp.max(scores, axis=1, keepdims=True)
            if not own:
                top_before = before[1][h, here]
                top = jnp.maximum(top_before[:, :1], top)
            weights = jnp.exp2((scores - top) * rate).astype(BF16)
            value = jnp.dot(weights, extended[...], preferred_element_type=F32)
            top = jnp.broadcast_to(top, (tile, LANES))
            if not own:
                keep = jnp.exp2((top_before - top) * rate)
                value = value + before[0][h, here] * jnp.concatenate([keep, keep], axis=1)
            yield h, start, tile, value
            if after is not None:
                after[0][h, here] = value
                after[1][h, here] = top


def finish_rows(out_refs, h, start, tile, value):
    length = out_refs[0].shape[0]
    result = (value[:, :HD] / value[:, HD:]).astype(BF16)
    for at in range(0, tile, length):
        out_refs[(start + at) // length][:, h * HD : (h + 1) * HD] = result[at : at + length]


def flash(q, length, own=None, state=(), chunks=(), final=False, base=1, after=()):
    group = len(q)
    heads = q[0].shape[1] // HD
    rows = group * length
    fixed = isinstance(base, int)
    has_own = own is not None
    specs = [] if fixed else [pl.BlockSpec(memory_space=pltpu.SMEM)]
    rest = list(q) + ([own] if has_own else []) + list(state) + list(chunks)
    specs = specs + [vmem()] * len(rest)

    def kernel(*refs):
        refs = list(refs)
        first = base if fixed else refs.pop(0)[0]
        q_refs = [refs.pop(0) for _ in range(group)]
        own_ref = refs.pop(0) if has_own else None
        held = None if has_own else (refs.pop(0), refs.pop(0))
        chunk_refs = [refs.pop(0) for _ in range(len(chunks))]
        extended = refs.pop()
        turn = lax.axis_index("ctx") // group
        outs = None if final else tuple(refs)
        if has_own:
            for done in flash_chunk(q_refs, own_ref, None, outs, extended, True, length):
                if final:
                    finish_rows(refs, *done)
            held = outs
        for number, ref in enumerate(chunk_refs):

            @pl.when(turn >= first + number)
            def _(ref=ref, held=held):
                for done in flash_chunk(q_refs, ref, held, outs, extended, False, length):
                    if final:
                        finish_rows(refs, *done)

            if not has_own and number == 0:

                @pl.when(turn < first)
                def _(held=held):
                    for h in range(heads):
                        if final:
                            finish_rows(refs, h, 0, rows, held[0][h])
                        else:
                            outs[0][h] = held[0][h]
                            outs[1][h] = held[1][h]

            held = outs

    if final:
        out_shape = [shape_of((length, heads * HD), BF16)] * group
    else:
        out_shape = [
            shape_of((heads, rows, HD + LANES), F32),
            shape_of((heads, rows, LANES), F32),
        ]
    parts = len(chunks) + has_own
    return launch(
        kernel,
        "flash",
        out_shape,
        *([] if fixed else [base]),
        *rest,
        after=after,
        in_specs=specs,
        flops=4 * heads * rows * rows * HD * parts,
        scratch=[pltpu.VMEM((rows, HD + LANES), BF16)],
    )


def widen(row, lanes):
    extra = lanes - row.shape[1]
    if not extra:
        return row
    return jnp.concatenate([row, jnp.zeros((row.shape[0], extra), row.dtype)], axis=1)


def project(x, step_weight, state_weight, after=()):
    length, channels = x.shape
    heads = step_weight.shape[1]

    def kernel(x_ref, step_ref, map_ref, out_ref):
        x = x_ref[...]
        out_ref[:, :heads] = jnp.dot(x, step_ref[...], preferred_element_type=F32)
        maps = lax.dot_general(
            x, map_ref[...], (((1,), (1,)), ((), ())), preferred_element_type=F32
        )
        out_ref[:, heads:] = widen(maps, LANES)

    return launch(
        kernel,
        "project",
        shape_of((length, heads + LANES), F32),
        x,
        step_weight,
        state_weight.T,
        after=after,
        flops=4 * length * channels * heads,
    )


def owners(heads):
    shape = (LANES, heads * DECAY_CHANNELS)
    head = lax.broadcasted_iota(jnp.int32, shape, 0)
    channel = lax.broadcasted_iota(jnp.int32, shape, 1)
    return (channel // DECAY_CHANNELS == head).astype(BF16)


def pack_row(row, rows):
    high = row.astype(BF16).astype(F32)
    rest = row - high
    middle = rest.astype(BF16).astype(F32)
    low = rest - middle
    return jnp.concatenate([high, middle, low, jnp.zeros((rows - 3, row.shape[1]), F32)], axis=0)


def unpack_row(rows):
    rows = rows.astype(F32)
    return rows[0:1] + rows[1:2] + rows[2:3]


def spread_total(rows, owner):
    wide = jnp.dot(rows, owner, preferred_element_type=F32)
    return wide[0:1] + wide[1:2] + wide[2:3]


def block_state(parts, bias, rate, x, q, states, group, after=()):
    length, channels = x.shape
    every = parts[0].shape[1] - LANES
    heads = bias.shape[1]
    width = channels // group
    columns = q.shape[1] // group
    bands = width // columns
    count = len(parts)

    def kernel(*refs):
        bias_ref, rate_ref, x_ref, q_ref = refs[count : count + 4]
        climb_ref, climb_t_ref, step_t_ref, maps_ref = refs[count + 4 : count + 8]
        outs = refs[count + 8 : count + 8 + group]
        held = refs[count + 8 + group]
        summed = refs[0][...]
        for ref in refs[1:count]:
            summed = summed + ref[...]
        shift = lax.rem(every - lax.axis_index("tp") * heads, jnp.int32(every))
        raw = pltpu.roll(summed[:, :every], shift, 1) + widen(bias_ref[...], every)
        step = jnp.maximum(raw, 0.0) + jnp.log1p(jnp.exp(-jnp.abs(raw)))
        log_decay = -widen(rate_ref[...], every) * step
        row = lax.broadcasted_iota(jnp.int32, (length, length), 0)
        column = lax.broadcasted_iota(jnp.int32, (length, length), 1)
        lower = (column <= row).astype(F32)
        climb = jnp.dot(
            lower, log_decay, precision=lax.Precision.HIGHEST, preferred_element_type=F32
        )
        maps = summed[:, every:]
        climb_ref[...] = climb * LOG2E
        maps_ref[...] = maps
        climb_t = climb.T
        step_t = step.T
        climb_t_ref[...] = climb_t[:heads] * LOG2E
        step_t_ref[...] = step_t[:heads]
        b_t = maps.T[:states]
        weight_t = jnp.exp(climb_t[:, length - 1 :] - climb_t) * step_t
        bundle = 4
        span = bundle * DECAY_CHANNELS
        owner = lax.broadcasted_iota(jnp.int32, (1, span), 1) // DECAY_CHANNELS
        for at in range(0, heads, bundle):
            feed = [b_t * weight_t[at + i : at + i + 1] for i in range(bundle)]
            feed = jnp.concatenate(feed, axis=0).astype(BF16)
            start = at * DECAY_CHANNELS
            product = jnp.dot(feed, x_ref[:, start : start + span], preferred_element_type=F32)
            state = product[:states]
            for i in range(1, bundle):
                state = jnp.where(owner == i, product[i * states : (i + 1) * states], state)
            piece, offset = divmod(start, width)
            band, offset = divmod(offset, columns)
            rows = slice(band * states, (band + 1) * states)
            held[piece, rows, offset : offset + span] = state.astype(BF16)
        totals = pack_row(climb[length - 1 :], states)
        for piece in range(group):
            at = piece * (heads // group)
            here = totals if not at else pltpu.roll(totals, every - at, 1)
            held[piece, bands * states :, :] = widen(here[:, :LANES], columns).astype(BF16)
        mine = place(group)
        for k in range(group):
            here = pl.ds(pl.multiple_of((mine ^ k) * columns, columns), columns)
            outs[k][:length] = q_ref[:, here]
            outs[k][length:] = held[mine ^ k]

    payload = shape_of((length + (bands + 1) * states, columns), BF16)
    result = launch(
        kernel,
        "block_state",
        [
            shape_of((length, every), F32),
            shape_of((heads, length), F32),
            shape_of((heads, length), F32),
            shape_of((length, LANES), F32),
        ]
        + [payload] * group,
        *parts,
        bias,
        rate,
        x,
        q,
        after=after,
        flops=32 * length * states * channels,
        scratch=[pltpu.VMEM((group, (bands + 1) * states, columns), BF16)],
    )
    return result[:4], result[4:]


def local_part(x, gate, climb, climb_t, step_t, maps, skip, states, after=()):
    length, channels = x.shape
    heads = channels // DECAY_CHANNELS

    def kernel(
        x_ref, gate_ref, climb_ref, climb_t_ref, step_t_ref, maps_ref, skip_ref, still_ref, scale_ref
    ):
        maps = maps_ref[...]
        inner = lax.dot_general(
            maps[:, states : 2 * states],
            maps[:, :states],
            (((1,), (1,)), ((), ())),
            precision=lax.Precision.HIGHEST,
            preferred_element_type=F32,
        )
        row = lax.broadcasted_iota(jnp.int32, (length, length), 0)
        column = lax.broadcasted_iota(jnp.int32, (length, length), 1)
        inner = jnp.where(column <= row, inner, 0.0)
        left = lax.broadcasted_iota(jnp.int32, (length, LANES), 1) < DECAY_CHANNELS

        for j in range(0, heads, 2):
            columns = slice(j * DECAY_CHANNELS, j * DECAY_CHANNELS + LANES)
            x = x_ref[:, columns]
            wide = [jnp.broadcast_to(climb_ref[:, i : i + 1], (length, length)) for i in (j, j + 1)]
            mixed = []
            for i in (j, j + 1):
                fall = jnp.minimum(wide[i - j] - climb_t_ref[i : i + 1], 0.0)
                mixed.append((inner * jnp.exp2(fall) * step_t_ref[i : i + 1]).astype(BF16))
            zero = jnp.zeros_like(x)
            feeds = jnp.concatenate([jnp.where(left, x, zero), jnp.where(left, zero, x)], axis=0)
            local = jnp.dot(jnp.concatenate(mixed, axis=1), feeds, preferred_element_type=F32)
            gain = jnp.where(left[:1], skip_ref[:, j : j + 1], skip_ref[:, j + 1 : j + 2])
            grown = jnp.exp2(jnp.where(left, wide[0], wide[1]))
            gate = gate_ref[:, columns].astype(F32)
            half = 0.5 * gate
            silu = half + half * jnp.tanh(half)
            still_ref[:, columns] = (local + gain * x.astype(F32)) * silu
            scale_ref[:, columns] = grown * silu

    return launch(
        kernel,
        "local_part",
        [shape_of((length, channels), F32)] * 2,
        x,
        gate,
        climb,
        climb_t,
        step_t,
        maps,
        skip,
        after=after,
        flops=4 * length * length * channels,
    )


def gather_blocks(group, states, length, refs, held):
    mine = place(group)
    for k in range(group):
        held[mine ^ k] = refs[k][length:]


def block_of(held, b, states, columns, width):
    bands = width // columns
    rows = [held[b, i * states : (i + 1) * states] for i in range(bands)]
    state = jnp.concatenate(rows, axis=1) if bands > 1 else rows[0]
    return state.astype(F32), held[b, bands * states :, :LANES]


def group_total(payloads, length, states, width, after=()):
    group = len(payloads)
    rows, columns = payloads[0].shape
    heads = width // DECAY_CHANNELS

    def kernel(*refs):
        out_ref, held = refs[group:]
        gather_blocks(group, states, length, refs[:group], held)
        owner = owners(heads)
        state, packed = block_of(held, 0, states, columns, width)
        total = unpack_row(packed)
        for b in range(1, group):
            more, packed = block_of(held, b, states, columns, width)
            state = jnp.exp(spread_total(packed, owner)) * state + more
            total = total + unpack_row(packed)
        out_ref[:, :width] = state.astype(BF16)
        out_ref[:, width:] = pack_row(total, states).astype(BF16)

    return launch(
        kernel,
        "group_total",
        shape_of((states, width + LANES), BF16),
        *payloads,
        after=after,
        scratch=[pltpu.VMEM((group, rows - length, columns), BF16)],
    )


def entering_states(payloads, earlier, length, states, width, after=()):
    group = len(payloads)
    rows, columns = payloads[0].shape
    heads = width // DECAY_CHANNELS
    count = len(earlier)

    def kernel(*refs):
        earlier_refs = refs[group : group + count]
        outs = refs[group + count : 2 * group + count]
        held, entering = refs[2 * group + count :]
        gather_blocks(group, states, length, refs[:group], held)
        owner = owners(heads)
        state = jnp.zeros((states, width), F32)
        for ref in reversed(earlier_refs):
            state = jnp.exp(spread_total(ref[:, width:], owner)) * state
            state = state + ref[:, :width].astype(F32)
        for b in range(group):
            entering[b] = state
            if b < group - 1:
                more, packed = block_of(held, b, states, columns, width)
                state = jnp.exp(spread_total(packed, owner)) * state + more
        mine = place(group)
        for k in range(group):
            outs[k][...] = entering[mine ^ k]

    return launch(
        kernel,
        "entering_states",
        [shape_of((states, width), F32)] * group,
        *payloads,
        *earlier,
        after=after,
        scratch=[
            pltpu.VMEM((group, rows - length, columns), BF16),
            pltpu.VMEM((group, states, width), F32),
        ],
    )


def carried_part(maps, still, scale, entering, states, after=()):
    length, channels = still.shape
    group = len(entering)
    width = channels // group
    span = min(width, 512)

    def kernel(maps_ref, still_ref, scale_ref, *refs):
        gated_ref, square_ref, held = refs[group:]
        mine = place(group)
        for k in range(group):
            held[mine ^ k] = refs[k][...]
        c = maps_ref[:, states : 2 * states]
        c_high = c.astype(BF16)
        c_low = (c - c_high.astype(F32)).astype(BF16)
        c = jnp.concatenate([c_high, c_low, c_high], axis=1)
        folded = jnp.zeros(square_ref.shape, F32)
        for at in range(0, channels, span):
            piece, offset = divmod(at, width)
            state = held[piece, :, offset : offset + span]
            high = state.astype(BF16)
            low = (state - high.astype(F32)).astype(BF16)
            carried = jnp.dot(
                c, jnp.concatenate([high, high, low], axis=0), preferred_element_type=F32
            )
            columns = slice(at, at + span)
            gated = still_ref[:, columns] + scale_ref[:, columns] * carried
            gated_ref[:, columns] = gated
            square = gated * gated
            for lane in range(0, span, LANES):
                folded = folded + square[:, lane : lane + LANES]
        square_ref[...] = folded

    return launch(
        kernel,
        "carried_part",
        [shape_of((length, channels), F32), shape_of((length, LANES), F32)],
        maps,
        still,
        scale,
        *entering,
        after=after,
        flops=6 * length * states * channels,
        scratch=[pltpu.VMEM((group, states, width), F32)],
    )


def norm(gated, gain, squares, every):
    length, channels = gated.shape
    count = len(squares)

    def kernel(gated_ref, gain_ref, *refs):
        out_ref = refs[count]
        square = refs[0][...]
        for ref in refs[1:count]:
            square = square + ref[...]
        mean = jnp.sum(square, axis=1, keepdims=True) / every
        factor = jnp.broadcast_to(lax.rsqrt(mean + 1e-05), square.shape)
        for at in range(0, channels, LANES):
            columns = slice(at, at + LANES)
            out_ref[:, columns] = (gated_ref[:, columns] * factor * gain_ref[:, columns]).astype(BF16)

    return launch(
        kernel, "norm", shape_of((length, channels), BF16), gated, gain, *squares
    )


def shared_parts(part):
    if lax.axis_size("tp") == 2:
        return [part, lax.ppermute(part, "tp", [(0, 1), (1, 0)])]
    return [lax.psum(part, "tp")]


def earlier_states(total, group, turns, count, states, width):
    if turns <= UNROLL:
        return [climb_up(total, group, count, steps) for steps in range(1, turns)]
    heads = width // DECAY_CHANNELS

    def one(_, carry):
        travelling, summed, ahead = carry
        travelling = climb_up(travelling, group, count)
        summed = summed + jnp.exp(ahead) * travelling[:, :width].astype(F32)
        more = unpack_row(travelling[:, width : width + heads])
        return travelling, summed, ahead + jnp.repeat(more, DECAY_CHANNELS, axis=1)

    start = (total, jnp.zeros((states, width), F32), jnp.zeros((1, width), F32))
    _, summed, _ = lax.fori_loop(1, turns, one, start)
    return [jnp.concatenate([summed.astype(BF16), jnp.zeros((states, LANES), BF16)], axis=1)]


def per_device(
    queries,
    keys,
    values,
    mixer_input,
    gate,
    step_weight,
    state_weight,
    step_bias,
    decay_rate,
    skip_gain,
    norm_gain,
):
    count = lax.axis_size("ctx")
    length = queries.shape[0]
    channels = mixer_input.shape[1]
    states = state_weight.shape[1] // 2
    group = math.gcd(keys.shape[1] // HD, count)
    turns = count // group
    width = channels // group

    packed = pack_kv(keys, values, group)
    parts = shared_parts(project(mixer_input, step_weight, state_weight, after=packed[:1]))
    blocks = swap(packed, group, count)
    (climb, climb_t, step_t, maps), payloads = block_state(
        parts, step_bias[None], decay_rate[None], mixer_input, queries, states, group
    )
    own = jnp.stack([tie(blocks[0], [climb])] + blocks[1:])
    sent = payloads[:1]
    payloads = swap(payloads, group, count)
    still, scale = local_part(
        mixer_input, gate, climb, climb_t, step_t, maps, skip_gain[None], states
    )
    ring = 1 < turns <= UNROLL
    arrived, ready = [], []
    if ring:
        arrived.append(climb_up(own, group, count))
    if ring and turns > 2:
        arrived[0] = tie(arrived[0], sent)
        ready = [arrived[0]]
        arrived.append(climb_up(arrived[0], group, count))
    total = group_total(payloads, length, states, width, after=[still] + ready)
    earlier = earlier_states(total, group, turns, count, states, width)
    state = flash(payloads, length, own=own, chunks=arrived[:-1][:1], after=[total])
    if ring and turns > 3:
        arrived[1] = tie(arrived[1], [state[1]] + earlier)
        ready = [arrived[1]]
        arrived.append(climb_up(arrived[1], group, count))
        for step in range(4, turns):
            arrived.append(climb_up(arrived[-1], group, count))
    entering = entering_states(payloads, earlier, length, states, width, after=ready)
    if ring and turns > 3:
        state = flash(
            payloads, length, state=state, chunks=arrived[1:-1], base=2, after=entering[:1]
        )
    entering = swap(entering, group, count)
    if turns > 1 and not ring:

        def one(step, carry):
            chunk, state = carry
            chunk = climb_up(chunk, group, count)
            state = flash(payloads, length, state=state, chunks=[chunk], base=jnp.reshape(step, (1,)))
            return chunk, tuple(state)

        chunk, state = lax.fori_loop(1, turns - 1, one, (own, tuple(state)))
        arrived.append(climb_up(chunk, group, count))
    gated, square = carried_part(maps, still, scale, entering, states)
    mamba_out = norm(
        gated, norm_gain[None], shared_parts(square), channels * lax.axis_size("tp")
    )
    if turns == 1:
        outs = flash(payloads, length, own=own, final=True)
    else:
        outs = flash(
            payloads, length, state=state, chunks=arrived[-1:], final=True, base=turns - 1
        )
    return join(swap(outs, group, count), group), mamba_out


def solution(mesh):
    return jax.shard_map(
        per_device,
        mesh=mesh,
        in_specs=(
            P("ctx", "tp"),
            P("ctx", "tp"),
            P("ctx", "tp"),
            P("ctx", "tp"),
            P("ctx", "tp"),
            P("tp", None),
            P("tp", None),
            P("tp"),
            P("tp"),
            P("tp"),
            P("tp"),
        ),
        out_specs=(P("ctx", "tp"), P("ctx", "tp")),
        check_vma=False,
    )
```

```python
import functools
import math

import jax
import jax.numpy as jnp
from jax import lax
from jax.experimental import pallas as pl
from jax.experimental.pallas import tpu as pltpu
from jax.sharding import PartitionSpec as P

HD = 128
DECAY_CHANNELS = 64
SCAN_TOKENS = 128
LANES = 128
UNROLL = 8
LOG2E = math.log2(math.e)
VMEM_LIMIT = 14 * 1024 * 1024

F32 = jnp.float32
BF16 = jnp.bfloat16


def vmem():
    return pl.BlockSpec(memory_space=pltpu.VMEM)


def hbm():
    return pl.BlockSpec(memory_space=pltpu.HBM)


def launch(kernel, name, out_shape, *inputs, after=(), flops=0, scratch=(), in_specs=None, out_specs=None, grid=None):
    count, skip = len(inputs), len(after)
    single = isinstance(out_shape, jax.ShapeDtypeStruct)
    shapes = [out_shape] if single else list(out_shape)
    size = sum(x.size * x.dtype.itemsize for x in list(inputs) + shapes)

    def body(*refs):
        kernel(*refs[:count], *refs[count + skip :])

    result = pl.pallas_call(
        body,
        **({} if grid is None else {"grid": grid}),
        out_shape=shapes,
        in_specs=(in_specs or [vmem()] * count) + [pl.BlockSpec(memory_space=pl.ANY)] * skip,
        out_specs=out_specs or [vmem()] * len(shapes),
        scratch_shapes=list(scratch),
        compiler_params=pltpu.CompilerParams(vmem_limit_bytes=VMEM_LIMIT),
        cost_estimate=pl.CostEstimate(flops=flops, bytes_accessed=size, transcendentals=0),
        name=name,
    )(*inputs, *after)
    return result[0] if single else result


def place(group):
    return lax.rem(lax.axis_index("ctx"), jnp.int32(group))


def swap(pieces, group, count):
    result = list(pieces)
    for k in reversed(range(1, group)):
        perm = [(i, (i // group) * group + ((i % group) ^ k)) for i in range(count)]
        result[k] = lax.ppermute(pieces[k], "ctx", perm)
    return result


def climb_up(array, group, count, steps=1):
    perm = [(i, i + group * steps) for i in range(count - group * steps)]
    return lax.ppermute(array, "ctx", perm)


def shape_of(shape, dtype):
    return jax.ShapeDtypeStruct(shape, dtype)


def tie(array, after):
    return pl.pallas_call(
        lambda *refs: None,
        out_shape=shape_of(array.shape, array.dtype),
        in_specs=[pl.BlockSpec(memory_space=pl.ANY)] * (1 + len(after)),
        out_specs=pl.BlockSpec(memory_space=pl.ANY),
        input_output_aliases={0: 0},
        compiler_params=pltpu.CompilerParams(vmem_limit_bytes=1024 * 1024),
        name="tie",
    )(array, *after)


def pack_kv(keys, values, group):
    length, width = keys.shape
    piece = width // group

    def kernel(k_ref, v_ref, *outs):
        mine = place(group)
        for k in range(group):
            columns = pl.ds(pl.multiple_of((mine ^ k) * piece, piece), piece)
            outs[k][0] = k_ref[:, columns]
            outs[k][1] = v_ref[:, columns]

    return launch(
        kernel,
        "pack_kv",
        [shape_of((2, length, piece), keys.dtype)] * group,
        keys,
        values,
        flops=5000000000,
        grid=(1,),
        in_specs=[pl.BlockSpec((length, width), lambda i: (0, 0))] * 2,
    )


def join(pieces, group):
    length, width = pieces[0].shape

    def kernel(*refs):
        out_ref, sems = refs[group:]
        mine = place(group)
        copies = []
        for k in range(group):
            columns = pl.ds(pl.multiple_of((mine ^ k) * width, width), width)
            copies.append(
                pltpu.make_async_copy(refs[group - 1 - k], out_ref.at[:, columns], sems.at[k])
            )
        for copy in copies:
            copy.start()
        for copy in copies:
            copy.wait()

    return launch(
        kernel,
        "join_heads",
        shape_of((length, width * group), pieces[0].dtype),
        *reversed(pieces),
        out_specs=[hbm()],
        scratch=[pltpu.SemaphoreType.DMA((group,))],
    )


def flash_chunk(q_refs, kv_ref, before, after, extended, own, length):
    group = len(q_refs)
    heads = q_refs[0].shape[1] // HD
    kv_heads = kv_ref.shape[3] // HD
    share = heads // kv_heads
    rows = group * length
    tile = min(rows, 2 * length)
    rate = LOG2E / math.sqrt(HD)
    for kv in range(kv_heads):
        lanes = slice(kv * HD, (kv + 1) * HD)
        keys = kv_ref[:, 0, :, lanes].reshape(rows, HD)
        extended[:, :HD] = kv_ref[:, 1, :, lanes].reshape(rows, HD)
        extended[:, HD:] = jnp.ones((rows, HD), BF16)
        tiles = [
            (h, start)
            for start in range(0, rows, tile)
            for h in range(kv * share, (kv + 1) * share)
        ]

        def score(h, start):
            parts = q_refs[start // length : (start + tile) // length]
            q = [ref[:length, h * HD : (h + 1) * HD] for ref in parts]
            q = jnp.concatenate(q, axis=0) if len(q) > 1 else q[0]
            scores = lax.dot_general(
                q, keys, (((1,), (1,)), ((), ())), preferred_element_type=F32
            )
            if own:
                flip = place(group) * length
                row = (lax.broadcasted_iota(jnp.int32, (tile, rows), 0) + start) ^ flip
                column = lax.broadcasted_iota(jnp.int32, (tile, rows), 1) ^ flip
                scores = jnp.where(column <= row, scores, -1e30)
            return scores

        ahead = score(*tiles[0])
        for n, (h, start) in enumerate(tiles):
            scores = ahead
            if n + 1 < len(tiles):
                ahead = score(*tiles[n + 1])
            here = slice(start, start + tile)
            top = jnp.max(scores, axis=1, keepdims=True)
            if not own:
                top_before = before[1][h, here]
                top = jnp.maximum(top_before[:, :1], top)
            weights = jnp.exp2((scores - top) * rate).astype(BF16)
            value = jnp.dot(weights, extended[...], preferred_element_type=F32)
            top = jnp.broadcast_to(top, (tile, LANES))
            if not own:
                keep = jnp.exp2((top_before - top) * rate)
                value = value + before[0][h, here] * jnp.concatenate([keep, keep], axis=1)
            yield h, start, tile, value
            if after is not None:
                after[0][h, here] = value
                after[1][h, here] = top


def finish_rows(out_refs, h, start, tile, value):
    length = out_refs[0].shape[0]
    result = (value[:, :HD] / value[:, HD:]).astype(BF16)
    for at in range(0, tile, length):
        out_refs[(start + at) // length][:, h * HD : (h + 1) * HD] = result[at : at + length]


def flash(q, length, own=None, state=(), chunks=(), final=False, base=1, after=()):
    group = len(q)
    heads = q[0].shape[1] // HD
    rows = group * length
    fixed = isinstance(base, int)
    has_own = own is not None
    specs = [] if fixed else [pl.BlockSpec(memory_space=pltpu.SMEM)]
    rest = list(q) + ([own] if has_own else []) + list(state) + list(chunks)
    specs = specs + [vmem()] * len(rest)

    def kernel(*refs):
        refs = list(refs)
        first = base if fixed else refs.pop(0)[0]
        q_refs = [refs.pop(0) for _ in range(group)]
        own_ref = refs.pop(0) if has_own else None
        held = None if has_own else (refs.pop(0), refs.pop(0))
        chunk_refs = [refs.pop(0) for _ in range(len(chunks))]
        extended = refs.pop()
        turn = lax.axis_index("ctx") // group
        outs = None if final else tuple(refs)
        if has_own:
            for done in flash_chunk(q_refs, own_ref, None, outs, extended, True, length):
                if final:
                    finish_rows(refs, *done)
            held = outs
        for number, ref in enumerate(chunk_refs):

            @pl.when(turn >= first + number)
            def _(ref=ref, held=held):
                for done in flash_chunk(q_refs, ref, held, outs, extended, False, length):
                    if final:
                        finish_rows(refs, *done)

            if not has_own and number == 0:

                @pl.when(turn < first)
                def _(held=held):
                    for h in range(heads):
                        if final:
                            finish_rows(refs, h, 0, rows, held[0][h])
                        else:
                            outs[0][h] = held[0][h]
                            outs[1][h] = held[1][h]

            held = outs

    if final:
        out_shape = [shape_of((length, heads * HD), BF16)] * group
    else:
        out_shape = [
            shape_of((heads, rows, HD + LANES), F32),
            shape_of((heads, rows, LANES), F32),
        ]
    parts = len(chunks) + has_own
    return launch(
        kernel,
        "flash",
        out_shape,
        *([] if fixed else [base]),
        *rest,
        after=after,
        in_specs=specs,
        flops=4 * heads * rows * rows * HD * parts,
        scratch=[pltpu.VMEM((rows, HD + LANES), BF16)],
    )


def widen(row, lanes):
    extra = lanes - row.shape[1]
    if not extra:
        return row
    return jnp.concatenate([row, jnp.zeros((row.shape[0], extra), row.dtype)], axis=1)


def project(x, step_weight, state_weight, after=()):
    length, channels = x.shape
    heads = step_weight.shape[1]

    def kernel(x_ref, step_ref, map_ref, out_ref):
        x = x_ref[...]
        out_ref[:, :heads] = jnp.dot(x, step_ref[...], preferred_element_type=F32)
        maps = lax.dot_general(
            x, map_ref[...], (((1,), (1,)), ((), ())), preferred_element_type=F32
        )
        out_ref[:, heads:] = widen(maps, LANES)

    return launch(
        kernel,
        "project",
        shape_of((length, heads + LANES), F32),
        x,
        step_weight,
        state_weight.T,
        after=after,
        flops=4 * length * channels * heads,
    )


def owners(heads):
    shape = (LANES, heads * DECAY_CHANNELS)
    head = lax.broadcasted_iota(jnp.int32, shape, 0)
    channel = lax.broadcasted_iota(jnp.int32, shape, 1)
    return (channel // DECAY_CHANNELS == head).astype(BF16)


def pack_row(row, rows):
    high = row.astype(BF16).astype(F32)
    rest = row - high
    middle = rest.astype(BF16).astype(F32)
    low = rest - middle
    return jnp.concatenate([high, middle, low, jnp.zeros((rows - 3, row.shape[1]), F32)], axis=0)


def unpack_row(rows):
    rows = rows.astype(F32)
    return rows[0:1] + rows[1:2] + rows[2:3]


def spread_total(rows, owner):
    wide = jnp.dot(rows, owner, preferred_element_type=F32)
    return wide[0:1] + wide[1:2] + wide[2:3]


def block_state(parts, bias, rate, x, q, states, group, after=()):
    length, channels = x.shape
    every = parts[0].shape[1] - LANES
    heads = bias.shape[1]
    width = channels // group
    columns = q.shape[1] // group
    bands = width // columns
    count = len(parts)

    def kernel(*refs):
        bias_ref, rate_ref, x_ref, q_ref = refs[count : count + 4]
        climb_ref, climb_t_ref, step_t_ref, maps_ref = refs[count + 4 : count + 8]
        outs = refs[count + 8 : count + 8 + group]
        held = refs[count + 8 + group]
        summed = refs[0][...]
        for ref in refs[1:count]:
            summed = summed + ref[...]
        shift = lax.rem(every - lax.axis_index("tp") * heads, jnp.int32(every))
        raw = pltpu.roll(summed[:, :every], shift, 1) + widen(bias_ref[...], every)
        step = jnp.maximum(raw, 0.0) + jnp.log1p(jnp.exp(-jnp.abs(raw)))
        log_decay = -widen(rate_ref[...], every) * step
        row = lax.broadcasted_iota(jnp.int32, (length, length), 0)
        column = lax.broadcasted_iota(jnp.int32, (length, length), 1)
        lower = (column <= row).astype(F32)
        climb = jnp.dot(
            lower, log_decay, precision=lax.Precision.HIGHEST, preferred_element_type=F32
        )
        maps = summed[:, every:]
        climb_ref[...] = climb * LOG2E
        maps_ref[...] = maps
        climb_t = climb.T
        step_t = step.T
        climb_t_ref[...] = climb_t[:heads] * LOG2E
        step_t_ref[...] = step_t[:heads]
        b_t = maps.T[:states]
        weight_t = jnp.exp(climb_t[:, length - 1 :] - climb_t) * step_t
        bundle = 4
        span = bundle * DECAY_CHANNELS
        owner = lax.broadcasted_iota(jnp.int32, (1, span), 1) // DECAY_CHANNELS
        for at in range(0, heads, bundle):
            feed = [b_t * weight_t[at + i : at + i + 1] for i in range(bundle)]
            feed = jnp.concatenate(feed, axis=0).astype(BF16)
            start = at * DECAY_CHANNELS
            product = jnp.dot(feed, x_ref[:, start : start + span], preferred_element_type=F32)
            state = product[:states]
            for i in range(1, bundle):
                state = jnp.where(owner == i, product[i * states : (i + 1) * states], state)
            piece, offset = divmod(start, width)
            band, offset = divmod(offset, columns)
            rows = slice(band * states, (band + 1) * states)
            held[piece, rows, offset : offset + span] = state.astype(BF16)
        totals = pack_row(climb[length - 1 :], states)
        for piece in range(group):
            at = piece * (heads // group)
            here = totals if not at else pltpu.roll(totals, every - at, 1)
            held[piece, bands * states :, :] = widen(here[:, :LANES], columns).astype(BF16)
        mine = place(group)
        for k in range(group):
            here = pl.ds(pl.multiple_of((mine ^ k) * columns, columns), columns)
            outs[k][:length] = q_ref[:, here]
            outs[k][length:] = held[mine ^ k]

    payload = shape_of((length + (bands + 1) * states, columns), BF16)
    result = launch(
        kernel,
        "block_state",
        [
            shape_of((length, every), F32),
            shape_of((heads, length), F32),
            shape_of((heads, length), F32),
            shape_of((length, LANES), F32),
        ]
        + [payload] * group,
        *parts,
        bias,
        rate,
        x,
        q,
        after=after,
        flops=32 * length * states * channels,
        scratch=[pltpu.VMEM((group, (bands + 1) * states, columns), BF16)],
    )
    return result[:4], result[4:]


def local_part(x, gate, climb, climb_t, step_t, maps, skip, states, after=()):
    length, channels = x.shape
    heads = channels // DECAY_CHANNELS

    def kernel(
        x_ref, gate_ref, climb_ref, climb_t_ref, step_t_ref, maps_ref, skip_ref, still_ref, scale_ref
    ):
        maps = maps_ref[...]
        inner = lax.dot_general(
            maps[:, states : 2 * states],
            maps[:, :states],
            (((1,), (1,)), ((), ())),
            precision=lax.Precision.HIGHEST,
            preferred_element_type=F32,
        )
        row = lax.broadcasted_iota(jnp.int32, (length, length), 0)
        column = lax.broadcasted_iota(jnp.int32, (length, length), 1)
        inner = jnp.where(column <= row, inner, 0.0)
        left = lax.broadcasted_iota(jnp.int32, (length, LANES), 1) < DECAY_CHANNELS

        for j in range(0, heads, 2):
            columns = slice(j * DECAY_CHANNELS, j * DECAY_CHANNELS + LANES)
            x = x_ref[:, columns]
            wide = [jnp.broadcast_to(climb_ref[:, i : i + 1], (length, length)) for i in (j, j + 1)]
            mixed = []
            for i in (j, j + 1):
                fall = jnp.minimum(wide[i - j] - climb_t_ref[i : i + 1], 0.0)
                mixed.append((inner * jnp.exp2(fall) * step_t_ref[i : i + 1]).astype(BF16))
            zero = jnp.zeros_like(x)
            feeds = jnp.concatenate([jnp.where(left, x, zero), jnp.where(left, zero, x)], axis=0)
            local = jnp.dot(jnp.concatenate(mixed, axis=1), feeds, preferred_element_type=F32)
            gain = jnp.where(left[:1], skip_ref[:, j : j + 1], skip_ref[:, j + 1 : j + 2])
            grown = jnp.exp2(jnp.where(left, wide[0], wide[1]))
            gate = gate_ref[:, columns].astype(F32)
            half = 0.5 * gate
            silu = half + half * jnp.tanh(half)
            still_ref[:, columns] = (local + gain * x.astype(F32)) * silu
            scale_ref[:, columns] = grown * silu

    return launch(
        kernel,
        "local_part",
        [shape_of((length, channels), F32)] * 2,
        x,
        gate,
        climb,
        climb_t,
        step_t,
        maps,
        skip,
        after=after,
        flops=4 * length * length * channels,
    )


def gather_blocks(group, states, length, refs, held):
    mine = place(group)
    for k in range(group):
        held[mine ^ k] = refs[k][length:]


def block_of(held, b, states, columns, width):
    bands = width // columns
    rows = [held[b, i * states : (i + 1) * states] for i in range(bands)]
    state = jnp.concatenate(rows, axis=1) if bands > 1 else rows[0]
    return state.astype(F32), held[b, bands * states :, :LANES]


def group_total(payloads, length, states, width, after=()):
    group = len(payloads)
    rows, columns = payloads[0].shape
    heads = width // DECAY_CHANNELS

    def kernel(*refs):
        out_ref, held = refs[group:]
        gather_blocks(group, states, length, refs[:group], held)
        owner = owners(heads)
        state, packed = block_of(held, 0, states, columns, width)
        total = unpack_row(packed)
        for b in range(1, group):
            more, packed = block_of(held, b, states, columns, width)
            state = jnp.exp(spread_total(packed, owner)) * state + more
            total = total + unpack_row(packed)
        out_ref[:, :width] = state.astype(BF16)
        out_ref[:, width:] = pack_row(total, states).astype(BF16)

    return launch(
        kernel,
        "group_total",
        shape_of((states, width + LANES), BF16),
        *payloads,
        after=after,
        scratch=[pltpu.VMEM((group, rows - length, columns), BF16)],
    )


def entering_states(payloads, earlier, length, states, width, after=()):
    group = len(payloads)
    rows, columns = payloads[0].shape
    heads = width // DECAY_CHANNELS
    count = len(earlier)

    def kernel(*refs):
        earlier_refs = refs[group : group + count]
        outs = refs[group + count : 2 * group + count]
        held, entering = refs[2 * group + count :]
        gather_blocks(group, states, length, refs[:group], held)
        owner = owners(heads)
        state = jnp.zeros((states, width), F32)
        for ref in reversed(earlier_refs):
            state = jnp.exp(spread_total(ref[:, width:], owner)) * state
            state = state + ref[:, :width].astype(F32)
        for b in range(group):
            entering[b] = state
            if b < group - 1:
                more, packed = block_of(held, b, states, columns, width)
                state = jnp.exp(spread_total(packed, owner)) * state + more
        mine = place(group)
        for k in range(group):
            outs[k][...] = entering[mine ^ k]

    return launch(
        kernel,
        "entering_states",
        [shape_of((states, width), F32)] * group,
        *payloads,
        *earlier,
        after=after,
        scratch=[
            pltpu.VMEM((group, rows - length, columns), BF16),
            pltpu.VMEM((group, states, width), F32),
        ],
    )


def carried_part(maps, still, scale, entering, states, after=()):
    length, channels = still.shape
    group = len(entering)
    width = channels // group
    span = min(width, 512)

    def kernel(maps_ref, still_ref, scale_ref, *refs):
        gated_ref, square_ref, held = refs[group:]
        mine = place(group)
        for k in range(group):
            held[mine ^ k] = refs[k][...]
        c = maps_ref[:, states : 2 * states]
        c_high = c.astype(BF16)
        c_low = (c - c_high.astype(F32)).astype(BF16)
        c = jnp.concatenate([c_high, c_low, c_high], axis=1)
        folded = jnp.zeros(square_ref.shape, F32)
        for at in range(0, channels, span):
            piece, offset = divmod(at, width)
            state = held[piece, :, offset : offset + span]
            high = state.astype(BF16)
            low = (state - high.astype(F32)).astype(BF16)
            carried = jnp.dot(
                c, jnp.concatenate([high, high, low], axis=0), preferred_element_type=F32
            )
            columns = slice(at, at + span)
            gated = still_ref[:, columns] + scale_ref[:, columns] * carried
            gated_ref[:, columns] = gated
            square = gated * gated
            for lane in range(0, span, LANES):
                folded = folded + square[:, lane : lane + LANES]
        square_ref[...] = folded

    return launch(
        kernel,
        "carried_part",
        [shape_of((length, channels), F32), shape_of((length, LANES), F32)],
        maps,
        still,
        scale,
        *entering,
        after=after,
        flops=6 * length * states * channels,
        scratch=[pltpu.VMEM((group, states, width), F32)],
    )


def norm(gated, gain, squares, every):
    length, channels = gated.shape
    count = len(squares)

    def kernel(gated_ref, gain_ref, *refs):
        out_ref = refs[count]
        square = refs[0][...]
        for ref in refs[1:count]:
            square = square + ref[...]
        mean = jnp.sum(square, axis=1, keepdims=True) / every
        factor = jnp.broadcast_to(lax.rsqrt(mean + 1e-05), square.shape)
        for at in range(0, channels, LANES):
            columns = slice(at, at + LANES)
            out_ref[:, columns] = (gated_ref[:, columns] * factor * gain_ref[:, columns]).astype(BF16)

    return launch(
        kernel, "norm", shape_of((length, channels), BF16), gated, gain, *squares
    )


def shared_parts(part):
    if lax.axis_size("tp") == 2:
        return [part, lax.ppermute(part, "tp", [(0, 1), (1, 0)])]
    return [lax.psum(part, "tp")]


def earlier_states(total, group, turns, count, states, width):
    if turns <= UNROLL:
        return [climb_up(total, group, count, steps) for steps in range(1, turns)]
    heads = width // DECAY_CHANNELS

    def one(_, carry):
        travelling, summed, ahead = carry
        travelling = climb_up(travelling, group, count)
        summed = summed + jnp.exp(ahead) * travelling[:, :width].astype(F32)
        more = unpack_row(travelling[:, width : width + heads])
        return travelling, summed, ahead + jnp.repeat(more, DECAY_CHANNELS, axis=1)

    start = (total, jnp.zeros((states, width), F32), jnp.zeros((1, width), F32))
    _, summed, _ = lax.fori_loop(1, turns, one, start)
    return [jnp.concatenate([summed.astype(BF16), jnp.zeros((states, LANES), BF16)], axis=1)]


def per_device(
    queries,
    keys,
    values,
    mixer_input,
    gate,
    step_weight,
    state_weight,
    step_bias,
    decay_rate,
    skip_gain,
    norm_gain,
):
    count = lax.axis_size("ctx")
    length = queries.shape[0]
    channels = mixer_input.shape[1]
    states = state_weight.shape[1] // 2
    group = math.gcd(keys.shape[1] // HD, count)
    turns = count // group
    width = channels // group

    packed = pack_kv(keys, values, group)
    parts = shared_parts(project(mixer_input, step_weight, state_weight, after=packed[:1]))
    blocks = swap(packed, group, count)
    (climb, climb_t, step_t, maps), payloads = block_state(
        parts, step_bias[None], decay_rate[None], mixer_input, queries, states, group
    )
    still, scale = local_part(
        mixer_input, gate, climb, climb_t, step_t, maps, skip_gain[None], states
    )
    own = jnp.stack([tie(blocks[0], [still])] + blocks[1:])
    sent = payloads[:1]
    payloads = swap(payloads, group, count)
    ring = 1 < turns <= UNROLL
    arrived, ready = [], []
    if ring:
        arrived.append(climb_up(own, group, count))
    if ring and turns > 2:
        arrived[0] = tie(arrived[0], sent)
        ready = [arrived[0]]
        arrived.append(climb_up(arrived[0], group, count))
    total = group_total(payloads, length, states, width, after=ready)
    earlier = earlier_states(total, group, turns, count, states, width)
    state = flash(payloads, length, own=own, chunks=arrived[:-1][:1], after=[total])
    if ring and turns > 3:
        arrived[1] = tie(arrived[1], [state[1]] + earlier[:1] + earlier[:0:-1])
        ready = [arrived[1]]
        arrived.append(climb_up(arrived[1], group, count))
        for step in range(4, turns):
            arrived.append(climb_up(arrived[-1], group, count))
    entering = entering_states(payloads, earlier, length, states, width, after=ready)
    if ring and turns > 3:
        state = flash(
            payloads, length, state=state, chunks=arrived[1:-1], base=2, after=entering[:1]
        )
    entering = swap(entering, group, count)
    if turns > 1 and not ring:

        def one(step, carry):
            chunk, state = carry
            chunk = climb_up(chunk, group, count)
            state = flash(payloads, length, state=state, chunks=[chunk], base=jnp.reshape(step, (1,)))
            return chunk, tuple(state)

        chunk, state = lax.fori_loop(1, turns - 1, one, (own, tuple(state)))
        arrived.append(climb_up(chunk, group, count))
    gated, square = carried_part(maps, still, scale, entering, states)
    mamba_out = norm(
        gated, norm_gain[None], shared_parts(square), channels * lax.axis_size("tp")
    )
    if turns == 1:
        outs = flash(payloads, length, own=own, final=True)
    else:
        outs = flash(
            payloads, length, state=state, chunks=arrived[-1:], final=True, base=turns - 1
        )
    return join(swap(outs, group, count), group), mamba_out


def solution(mesh):
    return jax.shard_map(
        per_device,
        mesh=mesh,
        in_specs=(
            P("ctx", "tp"),
            P("ctx", "tp"),
            P("ctx", "tp"),
            P("ctx", "tp"),
            P("ctx", "tp"),
            P("tp", None),
            P("tp", None),
            P("tp"),
            P("tp"),
            P("tp"),
            P("tp"),
        ),
        out_specs=(P("ctx", "tp"), P("ctx", "tp")),
        check_vma=False,
    )
```

```python
import functools
import math

import jax
import jax.numpy as jnp
from jax import lax
from jax.experimental import pallas as pl
from jax.experimental.pallas import tpu as pltpu
from jax.sharding import PartitionSpec as P

HD = 128
DECAY_CHANNELS = 64
SCAN_TOKENS = 128
LANES = 128
UNROLL = 8
LOG2E = math.log2(math.e)
VMEM_LIMIT = 14 * 1024 * 1024

F32 = jnp.float32
BF16 = jnp.bfloat16


def vmem():
    return pl.BlockSpec(memory_space=pltpu.VMEM)


def hbm():
    return pl.BlockSpec(memory_space=pltpu.HBM)


def launch(kernel, name, out_shape, *inputs, after=(), flops=0, scratch=(), in_specs=None, out_specs=None, grid=None):
    count, skip = len(inputs), len(after)
    single = isinstance(out_shape, jax.ShapeDtypeStruct)
    shapes = [out_shape] if single else list(out_shape)
    size = sum(x.size * x.dtype.itemsize for x in list(inputs) + shapes)

    def body(*refs):
        kernel(*refs[:count], *refs[count + skip :])

    result = pl.pallas_call(
        body,
        **({} if grid is None else {"grid": grid}),
        out_shape=shapes,
        in_specs=(in_specs or [vmem()] * count) + [pl.BlockSpec(memory_space=pl.ANY)] * skip,
        out_specs=out_specs or [vmem()] * len(shapes),
        scratch_shapes=list(scratch),
        compiler_params=pltpu.CompilerParams(vmem_limit_bytes=VMEM_LIMIT),
        cost_estimate=pl.CostEstimate(flops=flops, bytes_accessed=size, transcendentals=0),
        name=name,
    )(*inputs, *after)
    return result[0] if single else result


def place(group):
    return lax.rem(lax.axis_index("ctx"), jnp.int32(group))


def swap(pieces, group, count):
    result = list(pieces)
    for k in reversed(range(1, group)):
        perm = [(i, (i // group) * group + ((i % group) ^ k)) for i in range(count)]
        result[k] = lax.ppermute(pieces[k], "ctx", perm)
    return result


def climb_up(array, group, count, steps=1, first=0):
    perm = [(i, i + group * steps) for i in range(group * first, count - group * steps)]
    return lax.ppermute(array, "ctx", perm)


def shape_of(shape, dtype):
    return jax.ShapeDtypeStruct(shape, dtype)


def tie(array, after):
    return pl.pallas_call(
        lambda *refs: None,
        out_shape=shape_of(array.shape, array.dtype),
        in_specs=[pl.BlockSpec(memory_space=pl.ANY)] * (1 + len(after)),
        out_specs=pl.BlockSpec(memory_space=pl.ANY),
        input_output_aliases={0: 0},
        compiler_params=pltpu.CompilerParams(vmem_limit_bytes=1024 * 1024),
        name="tie",
    )(array, *after)


def pack_kv(keys, values, group):
    length, width = keys.shape
    piece = width // group

    def kernel(k_ref, v_ref, *outs):
        mine = place(group)
        for k in range(group):
            columns = pl.ds(pl.multiple_of((mine ^ k) * piece, piece), piece)
            outs[k][0] = k_ref[:, columns]
            outs[k][1] = v_ref[:, columns]

    return launch(
        kernel,
        "pack_kv",
        [shape_of((2, length, piece), keys.dtype)] * group,
        keys,
        values,
        flops=5000000000,
        grid=(1,),
        in_specs=[pl.BlockSpec((length, width), lambda i: (0, 0))] * 2,
    )


def join(pieces, group):
    length, width = pieces[0].shape

    def kernel(*refs):
        out_ref, sems = refs[group:]
        mine = place(group)
        copies = []
        for k in range(group):
            columns = pl.ds(pl.multiple_of((mine ^ k) * width, width), width)
            copies.append(
                pltpu.make_async_copy(refs[group - 1 - k], out_ref.at[:, columns], sems.at[k])
            )
        for copy in copies:
            copy.start()
        for copy in copies:
            copy.wait()

    return launch(
        kernel,
        "join_heads",
        shape_of((length, width * group), pieces[0].dtype),
        *reversed(pieces),
        out_specs=[hbm()],
        scratch=[pltpu.SemaphoreType.DMA((group,))],
    )


def flash_chunk(q_refs, kv_ref, before, after, extended, own, length):
    group = len(q_refs)
    heads = q_refs[0].shape[1] // HD
    kv_heads = kv_ref.shape[3] // HD
    share = heads // kv_heads
    rows = group * length
    tile = min(rows, 2 * length)
    rate = LOG2E / math.sqrt(HD)
    for kv in range(kv_heads):
        lanes = slice(kv * HD, (kv + 1) * HD)
        keys = kv_ref[:, 0, :, lanes].reshape(rows, HD)
        extended[:, :HD] = kv_ref[:, 1, :, lanes].reshape(rows, HD)
        extended[:, HD:] = jnp.ones((rows, HD), BF16)
        tiles = [
            (h, start)
            for start in range(0, rows, tile)
            for h in range(kv * share, (kv + 1) * share)
        ]

        def score(h, start):
            parts = q_refs[start // length : (start + tile) // length]
            q = [ref[:length, h * HD : (h + 1) * HD] for ref in parts]
            q = jnp.concatenate(q, axis=0) if len(q) > 1 else q[0]
            scores = lax.dot_general(
                q, keys, (((1,), (1,)), ((), ())), preferred_element_type=F32
            )
            if own:
                flip = place(group) * length
                row = (lax.broadcasted_iota(jnp.int32, (tile, rows), 0) + start) ^ flip
                column = lax.broadcasted_iota(jnp.int32, (tile, rows), 1) ^ flip
                scores = jnp.where(column <= row, scores, -1e30)
            return scores

        ahead = score(*tiles[0])
        for n, (h, start) in enumerate(tiles):
            scores = ahead
            if n + 1 < len(tiles):
                ahead = score(*tiles[n + 1])
            here = slice(start, start + tile)
            top = jnp.max(scores, axis=1, keepdims=True)
            if not own:
                top_before = before[1][h, here]
                top = jnp.maximum(top_before[:, :1], top)
            weights = jnp.exp2((scores - top) * rate).astype(BF16)
            value = jnp.dot(weights, extended[...], preferred_element_type=F32)
            top = jnp.broadcast_to(top, (tile, LANES))
            if not own:
                keep = jnp.exp2((top_before - top) * rate)
                value = value + before[0][h, here] * jnp.concatenate([keep, keep], axis=1)
            yield h, start, tile, value
            if after is not None:
                after[0][h, here] = value
                after[1][h, here] = top


def finish_rows(out_refs, h, start, tile, value):
    length = out_refs[0].shape[0]
    result = (value[:, :HD] / value[:, HD:]).astype(BF16)
    for at in range(0, tile, length):
        out_refs[(start + at) // length][:, h * HD : (h + 1) * HD] = result[at : at + length]


def flash(q, length, own=None, state=(), chunks=(), final=False, base=1, after=()):
    group = len(q)
    heads = q[0].shape[1] // HD
    rows = group * length
    fixed = isinstance(base, int)
    has_own = own is not None
    specs = [] if fixed else [pl.BlockSpec(memory_space=pltpu.SMEM)]
    rest = list(q) + ([own] if has_own else []) + list(state) + list(chunks)
    specs = specs + [vmem()] * len(rest)

    def kernel(*refs):
        refs = list(refs)
        first = base if fixed else refs.pop(0)[0]
        q_refs = [refs.pop(0) for _ in range(group)]
        own_ref = refs.pop(0) if has_own else None
        held = None if has_own else (refs.pop(0), refs.pop(0))
        chunk_refs = [refs.pop(0) for _ in range(len(chunks))]
        extended = refs.pop()
        turn = lax.axis_index("ctx") // group
        outs = None if final else tuple(refs)
        if has_own:
            for done in flash_chunk(q_refs, own_ref, None, outs, extended, True, length):
                if final:
                    finish_rows(refs, *done)
            held = outs
        for number, ref in enumerate(chunk_refs):

            @pl.when(turn >= first + number)
            def _(ref=ref, held=held):
                for done in flash_chunk(q_refs, ref, held, outs, extended, False, length):
                    if final:
                        finish_rows(refs, *done)

            if not has_own and number == 0:

                @pl.when(turn < first)
                def _(held=held):
                    for h in range(heads):
                        if final:
                            finish_rows(refs, h, 0, rows, held[0][h])
                        else:
                            outs[0][h] = held[0][h]
                            outs[1][h] = held[1][h]

            held = outs

    if final:
        out_shape = [shape_of((length, heads * HD), BF16)] * group
    else:
        out_shape = [
            shape_of((heads, rows, HD + LANES), F32),
            shape_of((heads, rows, LANES), F32),
        ]
    parts = len(chunks) + has_own
    return launch(
        kernel,
        "flash",
        out_shape,
        *([] if fixed else [base]),
        *rest,
        after=after,
        in_specs=specs,
        flops=4 * heads * rows * rows * HD * parts,
        scratch=[pltpu.VMEM((rows, HD + LANES), BF16)],
    )


def widen(row, lanes):
    extra = lanes - row.shape[1]
    if not extra:
        return row
    return jnp.concatenate([row, jnp.zeros((row.shape[0], extra), row.dtype)], axis=1)


def project(x, step_weight, state_weight, after=()):
    length, channels = x.shape
    heads = step_weight.shape[1]

    def kernel(x_ref, step_ref, map_ref, out_ref):
        x = x_ref[...]
        out_ref[:, :heads] = jnp.dot(x, step_ref[...], preferred_element_type=F32)
        maps = lax.dot_general(
            x, map_ref[...], (((1,), (1,)), ((), ())), preferred_element_type=F32
        )
        out_ref[:, heads:] = widen(maps, LANES)

    return launch(
        kernel,
        "project",
        shape_of((length, heads + LANES), F32),
        x,
        step_weight,
        state_weight.T,
        after=after,
        flops=4 * length * channels * heads,
    )


def owners(heads):
    shape = (LANES, heads * DECAY_CHANNELS)
    head = lax.broadcasted_iota(jnp.int32, shape, 0)
    channel = lax.broadcasted_iota(jnp.int32, shape, 1)
    return (channel // DECAY_CHANNELS == head).astype(BF16)


def pack_row(row, rows):
    high = row.astype(BF16).astype(F32)
    rest = row - high
    middle = rest.astype(BF16).astype(F32)
    low = rest - middle
    return jnp.concatenate([high, middle, low, jnp.zeros((rows - 3, row.shape[1]), F32)], axis=0)


def unpack_row(rows):
    rows = rows.astype(F32)
    return rows[0:1] + rows[1:2] + rows[2:3]


def spread_total(rows, owner):
    wide = jnp.dot(rows, owner, preferred_element_type=F32)
    return wide[0:1] + wide[1:2] + wide[2:3]


def block_state(parts, bias, rate, x, q, states, group, after=()):
    length, channels = x.shape
    every = parts[0].shape[1] - LANES
    heads = bias.shape[1]
    width = channels // group
    columns = q.shape[1] // group
    bands = width // columns
    count = len(parts)

    def kernel(*refs):
        bias_ref, rate_ref, x_ref, q_ref = refs[count : count + 4]
        climb_ref, climb_t_ref, step_t_ref, maps_ref = refs[count + 4 : count + 8]
        outs = refs[count + 8 : count + 8 + group]
        held = refs[count + 8 + group]
        summed = refs[0][...]
        for ref in refs[1:count]:
            summed = summed + ref[...]
        shift = lax.rem(every - lax.axis_index("tp") * heads, jnp.int32(every))
        raw = pltpu.roll(summed[:, :every], shift, 1) + widen(bias_ref[...], every)
        step = jnp.maximum(raw, 0.0) + jnp.log1p(jnp.exp(-jnp.abs(raw)))
        log_decay = -widen(rate_ref[...], every) * step
        row = lax.broadcasted_iota(jnp.int32, (length, length), 0)
        column = lax.broadcasted_iota(jnp.int32, (length, length), 1)
        lower = (column <= row).astype(F32)
        climb = jnp.dot(
            lower, log_decay, precision=lax.Precision.HIGHEST, preferred_element_type=F32
        )
        maps = summed[:, every:]
        climb_ref[...] = climb * LOG2E
        maps_ref[...] = maps
        climb_t = climb.T
        step_t = step.T
        climb_t_ref[...] = climb_t[:heads] * LOG2E
        step_t_ref[...] = step_t[:heads]
        b_t = maps.T[:states]
        weight_t = jnp.exp(climb_t[:, length - 1 :] - climb_t) * step_t
        bundle = 4
        span = bundle * DECAY_CHANNELS
        owner = lax.broadcasted_iota(jnp.int32, (1, span), 1) // DECAY_CHANNELS
        for at in range(0, heads, bundle):
            feed = [b_t * weight_t[at + i : at + i + 1] for i in range(bundle)]
            feed = jnp.concatenate(feed, axis=0).astype(BF16)
            start = at * DECAY_CHANNELS
            product = jnp.dot(feed, x_ref[:, start : start + span], preferred_element_type=F32)
            state = product[:states]
            for i in range(1, bundle):
                state = jnp.where(owner == i, product[i * states : (i + 1) * states], state)
            piece, offset = divmod(start, width)
            band, offset = divmod(offset, columns)
            rows = slice(band * states, (band + 1) * states)
            held[piece, rows, offset : offset + span] = state.astype(BF16)
        totals = pack_row(climb[length - 1 :], states)
        for piece in range(group):
            at = piece * (heads // group)
            here = totals if not at else pltpu.roll(totals, every - at, 1)
            held[piece, bands * states :, :] = widen(here[:, :LANES], columns).astype(BF16)
        mine = place(group)
        for k in range(group):
            here = pl.ds(pl.multiple_of((mine ^ k) * columns, columns), columns)
            outs[k][:length] = q_ref[:, here]
            outs[k][length:] = held[mine ^ k]

    payload = shape_of((length + (bands + 1) * states, columns), BF16)
    result = launch(
        kernel,
        "block_state",
        [
            shape_of((length, every), F32),
            shape_of((heads, length), F32),
            shape_of((heads, length), F32),
            shape_of((length, LANES), F32),
        ]
        + [payload] * group,
        *parts,
        bias,
        rate,
        x,
        q,
        after=after,
        flops=32 * length * states * channels,
        scratch=[pltpu.VMEM((group, (bands + 1) * states, columns), BF16)],
    )
    return result[:4], result[4:]


def local_part(x, gate, climb, climb_t, step_t, maps, skip, states, after=()):
    length, channels = x.shape
    heads = channels // DECAY_CHANNELS

    def kernel(
        x_ref, gate_ref, climb_ref, climb_t_ref, step_t_ref, maps_ref, skip_ref, still_ref, scale_ref
    ):
        maps = maps_ref[...]
        inner = lax.dot_general(
            maps[:, states : 2 * states],
            maps[:, :states],
            (((1,), (1,)), ((), ())),
            precision=lax.Precision.HIGHEST,
            preferred_element_type=F32,
        )
        row = lax.broadcasted_iota(jnp.int32, (length, length), 0)
        column = lax.broadcasted_iota(jnp.int32, (length, length), 1)
        inner = jnp.where(column <= row, inner, 0.0)
        left = lax.broadcasted_iota(jnp.int32, (length, LANES), 1) < DECAY_CHANNELS

        for j in range(0, heads, 2):
            columns = slice(j * DECAY_CHANNELS, j * DECAY_CHANNELS + LANES)
            x = x_ref[:, columns]
            wide = [jnp.broadcast_to(climb_ref[:, i : i + 1], (length, length)) for i in (j, j + 1)]
            mixed = []
            for i in (j, j + 1):
                fall = jnp.minimum(wide[i - j] - climb_t_ref[i : i + 1], 0.0)
                mixed.append((inner * jnp.exp2(fall) * step_t_ref[i : i + 1]).astype(BF16))
            zero = jnp.zeros_like(x)
            feeds = jnp.concatenate([jnp.where(left, x, zero), jnp.where(left, zero, x)], axis=0)
            local = jnp.dot(jnp.concatenate(mixed, axis=1), feeds, preferred_element_type=F32)
            gain = jnp.where(left[:1], skip_ref[:, j : j + 1], skip_ref[:, j + 1 : j + 2])
            grown = jnp.exp2(jnp.where(left, wide[0], wide[1]))
            gate = gate_ref[:, columns].astype(F32)
            half = 0.5 * gate
            silu = half + half * jnp.tanh(half)
            still_ref[:, columns] = (local + gain * x.astype(F32)) * silu
            scale_ref[:, columns] = grown * silu

    return launch(
        kernel,
        "local_part",
        [shape_of((length, channels), F32)] * 2,
        x,
        gate,
        climb,
        climb_t,
        step_t,
        maps,
        skip,
        after=after,
        flops=4 * length * length * channels,
    )


def gather_blocks(group, states, length, refs, held):
    mine = place(group)
    for k in range(group):
        held[mine ^ k] = refs[k][length:]


def block_of(held, b, states, columns, width):
    bands = width // columns
    rows = [held[b, i * states : (i + 1) * states] for i in range(bands)]
    state = jnp.concatenate(rows, axis=1) if bands > 1 else rows[0]
    return state.astype(F32), held[b, bands * states :, :LANES]


def group_total(payloads, length, states, width, after=()):
    group = len(payloads)
    rows, columns = payloads[0].shape
    heads = width // DECAY_CHANNELS

    def kernel(*refs):
        out_ref, held = refs[group:]
        gather_blocks(group, states, length, refs[:group], held)
        owner = owners(heads)
        state, packed = block_of(held, 0, states, columns, width)
        total = unpack_row(packed)
        for b in range(1, group):
            more, packed = block_of(held, b, states, columns, width)
            state = jnp.exp(spread_total(packed, owner)) * state + more
            total = total + unpack_row(packed)
        out_ref[:, :width] = state.astype(BF16)
        out_ref[:, width:] = pack_row(total, states).astype(BF16)

    return launch(
        kernel,
        "group_total",
        shape_of((states, width + LANES), BF16),
        *payloads,
        after=after,
        scratch=[pltpu.VMEM((group, rows - length, columns), BF16)],
    )


def entering_states(payloads, earlier, length, states, width, after=()):
    group = len(payloads)
    rows, columns = payloads[0].shape
    heads = width // DECAY_CHANNELS
    count = len(earlier)

    def kernel(*refs):
        earlier_refs = refs[group : group + count]
        outs = refs[group + count : 2 * group + count]
        held, entering = refs[2 * group + count :]
        gather_blocks(group, states, length, refs[:group], held)
        owner = owners(heads)
        state = jnp.zeros((states, width), F32)
        for ref in reversed(earlier_refs):
            state = jnp.exp(spread_total(ref[:, width:], owner)) * state
            state = state + ref[:, :width].astype(F32)
        for b in range(group):
            entering[b] = state
            if b < group - 1:
                more, packed = block_of(held, b, states, columns, width)
                state = jnp.exp(spread_total(packed, owner)) * state + more
        mine = place(group)
        for k in range(group):
            outs[k][...] = entering[mine ^ k]

    return launch(
        kernel,
        "entering_states",
        [shape_of((states, width), F32)] * group,
        *payloads,
        *earlier,
        after=after,
        scratch=[
            pltpu.VMEM((group, rows - length, columns), BF16),
            pltpu.VMEM((group, states, width), F32),
        ],
    )


def carried_part(maps, still, scale, entering, states, after=()):
    length, channels = still.shape
    group = len(entering)
    width = channels // group
    span = min(width, 512)

    def kernel(maps_ref, still_ref, scale_ref, *refs):
        gated_ref, square_ref, held = refs[group:]
        mine = place(group)
        for k in range(group):
            held[mine ^ k] = refs[k][...]
        c = maps_ref[:, states : 2 * states]
        c_high = c.astype(BF16)
        c_low = (c - c_high.astype(F32)).astype(BF16)
        c = jnp.concatenate([c_high, c_low, c_high], axis=1)
        folded = jnp.zeros(square_ref.shape, F32)
        for at in range(0, channels, span):
            piece, offset = divmod(at, width)
            state = held[piece, :, offset : offset + span]
            high = state.astype(BF16)
            low = (state - high.astype(F32)).astype(BF16)
            carried = jnp.dot(
                c, jnp.concatenate([high, high, low], axis=0), preferred_element_type=F32
            )
            columns = slice(at, at + span)
            gated = still_ref[:, columns] + scale_ref[:, columns] * carried
            gated_ref[:, columns] = gated
            square = gated * gated
            for lane in range(0, span, LANES):
                folded = folded + square[:, lane : lane + LANES]
        square_ref[...] = folded

    return launch(
        kernel,
        "carried_part",
        [shape_of((length, channels), F32), shape_of((length, LANES), F32)],
        maps,
        still,
        scale,
        *entering,
        after=after,
        flops=6 * length * states * channels,
        scratch=[pltpu.VMEM((group, states, width), F32)],
    )


def norm(gated, gain, squares, every):
    length, channels = gated.shape
    count = len(squares)

    def kernel(gated_ref, gain_ref, *refs):
        out_ref = refs[count]
        square = refs[0][...]
        for ref in refs[1:count]:
            square = square + ref[...]
        mean = jnp.sum(square, axis=1, keepdims=True) / every
        factor = jnp.broadcast_to(lax.rsqrt(mean + 1e-05), square.shape)
        for at in range(0, channels, LANES):
            columns = slice(at, at + LANES)
            out_ref[:, columns] = (gated_ref[:, columns] * factor * gain_ref[:, columns]).astype(BF16)

    return launch(
        kernel, "norm", shape_of((length, channels), BF16), gated, gain, *squares
    )


def shared_parts(part):
    if lax.axis_size("tp") == 2:
        return [part, lax.ppermute(part, "tp", [(0, 1), (1, 0)])]
    return [lax.psum(part, "tp")]


def earlier_states(total, group, turns, count, states, width):
    if turns <= UNROLL:
        return [climb_up(total, group, count, steps) for steps in range(1, turns)]
    heads = width // DECAY_CHANNELS

    def one(_, carry):
        travelling, summed, ahead = carry
        travelling = climb_up(travelling, group, count)
        summed = summed + jnp.exp(ahead) * travelling[:, :width].astype(F32)
        more = unpack_row(travelling[:, width : width + heads])
        return travelling, summed, ahead + jnp.repeat(more, DECAY_CHANNELS, axis=1)

    start = (total, jnp.zeros((states, width), F32), jnp.zeros((1, width), F32))
    _, summed, _ = lax.fori_loop(1, turns, one, start)
    return [jnp.concatenate([summed.astype(BF16), jnp.zeros((states, LANES), BF16)], axis=1)]


def per_device(
    queries,
    keys,
    values,
    mixer_input,
    gate,
    step_weight,
    state_weight,
    step_bias,
    decay_rate,
    skip_gain,
    norm_gain,
):
    count = lax.axis_size("ctx")
    length = queries.shape[0]
    channels = mixer_input.shape[1]
    states = state_weight.shape[1] // 2
    group = math.gcd(keys.shape[1] // HD, count)
    turns = count // group
    width = channels // group

    packed = pack_kv(keys, values, group)
    parts = shared_parts(project(mixer_input, step_weight, state_weight, after=packed[:1]))
    blocks = swap(packed, group, count)
    (climb, climb_t, step_t, maps), payloads = block_state(
        parts, step_bias[None], decay_rate[None], mixer_input, queries, states, group
    )
    still, scale = local_part(
        mixer_input, gate, climb, climb_t, step_t, maps, skip_gain[None], states
    )
    own = jnp.stack([tie(blocks[0], [still])] + blocks[1:])
    sent = payloads[:1]
    payloads = swap(payloads, group, count)
    ring = 1 < turns <= UNROLL
    arrived, ready = [], []
    if ring:
        arrived.append(climb_up(own, group, count))
    if ring and turns > 2:
        arrived[0] = tie(arrived[0], sent)
        ready = [arrived[0]]
        arrived.append(climb_up(arrived[0], group, count, first=1))
    total = group_total(payloads, length, states, width, after=ready)
    earlier = earlier_states(total, group, turns, count, states, width)
    state = flash(payloads, length, own=own, chunks=arrived[:-1][:1], after=[total])
    if ring and turns > 3:
        arrived[1] = tie(arrived[1], [state[1]] + earlier[:1] + earlier[:0:-1])
        ready = [arrived[1]]
        for step in range(2, turns - 1):
            arrived.append(climb_up(arrived[-1], group, count, first=step))
    entering = entering_states(payloads, earlier, length, states, width, after=ready)
    if ring and turns > 3:
        state = flash(
            payloads, length, state=state, chunks=arrived[1:-1], base=2, after=entering[:1]
        )
    entering = swap(entering, group, count)
    if turns > 1 and not ring:

        def one(step, carry):
            chunk, state = carry
            chunk = climb_up(chunk, group, count)
            state = flash(payloads, length, state=state, chunks=[chunk], base=jnp.reshape(step, (1,)))
            return chunk, tuple(state)

        chunk, state = lax.fori_loop(1, turns - 1, one, (own, tuple(state)))
        arrived.append(climb_up(chunk, group, count))
    gated, square = carried_part(maps, still, scale, entering, states)
    mamba_out = norm(
        gated, norm_gain[None], shared_parts(square), channels * lax.axis_size("tp")
    )
    if turns == 1:
        outs = flash(payloads, length, own=own, final=True)
    else:
        outs = flash(
            payloads, length, state=state, chunks=arrived[-1:], final=True, base=turns - 1
        )
    return join(swap(outs, group, count), group), mamba_out


def solution(mesh):
    return jax.shard_map(
        per_device,
        mesh=mesh,
        in_specs=(
            P("ctx", "tp"),
            P("ctx", "tp"),
            P("ctx", "tp"),
            P("ctx", "tp"),
            P("ctx", "tp"),
            P("tp", None),
            P("tp", None),
            P("tp"),
            P("tp"),
            P("tp"),
            P("tp"),
        ),
        out_specs=(P("ctx", "tp"), P("ctx", "tp")),
        check_vma=False,
    )
```

```python
import functools
import math

import jax
import jax.numpy as jnp
from jax import lax
from jax.experimental import pallas as pl
from jax.experimental.pallas import tpu as pltpu
from jax.sharding import PartitionSpec as P

HD = 128
DECAY_CHANNELS = 64
SCAN_TOKENS = 128
LANES = 128
UNROLL = 8
LOG2E = math.log2(math.e)
VMEM_LIMIT = 14 * 1024 * 1024

F32 = jnp.float32
BF16 = jnp.bfloat16


def vmem():
    return pl.BlockSpec(memory_space=pltpu.VMEM)


def hbm():
    return pl.BlockSpec(memory_space=pltpu.HBM)


def launch(kernel, name, out_shape, *inputs, after=(), flops=0, scratch=(), in_specs=None, out_specs=None, grid=None):
    count, skip = len(inputs), len(after)
    single = isinstance(out_shape, jax.ShapeDtypeStruct)
    shapes = [out_shape] if single else list(out_shape)
    size = sum(x.size * x.dtype.itemsize for x in list(inputs) + shapes)

    def body(*refs):
        kernel(*refs[:count], *refs[count + skip :])

    result = pl.pallas_call(
        body,
        **({} if grid is None else {"grid": grid}),
        out_shape=shapes,
        in_specs=(in_specs or [vmem()] * count) + [pl.BlockSpec(memory_space=pl.ANY)] * skip,
        out_specs=out_specs or [vmem()] * len(shapes),
        scratch_shapes=list(scratch),
        compiler_params=pltpu.CompilerParams(vmem_limit_bytes=VMEM_LIMIT),
        cost_estimate=pl.CostEstimate(flops=flops, bytes_accessed=size, transcendentals=0),
        name=name,
    )(*inputs, *after)
    return result[0] if single else result


def place(group):
    return lax.rem(lax.axis_index("ctx"), jnp.int32(group))


def swap(pieces, group, count):
    result = list(pieces)
    for k in reversed(range(1, group)):
        perm = [(i, (i // group) * group + ((i % group) ^ k)) for i in range(count)]
        result[k] = lax.ppermute(pieces[k], "ctx", perm)
    return result


def climb_up(array, group, count, steps=1, first=0):
    perm = [(i, i + group * steps) for i in range(group * first, count - group * steps)]
    return lax.ppermute(array, "ctx", perm)


def shape_of(shape, dtype):
    return jax.ShapeDtypeStruct(shape, dtype)


def tie(array, after):
    return pl.pallas_call(
        lambda *refs: None,
        out_shape=shape_of(array.shape, array.dtype),
        in_specs=[pl.BlockSpec(memory_space=pl.ANY)] * (1 + len(after)),
        out_specs=pl.BlockSpec(memory_space=pl.ANY),
        input_output_aliases={0: 0},
        compiler_params=pltpu.CompilerParams(vmem_limit_bytes=1024 * 1024),
        name="tie",
    )(array, *after)


def pack_kv(keys, values, group):
    length, width = keys.shape
    piece = width // group

    def kernel(k_ref, v_ref, *outs):
        mine = place(group)
        for k in range(group):
            columns = pl.ds(pl.multiple_of((mine ^ k) * piece, piece), piece)
            outs[k][0] = k_ref[:, columns]
            outs[k][1] = v_ref[:, columns]

    return launch(
        kernel,
        "pack_kv",
        [shape_of((2, length, piece), keys.dtype)] * group,
        keys,
        values,
        flops=5000000000,
        grid=(1,),
        in_specs=[pl.BlockSpec((length, width), lambda i: (0, 0))] * 2,
    )


def join(pieces, group):
    length, width = pieces[0].shape

    def kernel(*refs):
        out_ref, sems = refs[group:]
        mine = place(group)
        copies = []
        for k in range(group):
            columns = pl.ds(pl.multiple_of((mine ^ k) * width, width), width)
            copies.append(
                pltpu.make_async_copy(refs[group - 1 - k], out_ref.at[:, columns], sems.at[k])
            )
        for copy in copies:
            copy.start()
        for copy in copies:
            copy.wait()

    return launch(
        kernel,
        "join_heads",
        shape_of((length, width * group), pieces[0].dtype),
        *reversed(pieces),
        out_specs=[hbm()],
        scratch=[pltpu.SemaphoreType.DMA((group,))],
    )


def flash_chunk(q_refs, kv_ref, before, after, extended, own, length):
    group = len(q_refs)
    heads = q_refs[0].shape[1] // HD
    kv_heads = kv_ref.shape[3] // HD
    share = heads // kv_heads
    rows = group * length
    tile = min(rows, 2 * length)
    rate = LOG2E / math.sqrt(HD)
    for kv in range(kv_heads):
        lanes = slice(kv * HD, (kv + 1) * HD)
        keys = kv_ref[:, 0, :, lanes].reshape(rows, HD)
        extended[:, :HD] = kv_ref[:, 1, :, lanes].reshape(rows, HD)
        extended[:, HD:] = jnp.ones((rows, HD), BF16)
        tiles = [
            (h, start)
            for start in range(0, rows, tile)
            for h in range(kv * share, (kv + 1) * share)
        ]

        def score(h, start):
            parts = q_refs[start // length : (start + tile) // length]
            q = [ref[:length, h * HD : (h + 1) * HD] for ref in parts]
            q = jnp.concatenate(q, axis=0) if len(q) > 1 else q[0]
            scores = lax.dot_general(
                q, keys, (((1,), (1,)), ((), ())), preferred_element_type=F32
            )
            if own:
                flip = place(group) * length
                row = (lax.broadcasted_iota(jnp.int32, (tile, rows), 0) + start) ^ flip
                column = lax.broadcasted_iota(jnp.int32, (tile, rows), 1) ^ flip
                scores = jnp.where(column <= row, scores, -1e30)
            return scores

        ahead = score(*tiles[0])
        for n, (h, start) in enumerate(tiles):
            scores = ahead
            if n + 1 < len(tiles):
                ahead = score(*tiles[n + 1])
            here = slice(start, start + tile)
            top = jnp.broadcast_to(jnp.max(scores, axis=1, keepdims=True), (tile, LANES))
            if not own:
                top_before = before[1][h, here]
                top = jnp.maximum(top_before, top)
            across = [top] * (rows // LANES)
            across = jnp.concatenate(across, axis=1) if len(across) > 1 else top
            weights = jnp.exp2((scores - across) * rate).astype(BF16)
            value = jnp.dot(weights, extended[...], preferred_element_type=F32)
            if not own:
                keep = jnp.exp2((top_before - top) * rate)
                value = value + before[0][h, here] * jnp.concatenate([keep, keep], axis=1)
            yield h, start, tile, value
            if after is not None:
                after[0][h, here] = value
                after[1][h, here] = top


def finish_rows(out_refs, h, start, tile, value):
    length = out_refs[0].shape[0]
    result = (value[:, :HD] / value[:, HD:]).astype(BF16)
    for at in range(0, tile, length):
        out_refs[(start + at) // length][:, h * HD : (h + 1) * HD] = result[at : at + length]


def flash(q, length, own=None, state=(), chunks=(), final=False, base=1, after=()):
    group = len(q)
    heads = q[0].shape[1] // HD
    rows = group * length
    fixed = isinstance(base, int)
    has_own = own is not None
    specs = [] if fixed else [pl.BlockSpec(memory_space=pltpu.SMEM)]
    rest = list(q) + ([own] if has_own else []) + list(state) + list(chunks)
    specs = specs + [vmem()] * len(rest)

    def kernel(*refs):
        refs = list(refs)
        first = base if fixed else refs.pop(0)[0]
        q_refs = [refs.pop(0) for _ in range(group)]
        own_ref = refs.pop(0) if has_own else None
        held = None if has_own else (refs.pop(0), refs.pop(0))
        chunk_refs = [refs.pop(0) for _ in range(len(chunks))]
        extended = refs.pop()
        turn = lax.axis_index("ctx") // group
        outs = None if final else tuple(refs)
        if has_own:
            for done in flash_chunk(q_refs, own_ref, None, outs, extended, True, length):
                if final:
                    finish_rows(refs, *done)
            held = outs
        for number, ref in enumerate(chunk_refs):

            @pl.when(turn >= first + number)
            def _(ref=ref, held=held):
                for done in flash_chunk(q_refs, ref, held, outs, extended, False, length):
                    if final:
                        finish_rows(refs, *done)

            if not has_own and number == 0:

                @pl.when(turn < first)
                def _(held=held):
                    for h in range(heads):
                        if final:
                            finish_rows(refs, h, 0, rows, held[0][h])
                        else:
                            outs[0][h] = held[0][h]
                            outs[1][h] = held[1][h]

            held = outs

    if final:
        out_shape = [shape_of((length, heads * HD), BF16)] * group
    else:
        out_shape = [
            shape_of((heads, rows, HD + LANES), F32),
            shape_of((heads, rows, LANES), F32),
        ]
    parts = len(chunks) + has_own
    return launch(
        kernel,
        "flash",
        out_shape,
        *([] if fixed else [base]),
        *rest,
        after=after,
        in_specs=specs,
        flops=4 * heads * rows * rows * HD * parts,
        scratch=[pltpu.VMEM((rows, HD + LANES), BF16)],
    )


def widen(row, lanes):
    extra = lanes - row.shape[1]
    if not extra:
        return row
    return jnp.concatenate([row, jnp.zeros((row.shape[0], extra), row.dtype)], axis=1)


def project(x, step_weight, state_weight, after=()):
    length, channels = x.shape
    heads = step_weight.shape[1]

    def kernel(x_ref, step_ref, map_ref, out_ref):
        x = x_ref[...]
        out_ref[:, :heads] = jnp.dot(x, step_ref[...], preferred_element_type=F32)
        maps = lax.dot_general(
            x, map_ref[...], (((1,), (1,)), ((), ())), preferred_element_type=F32
        )
        out_ref[:, heads:] = widen(maps, LANES)

    return launch(
        kernel,
        "project",
        shape_of((length, heads + LANES), F32),
        x,
        step_weight,
        state_weight.T,
        after=after,
        flops=4 * length * channels * heads,
    )


def owners(heads):
    shape = (LANES, heads * DECAY_CHANNELS)
    head = lax.broadcasted_iota(jnp.int32, shape, 0)
    channel = lax.broadcasted_iota(jnp.int32, shape, 1)
    return (channel // DECAY_CHANNELS == head).astype(BF16)


def pack_row(row, rows):
    high = row.astype(BF16).astype(F32)
    rest = row - high
    middle = rest.astype(BF16).astype(F32)
    low = rest - middle
    return jnp.concatenate([high, middle, low, jnp.zeros((rows - 3, row.shape[1]), F32)], axis=0)


def unpack_row(rows):
    rows = rows.astype(F32)
    return rows[0:1] + rows[1:2] + rows[2:3]


def spread_total(rows, owner):
    wide = jnp.dot(rows, owner, preferred_element_type=F32)
    return wide[0:1] + wide[1:2] + wide[2:3]


def block_state(parts, bias, rate, x, q, states, group, after=()):
    length, channels = x.shape
    every = parts[0].shape[1] - LANES
    heads = bias.shape[1]
    width = channels // group
    columns = q.shape[1] // group
    bands = width // columns
    count = len(parts)

    def kernel(*refs):
        bias_ref, rate_ref, x_ref, q_ref = refs[count : count + 4]
        climb_ref, climb_t_ref, step_t_ref, maps_ref = refs[count + 4 : count + 8]
        outs = refs[count + 8 : count + 8 + group]
        held = refs[count + 8 + group]
        summed = refs[0][...]
        for ref in refs[1:count]:
            summed = summed + ref[...]
        shift = lax.rem(every - lax.axis_index("tp") * heads, jnp.int32(every))
        raw = pltpu.roll(summed[:, :every], shift, 1) + widen(bias_ref[...], every)
        step = jnp.maximum(raw, 0.0) + jnp.log1p(jnp.exp(-jnp.abs(raw)))
        log_decay = -widen(rate_ref[...], every) * step
        row = lax.broadcasted_iota(jnp.int32, (length, length), 0)
        column = lax.broadcasted_iota(jnp.int32, (length, length), 1)
        lower = (column <= row).astype(F32)
        climb = jnp.dot(
            lower, log_decay, precision=lax.Precision.HIGHEST, preferred_element_type=F32
        )
        maps = summed[:, every:]
        climb_ref[...] = climb * LOG2E
        maps_ref[...] = maps
        climb_t = climb.T
        step_t = step.T
        climb_t_ref[...] = climb_t[:heads] * LOG2E
        step_t_ref[...] = step_t[:heads]
        b_t = maps.T[:states]
        weight_t = jnp.exp(climb_t[:, length - 1 :] - climb_t) * step_t
        bundle = 4
        span = bundle * DECAY_CHANNELS
        owner = lax.broadcasted_iota(jnp.int32, (1, span), 1) // DECAY_CHANNELS
        for at in range(0, heads, bundle):
            feed = [b_t * weight_t[at + i : at + i + 1] for i in range(bundle)]
            feed = jnp.concatenate(feed, axis=0).astype(BF16)
            start = at * DECAY_CHANNELS
            product = jnp.dot(feed, x_ref[:, start : start + span], preferred_element_type=F32)
            state = product[:states]
            for i in range(1, bundle):
                state = jnp.where(owner == i, product[i * states : (i + 1) * states], state)
            piece, offset = divmod(start, width)
            band, offset = divmod(offset, columns)
            rows = slice(band * states, (band + 1) * states)
            held[piece, rows, offset : offset + span] = state.astype(BF16)
        totals = pack_row(climb[length - 1 :], states)
        for piece in range(group):
            at = piece * (heads // group)
            here = totals if not at else pltpu.roll(totals, every - at, 1)
            held[piece, bands * states :, :] = widen(here[:, :LANES], columns).astype(BF16)
        mine = place(group)
        for k in range(group):
            here = pl.ds(pl.multiple_of((mine ^ k) * columns, columns), columns)
            outs[k][:length] = q_ref[:, here]
            outs[k][length:] = held[mine ^ k]

    payload = shape_of((length + (bands + 1) * states, columns), BF16)
    result = launch(
        kernel,
        "block_state",
        [
            shape_of((length, every), F32),
            shape_of((heads, length), F32),
            shape_of((heads, length), F32),
            shape_of((length, LANES), F32),
        ]
        + [payload] * group,
        *parts,
        bias,
        rate,
        x,
        q,
        after=after,
        flops=32 * length * states * channels,
        scratch=[pltpu.VMEM((group, (bands + 1) * states, columns), BF16)],
    )
    return result[:4], result[4:]


def local_part(x, gate, climb, climb_t, step_t, maps, skip, states, after=()):
    length, channels = x.shape
    heads = channels // DECAY_CHANNELS

    def kernel(
        x_ref, gate_ref, climb_ref, climb_t_ref, step_t_ref, maps_ref, skip_ref, still_ref, scale_ref
    ):
        maps = maps_ref[...]
        inner = lax.dot_general(
            maps[:, states : 2 * states],
            maps[:, :states],
            (((1,), (1,)), ((), ())),
            precision=lax.Precision.HIGHEST,
            preferred_element_type=F32,
        )
        row = lax.broadcasted_iota(jnp.int32, (length, length), 0)
        column = lax.broadcasted_iota(jnp.int32, (length, length), 1)
        inner = jnp.where(column <= row, inner, 0.0)
        left = lax.broadcasted_iota(jnp.int32, (length, LANES), 1) < DECAY_CHANNELS

        for j in range(0, heads, 2):
            columns = slice(j * DECAY_CHANNELS, j * DECAY_CHANNELS + LANES)
            x = x_ref[:, columns]
            wide = [jnp.broadcast_to(climb_ref[:, i : i + 1], (length, length)) for i in (j, j + 1)]
            mixed = []
            for i in (j, j + 1):
                fall = jnp.minimum(wide[i - j] - climb_t_ref[i : i + 1], 0.0)
                mixed.append((inner * jnp.exp2(fall) * step_t_ref[i : i + 1]).astype(BF16))
            zero = jnp.zeros_like(x)
            feeds = jnp.concatenate([jnp.where(left, x, zero), jnp.where(left, zero, x)], axis=0)
            local = jnp.dot(jnp.concatenate(mixed, axis=1), feeds, preferred_element_type=F32)
            gain = jnp.where(left[:1], skip_ref[:, j : j + 1], skip_ref[:, j + 1 : j + 2])
            grown = jnp.exp2(jnp.where(left, wide[0], wide[1]))
            gate = gate_ref[:, columns].astype(F32)
            half = 0.5 * gate
            silu = half + half * jnp.tanh(half)
            still_ref[:, columns] = (local + gain * x.astype(F32)) * silu
            scale_ref[:, columns] = grown * silu

    return launch(
        kernel,
        "local_part",
        [shape_of((length, channels), F32)] * 2,
        x,
        gate,
        climb,
        climb_t,
        step_t,
        maps,
        skip,
        after=after,
        flops=4 * length * length * channels,
    )


def gather_blocks(group, states, length, refs, held):
    mine = place(group)
    for k in range(group):
        held[mine ^ k] = refs[k][length:]


def block_of(held, b, states, columns, width):
    bands = width // columns
    rows = [held[b, i * states : (i + 1) * states] for i in range(bands)]
    state = jnp.concatenate(rows, axis=1) if bands > 1 else rows[0]
    return state.astype(F32), held[b, bands * states :, :LANES]


def group_total(payloads, length, states, width, after=()):
    group = len(payloads)
    rows, columns = payloads[0].shape
    heads = width // DECAY_CHANNELS

    def kernel(*refs):
        out_ref, held = refs[group:]
        gather_blocks(group, states, length, refs[:group], held)
        owner = owners(heads)
        state, packed = block_of(held, 0, states, columns, width)
        total = unpack_row(packed)
        for b in range(1, group):
            more, packed = block_of(held, b, states, columns, width)
            state = jnp.exp(spread_total(packed, owner)) * state + more
            total = total + unpack_row(packed)
        out_ref[:, :width] = state.astype(BF16)
        out_ref[:, width:] = pack_row(total, states).astype(BF16)

    return launch(
        kernel,
        "group_total",
        shape_of((states, width + LANES), BF16),
        *payloads,
        after=after,
        scratch=[pltpu.VMEM((group, rows - length, columns), BF16)],
    )


def entering_states(payloads, earlier, length, states, width, after=()):
    group = len(payloads)
    rows, columns = payloads[0].shape
    heads = width // DECAY_CHANNELS
    count = len(earlier)

    def kernel(*refs):
        earlier_refs = refs[group : group + count]
        outs = refs[group + count : 2 * group + count]
        held, entering = refs[2 * group + count :]
        gather_blocks(group, states, length, refs[:group], held)
        owner = owners(heads)
        state = jnp.zeros((states, width), F32)
        for ref in reversed(earlier_refs):
            state = jnp.exp(spread_total(ref[:, width:], owner)) * state
            state = state + ref[:, :width].astype(F32)
        for b in range(group):
            entering[b] = state
            if b < group - 1:
                more, packed = block_of(held, b, states, columns, width)
                state = jnp.exp(spread_total(packed, owner)) * state + more
        mine = place(group)
        for k in range(group):
            outs[k][...] = entering[mine ^ k]

    return launch(
        kernel,
        "entering_states",
        [shape_of((states, width), F32)] * group,
        *payloads,
        *earlier,
        after=after,
        scratch=[
            pltpu.VMEM((group, rows - length, columns), BF16),
            pltpu.VMEM((group, states, width), F32),
        ],
    )


def carried_part(maps, still, scale, entering, states, after=()):
    length, channels = still.shape
    group = len(entering)
    width = channels // group
    span = min(width, 512)

    def kernel(maps_ref, still_ref, scale_ref, *refs):
        gated_ref, square_ref, held = refs[group:]
        mine = place(group)
        for k in range(group):
            held[mine ^ k] = refs[k][...]
        c = maps_ref[:, states : 2 * states]
        c_high = c.astype(BF16)
        c_low = (c - c_high.astype(F32)).astype(BF16)
        c = jnp.concatenate([c_high, c_low, c_high], axis=1)
        folded = jnp.zeros(square_ref.shape, F32)
        for at in range(0, channels, span):
            piece, offset = divmod(at, width)
            state = held[piece, :, offset : offset + span]
            high = state.astype(BF16)
            low = (state - high.astype(F32)).astype(BF16)
            carried = jnp.dot(
                c, jnp.concatenate([high, high, low], axis=0), preferred_element_type=F32
            )
            columns = slice(at, at + span)
            gated = still_ref[:, columns] + scale_ref[:, columns] * carried
            gated_ref[:, columns] = gated
            square = gated * gated
            for lane in range(0, span, LANES):
                folded = folded + square[:, lane : lane + LANES]
        square_ref[...] = folded

    return launch(
        kernel,
        "carried_part",
        [shape_of((length, channels), F32), shape_of((length, LANES), F32)],
        maps,
        still,
        scale,
        *entering,
        after=after,
        flops=6 * length * states * channels,
        scratch=[pltpu.VMEM((group, states, width), F32)],
    )


def norm(gated, gain, squares, every):
    length, channels = gated.shape
    count = len(squares)

    def kernel(gated_ref, gain_ref, *refs):
        out_ref = refs[count]
        square = refs[0][...]
        for ref in refs[1:count]:
            square = square + ref[...]
        mean = jnp.sum(square, axis=1, keepdims=True) / every
        factor = jnp.broadcast_to(lax.rsqrt(mean + 1e-05), square.shape)
        for at in range(0, channels, LANES):
            columns = slice(at, at + LANES)
            out_ref[:, columns] = (gated_ref[:, columns] * factor * gain_ref[:, columns]).astype(BF16)

    return launch(
        kernel, "norm", shape_of((length, channels), BF16), gated, gain, *squares
    )


def shared_parts(part):
    if lax.axis_size("tp") == 2:
        return [part, lax.ppermute(part, "tp", [(0, 1), (1, 0)])]
    return [lax.psum(part, "tp")]


def earlier_states(total, group, turns, count, states, width):
    if turns <= UNROLL:
        return [climb_up(total, group, count, steps) for steps in range(1, turns)]
    heads = width // DECAY_CHANNELS

    def one(_, carry):
        travelling, summed, ahead = carry
        travelling = climb_up(travelling, group, count)
        summed = summed + jnp.exp(ahead) * travelling[:, :width].astype(F32)
        more = unpack_row(travelling[:, width : width + heads])
        return travelling, summed, ahead + jnp.repeat(more, DECAY_CHANNELS, axis=1)

    start = (total, jnp.zeros((states, width), F32), jnp.zeros((1, width), F32))
    _, summed, _ = lax.fori_loop(1, turns, one, start)
    return [jnp.concatenate([summed.astype(BF16), jnp.zeros((states, LANES), BF16)], axis=1)]


def per_device(
    queries,
    keys,
    values,
    mixer_input,
    gate,
    step_weight,
    state_weight,
    step_bias,
    decay_rate,
    skip_gain,
    norm_gain,
):
    count = lax.axis_size("ctx")
    length = queries.shape[0]
    channels = mixer_input.shape[1]
    states = state_weight.shape[1] // 2
    group = math.gcd(keys.shape[1] // HD, count)
    turns = count // group
    width = channels // group

    packed = pack_kv(keys, values, group)
    parts = shared_parts(project(mixer_input, step_weight, state_weight, after=packed[:1]))
    blocks = swap(packed, group, count)
    (climb, climb_t, step_t, maps), payloads = block_state(
        parts, step_bias[None], decay_rate[None], mixer_input, queries, states, group
    )
    still, scale = local_part(
        mixer_input, gate, climb, climb_t, step_t, maps, skip_gain[None], states
    )
    own = jnp.stack([tie(blocks[0], [still])] + blocks[1:])
    sent = payloads[:1]
    payloads = swap(payloads, group, count)
    ring = 1 < turns <= UNROLL
    arrived, ready = [], []
    if ring:
        arrived.append(climb_up(own, group, count))
    if ring and turns > 2:
        arrived[0] = tie(arrived[0], sent)
        ready = [arrived[0]]
        arrived.append(climb_up(arrived[0], group, count, first=1))
    total = group_total(payloads, length, states, width, after=ready)
    earlier = earlier_states(total, group, turns, count, states, width)
    state = flash(payloads, length, own=own, chunks=arrived[:-1][:1], after=[total])
    if ring and turns > 3:
        arrived[1] = tie(arrived[1], [state[1]] + earlier[:1] + earlier[:0:-1])
        ready = [arrived[1]]
        for step in range(2, turns - 1):
            arrived.append(climb_up(arrived[-1], group, count, first=step))
    entering = entering_states(payloads, earlier, length, states, width, after=ready)
    if ring and turns > 3:
        state = flash(
            payloads, length, state=state, chunks=arrived[1:-1], base=2, after=entering[:1]
        )
    entering = swap(entering, group, count)
    if turns > 1 and not ring:

        def one(step, carry):
            chunk, state = carry
            chunk = climb_up(chunk, group, count)
            state = flash(payloads, length, state=state, chunks=[chunk], base=jnp.reshape(step, (1,)))
            return chunk, tuple(state)

        chunk, state = lax.fori_loop(1, turns - 1, one, (own, tuple(state)))
        arrived.append(climb_up(chunk, group, count))
    gated, square = carried_part(maps, still, scale, entering, states)
    squares = shared_parts(square)
    if turns == 1:
        outs = flash(payloads, length, own=own, final=True)
    else:
        outs = flash(
            payloads,
            length,
            state=state,
            chunks=arrived[-1:],
            final=True,
            base=turns - 1,
            after=[square],
        )
    attention_out = join(swap(outs, group, count), group)
    mamba_out = norm(gated, norm_gain[None], squares, channels * lax.axis_size("tp"))
    return attention_out, mamba_out


def solution(mesh):
    return jax.shard_map(
        per_device,
        mesh=mesh,
        in_specs=(
            P("ctx", "tp"),
            P("ctx", "tp"),
            P("ctx", "tp"),
            P("ctx", "tp"),
            P("ctx", "tp"),
            P("tp", None),
            P("tp", None),
            P("tp"),
            P("tp"),
            P("tp"),
            P("tp"),
        ),
        out_specs=(P("ctx", "tp"), P("ctx", "tp")),
        check_vma=False,
    )
```

```python
import functools
import math

import jax
import jax.numpy as jnp
from jax import lax
from jax.experimental import pallas as pl
from jax.experimental.pallas import tpu as pltpu
from jax.sharding import PartitionSpec as P

HD = 128
DECAY_CHANNELS = 64
SCAN_TOKENS = 128
LANES = 128
UNROLL = 8
LOG2E = math.log2(math.e)
VMEM_LIMIT = 14 * 1024 * 1024

F32 = jnp.float32
BF16 = jnp.bfloat16


def vmem():
    return pl.BlockSpec(memory_space=pltpu.VMEM)


def hbm():
    return pl.BlockSpec(memory_space=pltpu.HBM)


def launch(kernel, name, out_shape, *inputs, after=(), flops=0, scratch=(), in_specs=None, out_specs=None, grid=None):
    count, skip = len(inputs), len(after)
    single = isinstance(out_shape, jax.ShapeDtypeStruct)
    shapes = [out_shape] if single else list(out_shape)
    size = sum(x.size * x.dtype.itemsize for x in list(inputs) + shapes)

    def body(*refs):
        kernel(*refs[:count], *refs[count + skip :])

    result = pl.pallas_call(
        body,
        **({} if grid is None else {"grid": grid}),
        out_shape=shapes,
        in_specs=(in_specs or [vmem()] * count) + [pl.BlockSpec(memory_space=pl.ANY)] * skip,
        out_specs=out_specs or [vmem()] * len(shapes),
        scratch_shapes=list(scratch),
        compiler_params=pltpu.CompilerParams(vmem_limit_bytes=VMEM_LIMIT),
        cost_estimate=pl.CostEstimate(flops=flops, bytes_accessed=size, transcendentals=0),
        name=name,
    )(*inputs, *after)
    return result[0] if single else result


def place(group):
    return lax.rem(lax.axis_index("ctx"), jnp.int32(group))


def swap(pieces, group, count):
    result = list(pieces)
    for k in reversed(range(1, group)):
        perm = [(i, (i // group) * group + ((i % group) ^ k)) for i in range(count)]
        result[k] = lax.ppermute(pieces[k], "ctx", perm)
    return result


def climb_up(array, group, count, steps=1, first=0):
    perm = [(i, i + group * steps) for i in range(group * first, count - group * steps)]
    return lax.ppermute(array, "ctx", perm)


def shape_of(shape, dtype):
    return jax.ShapeDtypeStruct(shape, dtype)


def tie(array, after):
    return pl.pallas_call(
        lambda *refs: None,
        out_shape=shape_of(array.shape, array.dtype),
        in_specs=[pl.BlockSpec(memory_space=pl.ANY)] * (1 + len(after)),
        out_specs=pl.BlockSpec(memory_space=pl.ANY),
        input_output_aliases={0: 0},
        compiler_params=pltpu.CompilerParams(vmem_limit_bytes=1024 * 1024),
        name="tie",
    )(array, *after)


def pack_kv(keys, values, group):
    length, width = keys.shape
    piece = width // group

    def kernel(k_ref, v_ref, *outs):
        mine = place(group)
        for k in range(group):
            columns = pl.ds(pl.multiple_of((mine ^ k) * piece, piece), piece)
            outs[k][0] = k_ref[:, columns]
            outs[k][1] = v_ref[:, columns]

    return launch(
        kernel,
        "pack_kv",
        [shape_of((2, length, piece), keys.dtype)] * group,
        keys,
        values,
        flops=5000000000,
        grid=(1,),
        in_specs=[pl.BlockSpec((length, width), lambda i: (0, 0))] * 2,
    )


def join(pieces, group):
    length, width = pieces[0].shape

    def kernel(*refs):
        out_ref, sems = refs[group:]
        mine = place(group)
        copies = []
        for k in range(group):
            columns = pl.ds(pl.multiple_of((mine ^ k) * width, width), width)
            copies.append(
                pltpu.make_async_copy(refs[group - 1 - k], out_ref.at[:, columns], sems.at[k])
            )
        for copy in copies:
            copy.start()
        for copy in copies:
            copy.wait()

    return launch(
        kernel,
        "join_heads",
        shape_of((length, width * group), pieces[0].dtype),
        *reversed(pieces),
        out_specs=[hbm()],
        scratch=[pltpu.SemaphoreType.DMA((group,))],
    )


def flash_chunk(q_refs, kv_ref, before, after, extended, own, length):
    group = len(q_refs)
    heads = q_refs[0].shape[1] // HD
    kv_heads = kv_ref.shape[3] // HD
    share = heads // kv_heads
    rows = group * length
    tile = min(rows, 2 * length)
    rate = LOG2E / math.sqrt(HD)
    for kv in range(kv_heads):
        lanes = slice(kv * HD, (kv + 1) * HD)
        keys = kv_ref[:, 0, :, lanes].reshape(rows, HD)
        extended[:, :HD] = kv_ref[:, 1, :, lanes].reshape(rows, HD)
        extended[:, HD:] = jnp.ones((rows, HD), BF16)
        tiles = [
            (h, start)
            for start in range(0, rows, tile)
            for h in range(kv * share, (kv + 1) * share)
        ]

        def score(h, start):
            parts = q_refs[start // length : (start + tile) // length]
            q = [ref[:length, h * HD : (h + 1) * HD] for ref in parts]
            q = jnp.concatenate(q, axis=0) if len(q) > 1 else q[0]
            scores = lax.dot_general(
                q, keys, (((1,), (1,)), ((), ())), preferred_element_type=F32
            )
            if own:
                flip = place(group) * length
                row = (lax.broadcasted_iota(jnp.int32, (tile, rows), 0) + start) ^ flip
                column = lax.broadcasted_iota(jnp.int32, (tile, rows), 1) ^ flip
                scores = jnp.where(column <= row, scores, -1e30)
            return scores

        ahead = score(*tiles[0])
        for n, (h, start) in enumerate(tiles):
            scores = ahead
            if n + 1 < len(tiles):
                ahead = score(*tiles[n + 1])
            here = slice(start, start + tile)
            top = jnp.broadcast_to(jnp.max(scores, axis=1, keepdims=True), (tile, LANES))
            if not own:
                top_before = before[1][h, here]
                top = jnp.maximum(top_before, top)
            across = [top] * (rows // LANES)
            across = jnp.concatenate(across, axis=1) if len(across) > 1 else top
            weights = jnp.exp2((scores - across) * rate).astype(BF16)
            value = jnp.dot(weights, extended[...], preferred_element_type=F32)
            if not own:
                keep = jnp.exp2((top_before - top) * rate)
                value = value + before[0][h, here] * jnp.concatenate([keep, keep], axis=1)
            yield h, start, tile, value
            if after is not None:
                after[0][h, here] = value
                after[1][h, here] = top


def finish_rows(out_refs, h, start, tile, value):
    length = out_refs[0].shape[0]
    result = (value[:, :HD] / value[:, HD:]).astype(BF16)
    for at in range(0, tile, length):
        out_refs[(start + at) // length][:, h * HD : (h + 1) * HD] = result[at : at + length]


def flash(q, length, own=None, state=(), chunks=(), final=False, base=1, after=()):
    group = len(q)
    heads = q[0].shape[1] // HD
    rows = group * length
    fixed = isinstance(base, int)
    has_own = own is not None
    specs = [] if fixed else [pl.BlockSpec(memory_space=pltpu.SMEM)]
    rest = list(q) + ([own] if has_own else []) + list(state) + list(chunks)
    specs = specs + [vmem()] * len(rest)

    def kernel(*refs):
        refs = list(refs)
        first = base if fixed else refs.pop(0)[0]
        q_refs = [refs.pop(0) for _ in range(group)]
        own_ref = refs.pop(0) if has_own else None
        held = None if has_own else (refs.pop(0), refs.pop(0))
        chunk_refs = [refs.pop(0) for _ in range(len(chunks))]
        extended = refs.pop()
        turn = lax.axis_index("ctx") // group
        outs = None if final else tuple(refs)
        if has_own:
            for done in flash_chunk(q_refs, own_ref, None, outs, extended, True, length):
                if final:
                    finish_rows(refs, *done)
            held = outs
        for number, ref in enumerate(chunk_refs):

            @pl.when(turn >= first + number)
            def _(ref=ref, held=held):
                for done in flash_chunk(q_refs, ref, held, outs, extended, False, length):
                    if final:
                        finish_rows(refs, *done)

            if not has_own and number == 0:

                @pl.when(turn < first)
                def _(held=held):
                    for h in range(heads):
                        if final:
                            finish_rows(refs, h, 0, rows, held[0][h])
                        else:
                            outs[0][h] = held[0][h]
                            outs[1][h] = held[1][h]

            held = outs

    if final:
        out_shape = [shape_of((length, heads * HD), BF16)] * group
    else:
        out_shape = [
            shape_of((heads, rows, HD + LANES), F32),
            shape_of((heads, rows, LANES), F32),
        ]
    parts = len(chunks) + has_own
    return launch(
        kernel,
        "flash",
        out_shape,
        *([] if fixed else [base]),
        *rest,
        after=after,
        in_specs=specs,
        flops=4 * heads * rows * rows * HD * parts,
        scratch=[pltpu.VMEM((rows, HD + LANES), BF16)],
    )


def widen(row, lanes):
    extra = lanes - row.shape[1]
    if not extra:
        return row
    return jnp.concatenate([row, jnp.zeros((row.shape[0], extra), row.dtype)], axis=1)


def project(x, step_weight, state_weight, after=()):
    length, channels = x.shape
    heads = step_weight.shape[1]

    def kernel(x_ref, step_ref, map_ref, out_ref):
        x = x_ref[...]
        out_ref[:, :heads] = jnp.dot(x, step_ref[...], preferred_element_type=F32)
        maps = lax.dot_general(
            x, map_ref[...], (((1,), (1,)), ((), ())), preferred_element_type=F32
        )
        out_ref[:, heads:] = widen(maps, LANES)

    return launch(
        kernel,
        "project",
        shape_of((length, heads + LANES), F32),
        x,
        step_weight,
        state_weight.T,
        after=after,
        flops=4 * length * channels * heads,
    )


def owners(heads):
    shape = (LANES, heads * DECAY_CHANNELS)
    head = lax.broadcasted_iota(jnp.int32, shape, 0)
    channel = lax.broadcasted_iota(jnp.int32, shape, 1)
    return (channel // DECAY_CHANNELS == head).astype(BF16)


def pack_row(row, rows):
    high = row.astype(BF16).astype(F32)
    rest = row - high
    middle = rest.astype(BF16).astype(F32)
    low = rest - middle
    return jnp.concatenate([high, middle, low, jnp.zeros((rows - 3, row.shape[1]), F32)], axis=0)


def unpack_row(rows):
    rows = rows.astype(F32)
    return rows[0:1] + rows[1:2] + rows[2:3]


def spread_total(rows, owner):
    wide = jnp.dot(rows, owner, preferred_element_type=F32)
    return wide[0:1] + wide[1:2] + wide[2:3]


def block_state(parts, bias, rate, x, q, states, group, after=()):
    length, channels = x.shape
    every = parts[0].shape[1] - LANES
    heads = bias.shape[1]
    width = channels // group
    columns = q.shape[1] // group
    bands = width // columns
    count = len(parts)

    def kernel(*refs):
        bias_ref, rate_ref, x_ref, q_ref = refs[count : count + 4]
        climb_ref, climb_t_ref, step_t_ref, maps_ref = refs[count + 4 : count + 8]
        outs = refs[count + 8 : count + 8 + group]
        held = refs[count + 8 + group]
        summed = refs[0][...]
        for ref in refs[1:count]:
            summed = summed + ref[...]
        shift = lax.rem(every - lax.axis_index("tp") * heads, jnp.int32(every))
        raw = pltpu.roll(summed[:, :every], shift, 1) + widen(bias_ref[...], every)
        step = jnp.maximum(raw, 0.0) + jnp.log1p(jnp.exp(-jnp.abs(raw)))
        log_decay = -widen(rate_ref[...], every) * step
        row = lax.broadcasted_iota(jnp.int32, (length, length), 0)
        column = lax.broadcasted_iota(jnp.int32, (length, length), 1)
        lower = (column <= row).astype(F32)
        climb = jnp.dot(
            lower, log_decay, precision=lax.Precision.HIGHEST, preferred_element_type=F32
        )
        maps = summed[:, every:]
        climb_ref[...] = climb * LOG2E
        maps_ref[...] = maps
        climb_t = climb.T
        step_t = step.T
        climb_t_ref[...] = climb_t[:heads] * LOG2E
        step_t_ref[...] = step_t[:heads]
        b_t = maps.T[:states]
        weight_t = jnp.exp(climb_t[:, length - 1 :] - climb_t) * step_t
        bundle = 4
        span = bundle * DECAY_CHANNELS
        owner = lax.broadcasted_iota(jnp.int32, (1, span), 1) // DECAY_CHANNELS
        for at in range(0, heads, bundle):
            feed = [b_t * weight_t[at + i : at + i + 1] for i in range(bundle)]
            feed = jnp.concatenate(feed, axis=0).astype(BF16)
            start = at * DECAY_CHANNELS
            product = jnp.dot(feed, x_ref[:, start : start + span], preferred_element_type=F32)
            state = product[:states]
            for i in range(1, bundle):
                state = jnp.where(owner == i, product[i * states : (i + 1) * states], state)
            piece, offset = divmod(start, width)
            band, offset = divmod(offset, columns)
            rows = slice(band * states, (band + 1) * states)
            held[piece, rows, offset : offset + span] = state.astype(BF16)
        totals = pack_row(climb[length - 1 :], states)
        for piece in range(group):
            at = piece * (heads // group)
            here = totals if not at else pltpu.roll(totals, every - at, 1)
            held[piece, bands * states :, :] = widen(here[:, :LANES], columns).astype(BF16)
        mine = place(group)
        for k in range(group):
            here = pl.ds(pl.multiple_of((mine ^ k) * columns, columns), columns)
            outs[k][:length] = q_ref[:, here]
            outs[k][length:] = held[mine ^ k]

    payload = shape_of((length + (bands + 1) * states, columns), BF16)
    result = launch(
        kernel,
        "block_state",
        [
            shape_of((length, every), F32),
            shape_of((heads, length), F32),
            shape_of((heads, length), F32),
            shape_of((length, LANES), F32),
        ]
        + [payload] * group,
        *parts,
        bias,
        rate,
        x,
        q,
        after=after,
        flops=32 * length * states * channels,
        scratch=[pltpu.VMEM((group, (bands + 1) * states, columns), BF16)],
    )
    return result[:4], result[4:]


def local_part(x, gate, climb, climb_t, step_t, maps, skip, states, after=()):
    length, channels = x.shape
    heads = channels // DECAY_CHANNELS

    def kernel(
        x_ref, gate_ref, climb_ref, climb_t_ref, step_t_ref, maps_ref, skip_ref, still_ref, scale_ref
    ):
        maps = maps_ref[...]
        inner = lax.dot_general(
            maps[:, states : 2 * states],
            maps[:, :states],
            (((1,), (1,)), ((), ())),
            precision=lax.Precision.HIGHEST,
            preferred_element_type=F32,
        )
        row = lax.broadcasted_iota(jnp.int32, (length, length), 0)
        column = lax.broadcasted_iota(jnp.int32, (length, length), 1)
        inner = jnp.where(column <= row, inner, 0.0)
        left = lax.broadcasted_iota(jnp.int32, (length, LANES), 1) < DECAY_CHANNELS

        for j in range(0, heads, 2):
            columns = slice(j * DECAY_CHANNELS, j * DECAY_CHANNELS + LANES)
            x = x_ref[:, columns]
            wide = [jnp.broadcast_to(climb_ref[:, i : i + 1], (length, length)) for i in (j, j + 1)]
            mixed = []
            for i in (j, j + 1):
                fall = jnp.minimum(wide[i - j] - climb_t_ref[i : i + 1], 0.0)
                mixed.append((inner * jnp.exp2(fall) * step_t_ref[i : i + 1]).astype(BF16))
            zero = jnp.zeros_like(x)
            feeds = jnp.concatenate([jnp.where(left, x, zero), jnp.where(left, zero, x)], axis=0)
            local = jnp.dot(jnp.concatenate(mixed, axis=1), feeds, preferred_element_type=F32)
            gain = jnp.where(left[:1], skip_ref[:, j : j + 1], skip_ref[:, j + 1 : j + 2])
            grown = jnp.exp2(jnp.where(left, wide[0], wide[1]))
            gate = gate_ref[:, columns].astype(F32)
            half = 0.5 * gate
            silu = half + half * jnp.tanh(half)
            still_ref[:, columns] = (local + gain * x.astype(F32)) * silu
            scale_ref[:, columns] = grown * silu

    return launch(
        kernel,
        "local_part",
        [shape_of((length, channels), F32)] * 2,
        x,
        gate,
        climb,
        climb_t,
        step_t,
        maps,
        skip,
        after=after,
        flops=4 * length * length * channels,
    )


def gather_blocks(group, states, length, refs, held):
    mine = place(group)
    for k in range(group):
        held[mine ^ k] = refs[k][length:]


def block_of(held, b, states, columns, width):
    bands = width // columns
    rows = [held[b, i * states : (i + 1) * states] for i in range(bands)]
    state = jnp.concatenate(rows, axis=1) if bands > 1 else rows[0]
    return state.astype(F32), held[b, bands * states :, :LANES]


def group_total(payloads, length, states, width, after=()):
    group = len(payloads)
    rows, columns = payloads[0].shape
    heads = width // DECAY_CHANNELS

    def kernel(*refs):
        out_ref, held = refs[group:]
        gather_blocks(group, states, length, refs[:group], held)
        owner = owners(heads)
        state, packed = block_of(held, 0, states, columns, width)
        total = unpack_row(packed)
        for b in range(1, group):
            more, packed = block_of(held, b, states, columns, width)
            state = jnp.exp(spread_total(packed, owner)) * state + more
            total = total + unpack_row(packed)
        out_ref[:, :width] = state.astype(BF16)
        out_ref[:, width:] = pack_row(total, states).astype(BF16)

    return launch(
        kernel,
        "group_total",
        shape_of((states, width + LANES), BF16),
        *payloads,
        after=after,
        scratch=[pltpu.VMEM((group, rows - length, columns), BF16)],
    )


def entering_states(payloads, earlier, length, states, width, after=()):
    group = len(payloads)
    rows, columns = payloads[0].shape
    heads = width // DECAY_CHANNELS
    count = len(earlier)

    def kernel(*refs):
        earlier_refs = refs[group : group + count]
        outs = refs[group + count : 2 * group + count]
        held, entering = refs[2 * group + count :]
        gather_blocks(group, states, length, refs[:group], held)
        owner = owners(heads)
        state = jnp.zeros((states, width), F32)
        for ref in reversed(earlier_refs):
            state = jnp.exp(spread_total(ref[:, width:], owner)) * state
            state = state + ref[:, :width].astype(F32)
        for b in range(group):
            entering[b] = state
            if b < group - 1:
                more, packed = block_of(held, b, states, columns, width)
                state = jnp.exp(spread_total(packed, owner)) * state + more
        mine = place(group)
        for k in range(group):
            outs[k][...] = entering[mine ^ k]

    return launch(
        kernel,
        "entering_states",
        [shape_of((states, width), F32)] * group,
        *payloads,
        *earlier,
        after=after,
        scratch=[
            pltpu.VMEM((group, rows - length, columns), BF16),
            pltpu.VMEM((group, states, width), F32),
        ],
    )


def carried_part(maps, still, scale, entering, states, after=()):
    length, channels = still.shape
    group = len(entering)
    width = channels // group
    span = min(width, 512)

    def kernel(maps_ref, still_ref, scale_ref, *refs):
        gated_ref, square_ref, held = refs[group:]
        mine = place(group)
        for k in range(group):
            held[mine ^ k] = refs[k][...]
        c = maps_ref[:, states : 2 * states]
        c_high = c.astype(BF16)
        c_low = (c - c_high.astype(F32)).astype(BF16)
        c = jnp.concatenate([c_high, c_low, c_high], axis=1)
        folded = jnp.zeros(square_ref.shape, F32)
        for at in range(0, channels, span):
            piece, offset = divmod(at, width)
            state = held[piece, :, offset : offset + span]
            high = state.astype(BF16)
            low = (state - high.astype(F32)).astype(BF16)
            carried = jnp.dot(
                c, jnp.concatenate([high, high, low], axis=0), preferred_element_type=F32
            )
            columns = slice(at, at + span)
            gated = still_ref[:, columns] + scale_ref[:, columns] * carried
            gated_ref[:, columns] = gated
            square = gated * gated
            for lane in range(0, span, LANES):
                folded = folded + square[:, lane : lane + LANES]
        square_ref[...] = folded

    return launch(
        kernel,
        "carried_part",
        [shape_of((length, channels), F32), shape_of((length, LANES), F32)],
        maps,
        still,
        scale,
        *entering,
        after=after,
        flops=6 * length * states * channels,
        scratch=[pltpu.VMEM((group, states, width), F32)],
    )


def norm(gated, gain, squares, every):
    length, channels = gated.shape
    count = len(squares)

    def kernel(gated_ref, gain_ref, *refs):
        out_ref = refs[count]
        square = refs[0][...]
        for ref in refs[1:count]:
            square = square + ref[...]
        mean = jnp.sum(square, axis=1, keepdims=True) / every
        factor = jnp.broadcast_to(lax.rsqrt(mean + 1e-05), square.shape)
        for at in range(0, channels, LANES):
            columns = slice(at, at + LANES)
            out_ref[:, columns] = (gated_ref[:, columns] * factor * gain_ref[:, columns]).astype(BF16)

    return launch(
        kernel, "norm", shape_of((length, channels), BF16), gated, gain, *squares
    )


def shared_parts(part):
    if lax.axis_size("tp") == 2:
        return [part, lax.ppermute(part, "tp", [(0, 1), (1, 0)])]
    return [lax.psum(part, "tp")]


def earlier_states(total, group, turns, count, states, width):
    if turns <= UNROLL:
        return [climb_up(total, group, count, steps) for steps in range(1, turns)]
    heads = width // DECAY_CHANNELS

    def one(_, carry):
        travelling, summed, ahead = carry
        travelling = climb_up(travelling, group, count)
        summed = summed + jnp.exp(ahead) * travelling[:, :width].astype(F32)
        more = unpack_row(travelling[:, width : width + heads])
        return travelling, summed, ahead + jnp.repeat(more, DECAY_CHANNELS, axis=1)

    start = (total, jnp.zeros((states, width), F32), jnp.zeros((1, width), F32))
    _, summed, _ = lax.fori_loop(1, turns, one, start)
    return [jnp.concatenate([summed.astype(BF16), jnp.zeros((states, LANES), BF16)], axis=1)]


def per_device(
    queries,
    keys,
    values,
    mixer_input,
    gate,
    step_weight,
    state_weight,
    step_bias,
    decay_rate,
    skip_gain,
    norm_gain,
):
    count = lax.axis_size("ctx")
    length = queries.shape[0]
    channels = mixer_input.shape[1]
    states = state_weight.shape[1] // 2
    group = math.gcd(keys.shape[1] // HD, count)
    turns = count // group
    width = channels // group

    packed = pack_kv(keys, values, group)
    parts = shared_parts(project(mixer_input, step_weight, state_weight, after=packed[:1]))
    blocks = swap(packed, group, count)
    (climb, climb_t, step_t, maps), payloads = block_state(
        parts, step_bias[None], decay_rate[None], mixer_input, queries, states, group
    )
    still, scale = local_part(
        mixer_input, gate, climb, climb_t, step_t, maps, skip_gain[None], states
    )
    own = jnp.stack([tie(blocks[0], [still])] + blocks[1:])
    sent = payloads[:1]
    payloads = swap(payloads, group, count)
    ring = 1 < turns <= UNROLL
    arrived, ready = [], []
    if ring:
        arrived.append(climb_up(own, group, count))
    if ring and turns > 2:
        arrived[0] = tie(arrived[0], sent)
        ready = [arrived[0]]
        arrived.append(climb_up(arrived[0], group, count, first=1))
    total = group_total(payloads, length, states, width, after=ready)
    earlier = earlier_states(total, group, turns, count, states, width)
    state = flash(payloads, length, own=own, chunks=arrived[:-1][:1], after=[total])
    if ring and turns > 3:
        arrived[1] = tie(arrived[1], [state[1]] + earlier[:1] + earlier[:0:-1])
        ready = [arrived[1]]
        for step in range(2, turns - 1):
            arrived.append(climb_up(arrived[-1], group, count, first=step))
    entering = entering_states(payloads, earlier, length, states, width, after=ready)
    if ring and turns > 3:
        state = flash(
            payloads, length, state=state, chunks=arrived[1:-1], base=2, after=entering[:1]
        )
    entering = swap(entering, group, count)
    if turns > 1 and not ring:

        def one(step, carry):
            chunk, state = carry
            chunk = climb_up(chunk, group, count)
            state = flash(payloads, length, state=state, chunks=[chunk], base=jnp.reshape(step, (1,)))
            return chunk, tuple(state)

        chunk, state = lax.fori_loop(1, turns - 1, one, (own, tuple(state)))
        arrived.append(climb_up(chunk, group, count))
    gated, square = carried_part(maps, still, scale, entering, states)
    mamba_out = norm(
        gated, norm_gain[None], shared_parts(square), channels * lax.axis_size("tp")
    )
    if turns == 1:
        outs = flash(payloads, length, own=own, final=True)
    else:
        outs = flash(
            payloads, length, state=state, chunks=arrived[-1:], final=True, base=turns - 1
        )
    return join(swap(outs, group, count), group), mamba_out


def solution(mesh):
    return jax.shard_map(
        per_device,
        mesh=mesh,
        in_specs=(
            P("ctx", "tp"),
            P("ctx", "tp"),
            P("ctx", "tp"),
            P("ctx", "tp"),
            P("ctx", "tp"),
            P("tp", None),
            P("tp", None),
            P("tp"),
            P("tp"),
            P("tp"),
            P("tp"),
        ),
        out_specs=(P("ctx", "tp"), P("ctx", "tp")),
        check_vma=False,
    )
```

```python
import functools
import math

import jax
import jax.numpy as jnp
from jax import lax
from jax.experimental import pallas as pl
from jax.experimental.pallas import tpu as pltpu
from jax.sharding import PartitionSpec as P

HD = 128
DECAY_CHANNELS = 64
SCAN_TOKENS = 128
LANES = 128
UNROLL = 8
LOG2E = math.log2(math.e)
VMEM_LIMIT = 14 * 1024 * 1024

F32 = jnp.float32
BF16 = jnp.bfloat16


def vmem():
    return pl.BlockSpec(memory_space=pltpu.VMEM)


def hbm():
    return pl.BlockSpec(memory_space=pltpu.HBM)


def launch(kernel, name, out_shape, *inputs, after=(), flops=0, scratch=(), in_specs=None, out_specs=None, grid=None):
    count, skip = len(inputs), len(after)
    single = isinstance(out_shape, jax.ShapeDtypeStruct)
    shapes = [out_shape] if single else list(out_shape)
    size = sum(x.size * x.dtype.itemsize for x in list(inputs) + shapes)

    def body(*refs):
        kernel(*refs[:count], *refs[count + skip :])

    result = pl.pallas_call(
        body,
        **({} if grid is None else {"grid": grid}),
        out_shape=shapes,
        in_specs=(in_specs or [vmem()] * count) + [pl.BlockSpec(memory_space=pl.ANY)] * skip,
        out_specs=out_specs or [vmem()] * len(shapes),
        scratch_shapes=list(scratch),
        compiler_params=pltpu.CompilerParams(vmem_limit_bytes=VMEM_LIMIT),
        cost_estimate=pl.CostEstimate(flops=flops, bytes_accessed=size, transcendentals=0),
        name=name,
    )(*inputs, *after)
    return result[0] if single else result


def place(group):
    return lax.rem(lax.axis_index("ctx"), jnp.int32(group))


def swap(pieces, group, count):
    result = list(pieces)
    for k in reversed(range(1, group)):
        perm = [(i, (i // group) * group + ((i % group) ^ k)) for i in range(count)]
        result[k] = lax.ppermute(pieces[k], "ctx", perm)
    return result


def climb_up(array, group, count, steps=1, first=0):
    perm = [(i, i + group * steps) for i in range(group * first, count - group * steps)]
    return lax.ppermute(array, "ctx", perm)


def shape_of(shape, dtype):
    return jax.ShapeDtypeStruct(shape, dtype)


def tie(array, after):
    return pl.pallas_call(
        lambda *refs: None,
        out_shape=shape_of(array.shape, array.dtype),
        in_specs=[pl.BlockSpec(memory_space=pl.ANY)] * (1 + len(after)),
        out_specs=pl.BlockSpec(memory_space=pl.ANY),
        input_output_aliases={0: 0},
        compiler_params=pltpu.CompilerParams(vmem_limit_bytes=1024 * 1024),
        name="tie",
    )(array, *after)


def pack_kv(keys, values, group):
    length, width = keys.shape
    piece = width // group

    def kernel(k_ref, v_ref, *outs):
        mine = place(group)
        for k in range(group):
            columns = pl.ds(pl.multiple_of((mine ^ k) * piece, piece), piece)
            outs[k][0] = k_ref[:, columns]
            outs[k][1] = v_ref[:, columns]

    return launch(
        kernel,
        "pack_kv",
        [shape_of((2, length, piece), keys.dtype)] * group,
        keys,
        values,
        flops=5000000000,
        grid=(1,),
        in_specs=[pl.BlockSpec((length, width), lambda i: (0, 0))] * 2,
    )


def join(pieces, group):
    length, width = pieces[0].shape

    def kernel(*refs):
        out_ref, sems = refs[group:]
        mine = place(group)
        copies = []
        for k in range(group):
            columns = pl.ds(pl.multiple_of((mine ^ k) * width, width), width)
            copies.append(
                pltpu.make_async_copy(refs[group - 1 - k], out_ref.at[:, columns], sems.at[k])
            )
        for copy in copies:
            copy.start()
        for copy in copies:
            copy.wait()

    return launch(
        kernel,
        "join_heads",
        shape_of((length, width * group), pieces[0].dtype),
        *reversed(pieces),
        out_specs=[hbm()],
        scratch=[pltpu.SemaphoreType.DMA((group,))],
    )


def flash_chunk(q_refs, kv_ref, before, after, extended, own, length):
    group = len(q_refs)
    heads = q_refs[0].shape[1] // HD
    kv_heads = kv_ref.shape[3] // HD
    share = heads // kv_heads
    rows = group * length
    tile = min(rows, 2 * length)
    rate = LOG2E / math.sqrt(HD)
    for kv in range(kv_heads):
        lanes = slice(kv * HD, (kv + 1) * HD)
        keys = kv_ref[:, 0, :, lanes].reshape(rows, HD)
        extended[:, :HD] = kv_ref[:, 1, :, lanes].reshape(rows, HD)
        extended[:, HD:] = jnp.ones((rows, HD), BF16)
        tiles = [
            (h, start)
            for start in range(0, rows, tile)
            for h in range(kv * share, (kv + 1) * share)
        ]

        def score(h, start):
            parts = q_refs[start // length : (start + tile) // length]
            q = [ref[:length, h * HD : (h + 1) * HD] for ref in parts]
            q = jnp.concatenate(q, axis=0) if len(q) > 1 else q[0]
            scores = lax.dot_general(
                q, keys, (((1,), (1,)), ((), ())), preferred_element_type=F32
            )
            if own:
                flip = place(group) * length
                row = (lax.broadcasted_iota(jnp.int32, (tile, rows), 0) + start) ^ flip
                column = lax.broadcasted_iota(jnp.int32, (tile, rows), 1) ^ flip
                scores = jnp.where(column <= row, scores, -1e30)
            return scores

        ahead = score(*tiles[0])
        for n, (h, start) in enumerate(tiles):
            scores = ahead
            if n + 1 < len(tiles):
                ahead = score(*tiles[n + 1])
            here = slice(start, start + tile)
            top = jnp.broadcast_to(jnp.max(scores, axis=1, keepdims=True), (tile, LANES))
            if not own:
                top_before = before[1][h, here]
                top = jnp.maximum(top_before, top)
            across = [top] * (rows // LANES)
            across = jnp.concatenate(across, axis=1) if len(across) > 1 else top
            weights = jnp.exp2((scores - across) * rate).astype(BF16)
            value = jnp.dot(weights, extended[...], preferred_element_type=F32)
            if not own:
                keep = jnp.exp2((top_before - top) * rate)
                value = value + before[0][h, here] * jnp.concatenate([keep, keep], axis=1)
            yield h, start, tile, value
            if after is not None:
                after[0][h, here] = value
                after[1][h, here] = top


def finish_rows(out_refs, h, start, tile, value):
    length = out_refs[0].shape[0]
    result = (value[:, :HD] / value[:, HD:]).astype(BF16)
    for at in range(0, tile, length):
        out_refs[(start + at) // length][:, h * HD : (h + 1) * HD] = result[at : at + length]


def flash(q, length, own=None, state=(), chunks=(), final=False, base=1, after=()):
    group = len(q)
    heads = q[0].shape[1] // HD
    rows = group * length
    fixed = isinstance(base, int)
    has_own = own is not None
    specs = [] if fixed else [pl.BlockSpec(memory_space=pltpu.SMEM)]
    rest = list(q) + ([own] if has_own else []) + list(state) + list(chunks)
    specs = specs + [vmem()] * len(rest)

    def kernel(*refs):
        refs = list(refs)
        first = base if fixed else refs.pop(0)[0]
        q_refs = [refs.pop(0) for _ in range(group)]
        own_ref = refs.pop(0) if has_own else None
        held = None if has_own else (refs.pop(0), refs.pop(0))
        chunk_refs = [refs.pop(0) for _ in range(len(chunks))]
        extended = refs.pop()
        turn = lax.axis_index("ctx") // group
        outs = None if final else tuple(refs)
        if has_own:
            for done in flash_chunk(q_refs, own_ref, None, outs, extended, True, length):
                if final:
                    finish_rows(refs, *done)
            held = outs
        for number, ref in enumerate(chunk_refs):

            @pl.when(turn >= first + number)
            def _(ref=ref, held=held):
                for done in flash_chunk(q_refs, ref, held, outs, extended, False, length):
                    if final:
                        finish_rows(refs, *done)

            if not has_own and number == 0:

                @pl.when(turn < first)
                def _(held=held):
                    for h in range(heads):
                        if final:
                            finish_rows(refs, h, 0, rows, held[0][h])
                        else:
                            outs[0][h] = held[0][h]
                            outs[1][h] = held[1][h]

            held = outs

    if final:
        out_shape = [shape_of((length, heads * HD), BF16)] * group
    else:
        out_shape = [
            shape_of((heads, rows, HD + LANES), F32),
            shape_of((heads, rows, LANES), F32),
        ]
    parts = len(chunks) + has_own
    return launch(
        kernel,
        "flash",
        out_shape,
        *([] if fixed else [base]),
        *rest,
        after=after,
        in_specs=specs,
        flops=4 * heads * rows * rows * HD * parts,
        scratch=[pltpu.VMEM((rows, HD + LANES), BF16)],
    )


def widen(row, lanes):
    extra = lanes - row.shape[1]
    if not extra:
        return row
    return jnp.concatenate([row, jnp.zeros((row.shape[0], extra), row.dtype)], axis=1)


def project(x, step_weight, state_weight, after=()):
    length, channels = x.shape
    heads = step_weight.shape[1]

    def kernel(x_ref, step_ref, map_ref, out_ref):
        x = x_ref[...]
        out_ref[:, :heads] = jnp.dot(x, step_ref[...], preferred_element_type=F32)
        maps = lax.dot_general(
            x, map_ref[...], (((1,), (1,)), ((), ())), preferred_element_type=F32
        )
        out_ref[:, heads:] = widen(maps, LANES)

    return launch(
        kernel,
        "project",
        shape_of((length, heads + LANES), F32),
        x,
        step_weight,
        state_weight.T,
        after=after,
        flops=4 * length * channels * heads,
    )


def owners(heads):
    shape = (LANES, heads * DECAY_CHANNELS)
    head = lax.broadcasted_iota(jnp.int32, shape, 0)
    channel = lax.broadcasted_iota(jnp.int32, shape, 1)
    return (channel // DECAY_CHANNELS == head).astype(BF16)


def pack_row(row, rows):
    high = row.astype(BF16).astype(F32)
    rest = row - high
    middle = rest.astype(BF16).astype(F32)
    low = rest - middle
    return jnp.concatenate([high, middle, low, jnp.zeros((rows - 3, row.shape[1]), F32)], axis=0)


def unpack_row(rows):
    rows = rows.astype(F32)
    return rows[0:1] + rows[1:2] + rows[2:3]


def spread_total(rows, owner):
    wide = jnp.dot(rows, owner, preferred_element_type=F32)
    return wide[0:1] + wide[1:2] + wide[2:3]


def block_state(parts, bias, rate, x, q, states, group, after=()):
    length, channels = x.shape
    every = parts[0].shape[1] - LANES
    heads = bias.shape[1]
    width = channels // group
    columns = q.shape[1] // group
    bands = width // columns
    count = len(parts)

    def kernel(*refs):
        bias_ref, rate_ref, x_ref, q_ref = refs[count : count + 4]
        climb_ref, climb_t_ref, step_t_ref, maps_ref = refs[count + 4 : count + 8]
        outs = refs[count + 8 : count + 8 + group]
        held = refs[count + 8 + group]
        summed = refs[0][...]
        for ref in refs[1:count]:
            summed = summed + ref[...]
        shift = lax.rem(every - lax.axis_index("tp") * heads, jnp.int32(every))
        raw = pltpu.roll(summed[:, :every], shift, 1) + widen(bias_ref[...], every)
        step = jnp.maximum(raw, 0.0) + jnp.log1p(jnp.exp(-jnp.abs(raw)))
        log_decay = -widen(rate_ref[...], every) * step
        row = lax.broadcasted_iota(jnp.int32, (length, length), 0)
        column = lax.broadcasted_iota(jnp.int32, (length, length), 1)
        lower = (column <= row).astype(F32)
        climb = jnp.dot(
            lower, log_decay, precision=lax.Precision.HIGHEST, preferred_element_type=F32
        )
        maps = summed[:, every:]
        climb_ref[...] = climb * LOG2E
        maps_ref[...] = maps
        climb_t = climb.T
        step_t = step.T
        climb_t_ref[...] = climb_t[:heads] * LOG2E
        step_t_ref[...] = step_t[:heads]
        b_t = maps.T[:states]
        weight_t = jnp.exp(climb_t[:, length - 1 :] - climb_t) * step_t
        bundle = 4
        span = bundle * DECAY_CHANNELS
        owner = lax.broadcasted_iota(jnp.int32, (1, span), 1) // DECAY_CHANNELS
        for at in range(0, heads, bundle):
            feed = [b_t * weight_t[at + i : at + i + 1] for i in range(bundle)]
            feed = jnp.concatenate(feed, axis=0).astype(BF16)
            start = at * DECAY_CHANNELS
            product = jnp.dot(feed, x_ref[:, start : start + span], preferred_element_type=F32)
            state = product[:states]
            for i in range(1, bundle):
                state = jnp.where(owner == i, product[i * states : (i + 1) * states], state)
            piece, offset = divmod(start, width)
            band, offset = divmod(offset, columns)
            rows = slice(band * states, (band + 1) * states)
            held[piece, rows, offset : offset + span] = state.astype(BF16)
        totals = pack_row(climb[length - 1 :], states)
        for piece in range(group):
            at = piece * (heads // group)
            here = totals if not at else pltpu.roll(totals, every - at, 1)
            held[piece, bands * states :, :] = widen(here[:, :LANES], columns).astype(BF16)
        mine = place(group)
        for k in range(group):
            here = pl.ds(pl.multiple_of((mine ^ k) * columns, columns), columns)
            outs[k][:length] = q_ref[:, here]
            outs[k][length:] = held[mine ^ k]

    payload = shape_of((length + (bands + 1) * states, columns), BF16)
    result = launch(
        kernel,
        "block_state",
        [
            shape_of((length, every), F32),
            shape_of((heads, length), F32),
            shape_of((heads, length), F32),
            shape_of((length, LANES), F32),
        ]
        + [payload] * group,
        *parts,
        bias,
        rate,
        x,
        q,
        after=after,
        flops=32 * length * states * channels,
        scratch=[pltpu.VMEM((group, (bands + 1) * states, columns), BF16)],
    )
    return result[:4], result[4:]


def local_part(x, gate, climb, climb_t, step_t, maps, skip, states, after=()):
    length, channels = x.shape
    heads = channels // DECAY_CHANNELS

    def kernel(
        x_ref, gate_ref, climb_ref, climb_t_ref, step_t_ref, maps_ref, skip_ref, still_ref, scale_ref
    ):
        maps = maps_ref[...]
        inner = lax.dot_general(
            maps[:, states : 2 * states],
            maps[:, :states],
            (((1,), (1,)), ((), ())),
            precision=lax.Precision.HIGHEST,
            preferred_element_type=F32,
        )
        row = lax.broadcasted_iota(jnp.int32, (length, length), 0)
        column = lax.broadcasted_iota(jnp.int32, (length, length), 1)
        inner = jnp.where(column <= row, inner, 0.0)
        left = lax.broadcasted_iota(jnp.int32, (length, LANES), 1) < DECAY_CHANNELS

        for j in range(0, heads, 2):
            columns = slice(j * DECAY_CHANNELS, j * DECAY_CHANNELS + LANES)
            x = x_ref[:, columns]
            wide = [jnp.broadcast_to(climb_ref[:, i : i + 1], (length, length)) for i in (j, j + 1)]
            mixed = []
            for i in (j, j + 1):
                fall = jnp.minimum(wide[i - j] - climb_t_ref[i : i + 1], 0.0)
                mixed.append((inner * jnp.exp2(fall) * step_t_ref[i : i + 1]).astype(BF16))
            zero = jnp.zeros_like(x)
            feeds = jnp.concatenate([jnp.where(left, x, zero), jnp.where(left, zero, x)], axis=0)
            local = jnp.dot(jnp.concatenate(mixed, axis=1), feeds, preferred_element_type=F32)
            gain = jnp.where(left[:1], skip_ref[:, j : j + 1], skip_ref[:, j + 1 : j + 2])
            grown = jnp.exp2(jnp.where(left, wide[0], wide[1]))
            gate = gate_ref[:, columns].astype(F32)
            half = 0.5 * gate
            silu = half + half * jnp.tanh(half)
            still_ref[:, columns] = (local + gain * x.astype(F32)) * silu
            scale_ref[:, columns] = grown * silu

    return launch(
        kernel,
        "local_part",
        [shape_of((length, channels), F32)] * 2,
        x,
        gate,
        climb,
        climb_t,
        step_t,
        maps,
        skip,
        after=after,
        flops=4 * length * length * channels,
    )


def gather_blocks(group, states, length, refs, held):
    mine = place(group)
    for k in range(group):
        held[mine ^ k] = refs[k][length:]


def block_of(held, b, states, columns, width):
    bands = width // columns
    rows = [held[b, i * states : (i + 1) * states] for i in range(bands)]
    state = jnp.concatenate(rows, axis=1) if bands > 1 else rows[0]
    return state.astype(F32), held[b, bands * states :, :LANES]


def group_total(payloads, length, states, width, after=()):
    group = len(payloads)
    rows, columns = payloads[0].shape
    heads = width // DECAY_CHANNELS

    def kernel(*refs):
        out_ref, held = refs[group:]
        gather_blocks(group, states, length, refs[:group], held)
        owner = owners(heads)
        state, packed = block_of(held, 0, states, columns, width)
        total = unpack_row(packed)
        for b in range(1, group):
            more, packed = block_of(held, b, states, columns, width)
            state = jnp.exp(spread_total(packed, owner)) * state + more
            total = total + unpack_row(packed)
        out_ref[:, :width] = state.astype(BF16)
        out_ref[:, width:] = pack_row(total, states).astype(BF16)

    return launch(
        kernel,
        "group_total",
        shape_of((states, width + LANES), BF16),
        *payloads,
        after=after,
        scratch=[pltpu.VMEM((group, rows - length, columns), BF16)],
    )


def entering_states(payloads, earlier, length, states, width, after=()):
    group = len(payloads)
    rows, columns = payloads[0].shape
    heads = width // DECAY_CHANNELS
    count = len(earlier)

    def kernel(*refs):
        earlier_refs = refs[group : group + count]
        outs = refs[group + count : 2 * group + count]
        held, entering = refs[2 * group + count :]
        gather_blocks(group, states, length, refs[:group], held)
        owner = owners(heads)
        state = jnp.zeros((states, width), F32)
        for ref in reversed(earlier_refs):
            state = jnp.exp(spread_total(ref[:, width:], owner)) * state
            state = state + ref[:, :width].astype(F32)
        for b in range(group):
            entering[b] = state
            if b < group - 1:
                more, packed = block_of(held, b, states, columns, width)
                state = jnp.exp(spread_total(packed, owner)) * state + more
        mine = place(group)
        for k in range(group):
            outs[k][...] = entering[mine ^ k]

    return launch(
        kernel,
        "entering_states",
        [shape_of((states, width), F32)] * group,
        *payloads,
        *earlier,
        after=after,
        scratch=[
            pltpu.VMEM((group, rows - length, columns), BF16),
            pltpu.VMEM((group, states, width), F32),
        ],
    )


def carried_part(maps, still, scale, entering, states, after=()):
    length, channels = still.shape
    group = len(entering)
    width = channels // group
    span = min(width, 512)

    def kernel(maps_ref, still_ref, scale_ref, *refs):
        gated_ref, square_ref, held = refs[group:]
        mine = place(group)
        for k in range(group):
            held[mine ^ k] = refs[k][...]
        c = maps_ref[:, states : 2 * states]
        c_high = c.astype(BF16)
        c_low = (c - c_high.astype(F32)).astype(BF16)
        c = jnp.concatenate([c_high, c_low, c_high], axis=1)
        folded = jnp.zeros(square_ref.shape, F32)
        for at in range(0, channels, span):
            piece, offset = divmod(at, width)
            state = held[piece, :, offset : offset + span]
            high = state.astype(BF16)
            low = (state - high.astype(F32)).astype(BF16)
            carried = jnp.dot(
                c, jnp.concatenate([high, high, low], axis=0), preferred_element_type=F32
            )
            columns = slice(at, at + span)
            gated = still_ref[:, columns] + scale_ref[:, columns] * carried
            gated_ref[:, columns] = gated
            square = gated * gated
            for lane in range(0, span, LANES):
                folded = folded + square[:, lane : lane + LANES]
        square_ref[...] = folded

    return launch(
        kernel,
        "carried_part",
        [shape_of((length, channels), F32), shape_of((length, LANES), F32)],
        maps,
        still,
        scale,
        *entering,
        after=after,
        flops=6 * length * states * channels,
        scratch=[pltpu.VMEM((group, states, width), F32)],
    )


def norm(gated, gain, squares, every):
    length, channels = gated.shape
    count = len(squares)

    def kernel(gated_ref, gain_ref, *refs):
        out_ref = refs[count]
        square = refs[0][...]
        for ref in refs[1:count]:
            square = square + ref[...]
        mean = jnp.sum(square, axis=1, keepdims=True) / every
        factor = jnp.broadcast_to(lax.rsqrt(mean + 1e-05), square.shape)
        for at in range(0, channels, LANES):
            columns = slice(at, at + LANES)
            out_ref[:, columns] = (gated_ref[:, columns] * factor * gain_ref[:, columns]).astype(BF16)

    return launch(
        kernel, "norm", shape_of((length, channels), BF16), gated, gain, *squares
    )


def shared_parts(part):
    if lax.axis_size("tp") == 2:
        return [part, lax.ppermute(part, "tp", [(0, 1), (1, 0)])]
    return [lax.psum(part, "tp")]


def earlier_states(total, group, turns, count, states, width):
    if turns <= UNROLL:
        return [climb_up(total, group, count, steps) for steps in range(1, turns)]
    heads = width // DECAY_CHANNELS

    def one(_, carry):
        travelling, summed, ahead = carry
        travelling = climb_up(travelling, group, count)
        summed = summed + jnp.exp(ahead) * travelling[:, :width].astype(F32)
        more = unpack_row(travelling[:, width : width + heads])
        return travelling, summed, ahead + jnp.repeat(more, DECAY_CHANNELS, axis=1)

    start = (total, jnp.zeros((states, width), F32), jnp.zeros((1, width), F32))
    _, summed, _ = lax.fori_loop(1, turns, one, start)
    return [jnp.concatenate([summed.astype(BF16), jnp.zeros((states, LANES), BF16)], axis=1)]


def per_device(
    queries,
    keys,
    values,
    mixer_input,
    gate,
    step_weight,
    state_weight,
    step_bias,
    decay_rate,
    skip_gain,
    norm_gain,
):
    count = lax.axis_size("ctx")
    length = queries.shape[0]
    channels = mixer_input.shape[1]
    states = state_weight.shape[1] // 2
    group = math.gcd(keys.shape[1] // HD, count)
    turns = count // group
    width = channels // group

    packed = pack_kv(keys, values, group)
    parts = shared_parts(project(mixer_input, step_weight, state_weight, after=packed[:1]))
    blocks = swap(packed, group, count)
    (climb, climb_t, step_t, maps), payloads = block_state(
        parts, step_bias[None], decay_rate[None], mixer_input, queries, states, group
    )
    still, scale = local_part(
        mixer_input, gate, climb, climb_t, step_t, maps, skip_gain[None], states
    )
    own = jnp.stack([tie(blocks[0], [climb])] + blocks[1:])
    sent = payloads[:1]
    payloads = swap(payloads, group, count)
    ring = 1 < turns <= UNROLL
    arrived, ready = [], []
    if ring:
        arrived.append(climb_up(own, group, count))
    if ring and turns > 2:
        arrived[0] = tie(arrived[0], list(sent) + [still])
        ready = [arrived[0]]
        arrived.append(climb_up(arrived[0], group, count, first=1))
    total = group_total(payloads, length, states, width, after=ready)
    earlier = earlier_states(total, group, turns, count, states, width)
    state = flash(payloads, length, own=own, chunks=arrived[:-1][:1], after=[total])
    if ring and turns > 3:
        arrived[1] = tie(arrived[1], [state[1]] + earlier[:1] + earlier[:0:-1])
        ready = [arrived[1]]
        for step in range(2, turns - 1):
            arrived.append(climb_up(arrived[-1], group, count, first=step))
    entering = entering_states(payloads, earlier, length, states, width, after=ready)
    if ring and turns > 3:
        state = flash(
            payloads, length, state=state, chunks=arrived[1:-1], base=2, after=entering[:1]
        )
    entering = swap(entering, group, count)
    if turns > 1 and not ring:

        def one(step, carry):
            chunk, state = carry
            chunk = climb_up(chunk, group, count)
            state = flash(payloads, length, state=state, chunks=[chunk], base=jnp.reshape(step, (1,)))
            return chunk, tuple(state)

        chunk, state = lax.fori_loop(1, turns - 1, one, (own, tuple(state)))
        arrived.append(climb_up(chunk, group, count))
    gated, square = carried_part(maps, still, scale, entering, states)
    mamba_out = norm(
        gated, norm_gain[None], shared_parts(square), channels * lax.axis_size("tp")
    )
    if turns == 1:
        outs = flash(payloads, length, own=own, final=True)
    else:
        outs = flash(
            payloads, length, state=state, chunks=arrived[-1:], final=True, base=turns - 1
        )
    return join(swap(outs, group, count), group), mamba_out


def solution(mesh):
    return jax.shard_map(
        per_device,
        mesh=mesh,
        in_specs=(
            P("ctx", "tp"),
            P("ctx", "tp"),
            P("ctx", "tp"),
            P("ctx", "tp"),
            P("ctx", "tp"),
            P("tp", None),
            P("tp", None),
            P("tp"),
            P("tp"),
            P("tp"),
            P("tp"),
        ),
        out_specs=(P("ctx", "tp"), P("ctx", "tp")),
        check_vma=False,
    )
```

```python
import functools
import math

import jax
import jax.numpy as jnp
from jax import lax
from jax.experimental import pallas as pl
from jax.experimental.pallas import tpu as pltpu
from jax.sharding import PartitionSpec as P

HD = 128
DECAY_CHANNELS = 64
SCAN_TOKENS = 128
LANES = 128
UNROLL = 8
LOG2E = math.log2(math.e)
VMEM_LIMIT = 14 * 1024 * 1024

F32 = jnp.float32
BF16 = jnp.bfloat16


def vmem():
    return pl.BlockSpec(memory_space=pltpu.VMEM)


def hbm():
    return pl.BlockSpec(memory_space=pltpu.HBM)


def launch(kernel, name, out_shape, *inputs, after=(), flops=0, scratch=(), in_specs=None, out_specs=None, grid=None):
    count, skip = len(inputs), len(after)
    single = isinstance(out_shape, jax.ShapeDtypeStruct)
    shapes = [out_shape] if single else list(out_shape)
    size = sum(x.size * x.dtype.itemsize for x in list(inputs) + shapes)

    def body(*refs):
        kernel(*refs[:count], *refs[count + skip :])

    result = pl.pallas_call(
        body,
        **({} if grid is None else {"grid": grid}),
        out_shape=shapes,
        in_specs=(in_specs or [vmem()] * count) + [pl.BlockSpec(memory_space=pl.ANY)] * skip,
        out_specs=out_specs or [vmem()] * len(shapes),
        scratch_shapes=list(scratch),
        compiler_params=pltpu.CompilerParams(vmem_limit_bytes=VMEM_LIMIT),
        cost_estimate=pl.CostEstimate(flops=flops, bytes_accessed=size, transcendentals=0),
        name=name,
    )(*inputs, *after)
    return result[0] if single else result


def place(group):
    return lax.rem(lax.axis_index("ctx"), jnp.int32(group))


def swap(pieces, group, count):
    result = list(pieces)
    for k in reversed(range(1, group)):
        perm = [(i, (i // group) * group + ((i % group) ^ k)) for i in range(count)]
        result[k] = lax.ppermute(pieces[k], "ctx", perm)
    return result


def climb_up(array, group, count, steps=1, first=0):
    perm = [(i, i + group * steps) for i in range(group * first, count - group * steps)]
    return lax.ppermute(array, "ctx", perm)


def shape_of(shape, dtype):
    return jax.ShapeDtypeStruct(shape, dtype)


def tie(array, after):
    return pl.pallas_call(
        lambda *refs: None,
        out_shape=shape_of(array.shape, array.dtype),
        in_specs=[pl.BlockSpec(memory_space=pl.ANY)] * (1 + len(after)),
        out_specs=pl.BlockSpec(memory_space=pl.ANY),
        input_output_aliases={0: 0},
        compiler_params=pltpu.CompilerParams(vmem_limit_bytes=1024 * 1024),
        name="tie",
    )(array, *after)


def pack_kv(keys, values, group):
    length, width = keys.shape
    piece = width // group

    def kernel(k_ref, v_ref, *outs):
        mine = place(group)
        for k in range(group):
            columns = pl.ds(pl.multiple_of((mine ^ k) * piece, piece), piece)
            outs[k][0] = k_ref[:, columns]
            outs[k][1] = v_ref[:, columns]

    return launch(
        kernel,
        "pack_kv",
        [shape_of((2, length, piece), keys.dtype)] * group,
        keys,
        values,
        flops=5000000000,
        grid=(1,),
        in_specs=[pl.BlockSpec((length, width), lambda i: (0, 0))] * 2,
    )


def join(pieces, group):
    length, width = pieces[0].shape

    def kernel(*refs):
        out_ref, sems = refs[group:]
        mine = place(group)
        copies = []
        for k in range(group):
            columns = pl.ds(pl.multiple_of((mine ^ k) * width, width), width)
            copies.append(
                pltpu.make_async_copy(refs[group - 1 - k], out_ref.at[:, columns], sems.at[k])
            )
        for copy in copies:
            copy.start()
        for copy in copies:
            copy.wait()

    return launch(
        kernel,
        "join_heads",
        shape_of((length, width * group), pieces[0].dtype),
        *reversed(pieces),
        out_specs=[hbm()],
        scratch=[pltpu.SemaphoreType.DMA((group,))],
    )


def flash_chunk(q_refs, kv_ref, before, after, extended, own, length):
    group = len(q_refs)
    heads = q_refs[0].shape[1] // HD
    kv_heads = kv_ref.shape[3] // HD
    share = heads // kv_heads
    rows = group * length
    tile = min(rows, 2 * length)
    rate = LOG2E / math.sqrt(HD)
    for kv in range(kv_heads):
        lanes = slice(kv * HD, (kv + 1) * HD)
        keys = kv_ref[:, 0, :, lanes].reshape(rows, HD)
        extended[:, :HD] = kv_ref[:, 1, :, lanes].reshape(rows, HD)
        extended[:, HD:] = jnp.ones((rows, HD), BF16)
        tiles = [
            (h, start)
            for start in range(0, rows, tile)
            for h in range(kv * share, (kv + 1) * share)
        ]

        def score(h, start):
            parts = q_refs[start // length : (start + tile) // length]
            q = [ref[:length, h * HD : (h + 1) * HD] for ref in parts]
            q = jnp.concatenate(q, axis=0) if len(q) > 1 else q[0]
            scores = lax.dot_general(
                q, keys, (((1,), (1,)), ((), ())), preferred_element_type=F32
            )
            if own:
                flip = place(group) * length
                row = (lax.broadcasted_iota(jnp.int32, (tile, rows), 0) + start) ^ flip
                column = lax.broadcasted_iota(jnp.int32, (tile, rows), 1) ^ flip
                scores = jnp.where(column <= row, scores, -1e30)
            return scores

        ahead = score(*tiles[0])
        for n, (h, start) in enumerate(tiles):
            scores = ahead
            if n + 1 < len(tiles):
                ahead = score(*tiles[n + 1])
            here = slice(start, start + tile)
            top = jnp.max(scores, axis=1, keepdims=True) * rate
            top = jnp.broadcast_to(top, (tile, LANES))
            if not own:
                top_before = before[1][h, here]
                top = jnp.maximum(top_before, top)
            across = [top] * (rows // LANES)
            across = jnp.concatenate(across, axis=1) if len(across) > 1 else top
            weights = jnp.exp2(scores * rate - across).astype(BF16)
            value = jnp.dot(weights, extended[...], preferred_element_type=F32)
            if not own:
                keep = jnp.exp2(top_before - top)
                value = value + before[0][h, here] * jnp.concatenate([keep, keep], axis=1)
            yield h, start, tile, value
            if after is not None:
                after[0][h, here] = value
                after[1][h, here] = top


def finish_rows(out_refs, h, start, tile, value):
    length = out_refs[0].shape[0]
    result = (value[:, :HD] / value[:, HD:]).astype(BF16)
    for at in range(0, tile, length):
        out_refs[(start + at) // length][:, h * HD : (h + 1) * HD] = result[at : at + length]


def flash(q, length, own=None, state=(), chunks=(), final=False, base=1, after=()):
    group = len(q)
    heads = q[0].shape[1] // HD
    rows = group * length
    fixed = isinstance(base, int)
    has_own = own is not None
    specs = [] if fixed else [pl.BlockSpec(memory_space=pltpu.SMEM)]
    rest = list(q) + ([own] if has_own else []) + list(state) + list(chunks)
    specs = specs + [vmem()] * len(rest)

    def kernel(*refs):
        refs = list(refs)
        first = base if fixed else refs.pop(0)[0]
        q_refs = [refs.pop(0) for _ in range(group)]
        own_ref = refs.pop(0) if has_own else None
        held = None if has_own else (refs.pop(0), refs.pop(0))
        chunk_refs = [refs.pop(0) for _ in range(len(chunks))]
        extended = refs.pop()
        turn = lax.axis_index("ctx") // group
        outs = None if final else tuple(refs)
        if has_own:
            for done in flash_chunk(q_refs, own_ref, None, outs, extended, True, length):
                if final:
                    finish_rows(refs, *done)
            held = outs
        for number, ref in enumerate(chunk_refs):

            @pl.when(turn >= first + number)
            def _(ref=ref, held=held):
                for done in flash_chunk(q_refs, ref, held, outs, extended, False, length):
                    if final:
                        finish_rows(refs, *done)

            if not has_own and number == 0:

                @pl.when(turn < first)
                def _(held=held):
                    for h in range(heads):
                        if final:
                            finish_rows(refs, h, 0, rows, held[0][h])
                        else:
                            outs[0][h] = held[0][h]
                            outs[1][h] = held[1][h]

            held = outs

    if final:
        out_shape = [shape_of((length, heads * HD), BF16)] * group
    else:
        out_shape = [
            shape_of((heads, rows, HD + LANES), F32),
            shape_of((heads, rows, LANES), F32),
        ]
    parts = len(chunks) + has_own
    return launch(
        kernel,
        "flash",
        out_shape,
        *([] if fixed else [base]),
        *rest,
        after=after,
        in_specs=specs,
        flops=4 * heads * rows * rows * HD * parts,
        scratch=[pltpu.VMEM((rows, HD + LANES), BF16)],
    )


def widen(row, lanes):
    extra = lanes - row.shape[1]
    if not extra:
        return row
    return jnp.concatenate([row, jnp.zeros((row.shape[0], extra), row.dtype)], axis=1)


def project(x, step_weight, state_weight, after=()):
    length, channels = x.shape
    heads = step_weight.shape[1]

    def kernel(x_ref, step_ref, map_ref, out_ref):
        x = x_ref[...]
        out_ref[:, :heads] = jnp.dot(x, step_ref[...], preferred_element_type=F32)
        maps = lax.dot_general(
            x, map_ref[...], (((1,), (1,)), ((), ())), preferred_element_type=F32
        )
        out_ref[:, heads:] = widen(maps, LANES)

    return launch(
        kernel,
        "project",
        shape_of((length, heads + LANES), F32),
        x,
        step_weight,
        state_weight.T,
        after=after,
        flops=4 * length * channels * heads,
    )


def owners(heads):
    shape = (LANES, heads * DECAY_CHANNELS)
    head = lax.broadcasted_iota(jnp.int32, shape, 0)
    channel = lax.broadcasted_iota(jnp.int32, shape, 1)
    return (channel // DECAY_CHANNELS == head).astype(BF16)


def pack_row(row, rows):
    high = row.astype(BF16).astype(F32)
    rest = row - high
    middle = rest.astype(BF16).astype(F32)
    low = rest - middle
    return jnp.concatenate([high, middle, low, jnp.zeros((rows - 3, row.shape[1]), F32)], axis=0)


def unpack_row(rows):
    rows = rows.astype(F32)
    return rows[0:1] + rows[1:2] + rows[2:3]


def spread_total(rows, owner):
    wide = jnp.dot(rows, owner, preferred_element_type=F32)
    return wide[0:1] + wide[1:2] + wide[2:3]


def block_state(parts, bias, rate, x, q, states, group, after=()):
    length, channels = x.shape
    every = parts[0].shape[1] - LANES
    heads = bias.shape[1]
    width = channels // group
    columns = q.shape[1] // group
    bands = width // columns
    count = len(parts)

    def kernel(*refs):
        bias_ref, rate_ref, x_ref, q_ref = refs[count : count + 4]
        climb_ref, climb_t_ref, step_t_ref, maps_ref = refs[count + 4 : count + 8]
        outs = refs[count + 8 : count + 8 + group]
        held = refs[count + 8 + group]
        summed = refs[0][...]
        for ref in refs[1:count]:
            summed = summed + ref[...]
        shift = lax.rem(every - lax.axis_index("tp") * heads, jnp.int32(every))
        raw = pltpu.roll(summed[:, :every], shift, 1) + widen(bias_ref[...], every)
        step = jnp.maximum(raw, 0.0) + jnp.log1p(jnp.exp(-jnp.abs(raw)))
        log_decay = -widen(rate_ref[...], every) * step
        row = lax.broadcasted_iota(jnp.int32, (length, length), 0)
        column = lax.broadcasted_iota(jnp.int32, (length, length), 1)
        lower = (column <= row).astype(F32)
        climb = jnp.dot(
            lower, log_decay, precision=lax.Precision.HIGHEST, preferred_element_type=F32
        )
        maps = summed[:, every:]
        climb_ref[...] = climb * LOG2E
        maps_ref[...] = maps
        climb_t = climb.T
        step_t = step.T
        climb_t_ref[...] = climb_t[:heads] * LOG2E
        step_t_ref[...] = step_t[:heads]
        b_t = maps.T[:states]
        weight_t = jnp.exp(climb_t[:, length - 1 :] - climb_t) * step_t
        bundle = 4
        span = bundle * DECAY_CHANNELS
        owner = lax.broadcasted_iota(jnp.int32, (1, span), 1) // DECAY_CHANNELS
        for at in range(0, heads, bundle):
            feed = [b_t * weight_t[at + i : at + i + 1] for i in range(bundle)]
            feed = jnp.concatenate(feed, axis=0).astype(BF16)
            start = at * DECAY_CHANNELS
            product = jnp.dot(feed, x_ref[:, start : start + span], preferred_element_type=F32)
            state = product[:states]
            for i in range(1, bundle):
                state = jnp.where(owner == i, product[i * states : (i + 1) * states], state)
            piece, offset = divmod(start, width)
            band, offset = divmod(offset, columns)
            rows = slice(band * states, (band + 1) * states)
            held[piece, rows, offset : offset + span] = state.astype(BF16)
        totals = pack_row(climb[length - 1 :], states)
        for piece in range(group):
            at = piece * (heads // group)
            here = totals if not at else pltpu.roll(totals, every - at, 1)
            held[piece, bands * states :, :] = widen(here[:, :LANES], columns).astype(BF16)
        mine = place(group)
        for k in range(group):
            here = pl.ds(pl.multiple_of((mine ^ k) * columns, columns), columns)
            outs[k][:length] = q_ref[:, here]
            outs[k][length:] = held[mine ^ k]

    payload = shape_of((length + (bands + 1) * states, columns), BF16)
    result = launch(
        kernel,
        "block_state",
        [
            shape_of((length, every), F32),
            shape_of((heads, length), F32),
            shape_of((heads, length), F32),
            shape_of((length, LANES), F32),
        ]
        + [payload] * group,
        *parts,
        bias,
        rate,
        x,
        q,
        after=after,
        flops=32 * length * states * channels,
        scratch=[pltpu.VMEM((group, (bands + 1) * states, columns), BF16)],
    )
    return result[:4], result[4:]


def local_part(x, gate, climb, climb_t, step_t, maps, skip, states, after=()):
    length, channels = x.shape
    heads = channels // DECAY_CHANNELS

    def kernel(
        x_ref, gate_ref, climb_ref, climb_t_ref, step_t_ref, maps_ref, skip_ref, still_ref, scale_ref
    ):
        maps = maps_ref[...]
        inner = lax.dot_general(
            maps[:, states : 2 * states],
            maps[:, :states],
            (((1,), (1,)), ((), ())),
            precision=lax.Precision.HIGHEST,
            preferred_element_type=F32,
        )
        row = lax.broadcasted_iota(jnp.int32, (length, length), 0)
        column = lax.broadcasted_iota(jnp.int32, (length, length), 1)
        inner = jnp.where(column <= row, inner, 0.0)
        left = lax.broadcasted_iota(jnp.int32, (length, LANES), 1) < DECAY_CHANNELS

        for j in range(0, heads, 2):
            columns = slice(j * DECAY_CHANNELS, j * DECAY_CHANNELS + LANES)
            x = x_ref[:, columns]
            wide = [jnp.broadcast_to(climb_ref[:, i : i + 1], (length, length)) for i in (j, j + 1)]
            mixed = []
            for i in (j, j + 1):
                fall = jnp.minimum(wide[i - j] - climb_t_ref[i : i + 1], 0.0)
                mixed.append((inner * jnp.exp2(fall) * step_t_ref[i : i + 1]).astype(BF16))
            zero = jnp.zeros_like(x)
            feeds = jnp.concatenate([jnp.where(left, x, zero), jnp.where(left, zero, x)], axis=0)
            local = jnp.dot(jnp.concatenate(mixed, axis=1), feeds, preferred_element_type=F32)
            gain = jnp.where(left[:1], skip_ref[:, j : j + 1], skip_ref[:, j + 1 : j + 2])
            grown = jnp.exp2(jnp.where(left, wide[0], wide[1]))
            gate = gate_ref[:, columns].astype(F32)
            half = 0.5 * gate
            silu = half + half * jnp.tanh(half)
            still_ref[:, columns] = (local + gain * x.astype(F32)) * silu
            scale_ref[:, columns] = grown * silu

    return launch(
        kernel,
        "local_part",
        [shape_of((length, channels), F32)] * 2,
        x,
        gate,
        climb,
        climb_t,
        step_t,
        maps,
        skip,
        after=after,
        flops=4 * length * length * channels,
    )


def gather_blocks(group, states, length, refs, held):
    mine = place(group)
    for k in range(group):
        held[mine ^ k] = refs[k][length:]


def block_of(held, b, states, columns, width):
    bands = width // columns
    rows = [held[b, i * states : (i + 1) * states] for i in range(bands)]
    state = jnp.concatenate(rows, axis=1) if bands > 1 else rows[0]
    return state.astype(F32), held[b, bands * states :, :LANES]


def group_total(payloads, length, states, width, after=()):
    group = len(payloads)
    rows, columns = payloads[0].shape
    heads = width // DECAY_CHANNELS

    def kernel(*refs):
        out_ref, held = refs[group:]
        gather_blocks(group, states, length, refs[:group], held)
        owner = owners(heads)
        state, packed = block_of(held, 0, states, columns, width)
        total = unpack_row(packed)
        for b in range(1, group):
            more, packed = block_of(held, b, states, columns, width)
            state = jnp.exp(spread_total(packed, owner)) * state + more
            total = total + unpack_row(packed)
        out_ref[:, :width] = state.astype(BF16)
        out_ref[:, width:] = pack_row(total, states).astype(BF16)

    return launch(
        kernel,
        "group_total",
        shape_of((states, width + LANES), BF16),
        *payloads,
        after=after,
        scratch=[pltpu.VMEM((group, rows - length, columns), BF16)],
    )


def entering_states(payloads, earlier, length, states, width, after=()):
    group = len(payloads)
    rows, columns = payloads[0].shape
    heads = width // DECAY_CHANNELS
    count = len(earlier)

    def kernel(*refs):
        earlier_refs = refs[group : group + count]
        outs = refs[group + count : 2 * group + count]
        held, entering = refs[2 * group + count :]
        gather_blocks(group, states, length, refs[:group], held)
        owner = owners(heads)
        state = jnp.zeros((states, width), F32)
        for ref in reversed(earlier_refs):
            state = jnp.exp(spread_total(ref[:, width:], owner)) * state
            state = state + ref[:, :width].astype(F32)
        for b in range(group):
            entering[b] = state
            if b < group - 1:
                more, packed = block_of(held, b, states, columns, width)
                state = jnp.exp(spread_total(packed, owner)) * state + more
        mine = place(group)
        for k in range(group):
            outs[k][...] = entering[mine ^ k]

    return launch(
        kernel,
        "entering_states",
        [shape_of((states, width), F32)] * group,
        *payloads,
        *earlier,
        after=after,
        scratch=[
            pltpu.VMEM((group, rows - length, columns), BF16),
            pltpu.VMEM((group, states, width), F32),
        ],
    )


def carried_part(maps, still, scale, entering, states, after=()):
    length, channels = still.shape
    group = len(entering)
    width = channels // group
    span = min(width, 512)

    def kernel(maps_ref, still_ref, scale_ref, *refs):
        gated_ref, square_ref, held = refs[group:]
        mine = place(group)
        for k in range(group):
            held[mine ^ k] = refs[k][...]
        c = maps_ref[:, states : 2 * states]
        c_high = c.astype(BF16)
        c_low = (c - c_high.astype(F32)).astype(BF16)
        c = jnp.concatenate([c_high, c_low, c_high], axis=1)
        folded = jnp.zeros(square_ref.shape, F32)
        for at in range(0, channels, span):
            piece, offset = divmod(at, width)
            state = held[piece, :, offset : offset + span]
            high = state.astype(BF16)
            low = (state - high.astype(F32)).astype(BF16)
            carried = jnp.dot(
                c, jnp.concatenate([high, high, low], axis=0), preferred_element_type=F32
            )
            columns = slice(at, at + span)
            gated = still_ref[:, columns] + scale_ref[:, columns] * carried
            gated_ref[:, columns] = gated
            square = gated * gated
            for lane in range(0, span, LANES):
                folded = folded + square[:, lane : lane + LANES]
        square_ref[...] = folded

    return launch(
        kernel,
        "carried_part",
        [shape_of((length, channels), F32), shape_of((length, LANES), F32)],
        maps,
        still,
        scale,
        *entering,
        after=after,
        flops=6 * length * states * channels,
        scratch=[pltpu.VMEM((group, states, width), F32)],
    )


def norm(gated, gain, squares, every):
    length, channels = gated.shape
    count = len(squares)

    def kernel(gated_ref, gain_ref, *refs):
        out_ref = refs[count]
        square = refs[0][...]
        for ref in refs[1:count]:
            square = square + ref[...]
        mean = jnp.sum(square, axis=1, keepdims=True) / every
        factor = jnp.broadcast_to(lax.rsqrt(mean + 1e-05), square.shape)
        for at in range(0, channels, LANES):
            columns = slice(at, at + LANES)
            out_ref[:, columns] = (gated_ref[:, columns] * factor * gain_ref[:, columns]).astype(BF16)

    return launch(
        kernel, "norm", shape_of((length, channels), BF16), gated, gain, *squares
    )


def shared_parts(part):
    if lax.axis_size("tp") == 2:
        return [part, lax.ppermute(part, "tp", [(0, 1), (1, 0)])]
    return [lax.psum(part, "tp")]


def earlier_states(total, group, turns, count, states, width):
    if turns <= UNROLL:
        return [climb_up(total, group, count, steps) for steps in range(1, turns)]
    heads = width // DECAY_CHANNELS

    def one(_, carry):
        travelling, summed, ahead = carry
        travelling = climb_up(travelling, group, count)
        summed = summed + jnp.exp(ahead) * travelling[:, :width].astype(F32)
        more = unpack_row(travelling[:, width : width + heads])
        return travelling, summed, ahead + jnp.repeat(more, DECAY_CHANNELS, axis=1)

    start = (total, jnp.zeros((states, width), F32), jnp.zeros((1, width), F32))
    _, summed, _ = lax.fori_loop(1, turns, one, start)
    return [jnp.concatenate([summed.astype(BF16), jnp.zeros((states, LANES), BF16)], axis=1)]


def per_device(
    queries,
    keys,
    values,
    mixer_input,
    gate,
    step_weight,
    state_weight,
    step_bias,
    decay_rate,
    skip_gain,
    norm_gain,
):
    count = lax.axis_size("ctx")
    length = queries.shape[0]
    channels = mixer_input.shape[1]
    states = state_weight.shape[1] // 2
    group = math.gcd(keys.shape[1] // HD, count)
    turns = count // group
    width = channels // group

    packed = pack_kv(keys, values, group)
    parts = shared_parts(project(mixer_input, step_weight, state_weight, after=packed[:1]))
    blocks = swap(packed, group, count)
    (climb, climb_t, step_t, maps), payloads = block_state(
        parts, step_bias[None], decay_rate[None], mixer_input, queries, states, group
    )
    still, scale = local_part(
        mixer_input, gate, climb, climb_t, step_t, maps, skip_gain[None], states
    )
    own = jnp.stack([tie(blocks[0], [climb])] + blocks[1:])
    sent = payloads[:1]
    payloads = swap(payloads, group, count)
    ring = 1 < turns <= UNROLL
    arrived, ready = [], []
    if ring:
        arrived.append(climb_up(own, group, count))
    if ring and turns > 2:
        arrived[0] = tie(arrived[0], list(sent) + [still])
        ready = [arrived[0]]
        arrived.append(climb_up(arrived[0], group, count, first=1))
    total = group_total(payloads, length, states, width, after=ready)
    earlier = earlier_states(total, group, turns, count, states, width)
    state = flash(payloads, length, own=own, chunks=arrived[:-1][:1], after=[total])
    if ring and turns > 3:
        arrived[1] = tie(arrived[1], [state[1]] + earlier[:1] + earlier[:0:-1])
        ready = [arrived[1]]
        for step in range(2, turns - 1):
            arrived.append(climb_up(arrived[-1], group, count, first=step))
    entering = entering_states(payloads, earlier, length, states, width, after=ready)
    if ring and turns > 3:
        state = flash(
            payloads, length, state=state, chunks=arrived[1:-1], base=2, after=entering[:1]
        )
    entering = swap(entering, group, count)
    if turns > 1 and not ring:

        def one(step, carry):
            chunk, state = carry
            chunk = climb_up(chunk, group, count)
            state = flash(payloads, length, state=state, chunks=[chunk], base=jnp.reshape(step, (1,)))
            return chunk, tuple(state)

        chunk, state = lax.fori_loop(1, turns - 1, one, (own, tuple(state)))
        arrived.append(climb_up(chunk, group, count))
    gated, square = carried_part(maps, still, scale, entering, states)
    mamba_out = norm(
        gated, norm_gain[None], shared_parts(square), channels * lax.axis_size("tp")
    )
    if turns == 1:
        outs = flash(payloads, length, own=own, final=True)
    else:
        outs = flash(
            payloads, length, state=state, chunks=arrived[-1:], final=True, base=turns - 1
        )
    return join(swap(outs, group, count), group), mamba_out


def solution(mesh):
    return jax.shard_map(
        per_device,
        mesh=mesh,
        in_specs=(
            P("ctx", "tp"),
            P("ctx", "tp"),
            P("ctx", "tp"),
            P("ctx", "tp"),
            P("ctx", "tp"),
            P("tp", None),
            P("tp", None),
            P("tp"),
            P("tp"),
            P("tp"),
            P("tp"),
        ),
        out_specs=(P("ctx", "tp"), P("ctx", "tp")),
        check_vma=False,
    )
```
